256 devices in a mesh: ia: 8 (over z), ja: 16 (over x, y_lo, core), ka: 2 (over y_hi).
Axes of the slice: x: 4, y: 4 (y_hi: 2, y_lo: 2; y = y_hi * 2 + y_lo), z: 8, core: 2. Of those that a mesh axis runs over, the one named last changes fastest.
Arguments:
- tensor: float32 [1024, 1024, 512], P('ia', 'ja', 'ka'), may hold values from -6 to 6
- factor_b: float32 [16, 64, 256], P('ja', ('ia', 'ka')), may hold values from -0.1875 to 0.1875
- factor_c: float32 [2, 256, 256], P('ka', ('ia', 'ja')), may hold values from -0.25 to 0.25
Outputs:
- new_a: float32 [8, 128, 256], P('ia', ('ja', 'ka'))
- new_b: float32 [16, 64, 256], P('ja', ('ia', 'ka'))
- new_c: float32 [2, 256, 256], P('ka', ('ia', 'ja'))
The draws below stay inside these ranges and needn't reach their ends.
All inputs are finite; a program needn't handle non-finite values.
Results may differ from the reference program's by a relative error of at most 0.00011.
Values sent between devices are 32-bit elements; how exact they have to be, the bound alone decides.
A program may use at most 64 MiB of HBM per device.

```python
import jax
import jax.numpy as jnp
from jax import lax

I_DEV = 128
J_DEV = 64
K_DEV = 256
R = 256
I = 1024
J = 1024
K = 512
N_IA = 8
N_JA = 16
N_KA = 2


def level_of(own_key, extent, pieces, smallest, high):
    level, own = 1.0, jax.random.fold_in(own_key, 6)
    for axis_at, shards_of in pieces:
        heights = jnp.exp(jax.random.uniform(jax.random.fold_in(own, axis_at), (shards_of,), jnp.float32, smallest / len(pieces), high / len(pieces)))
        level = level * jnp.repeat(heights, extent[axis_at] // shards_of).reshape([-1 if axis == axis_at else 1 for axis in range(len(extent))])
    return level


def centred(rng, shape, width, limit, cuts=(), dtype=jnp.bfloat16):
    array = jax.random.normal(rng, shape, jnp.float32) * width
    if len(cuts) > 0:
        array = level_of(rng, shape, cuts, -0.22, 0.18) * array
    return jnp.clip(array, min=-limit, max=limit).astype(dtype)


def setup_inputs(seed: int = 0) -> dict:
    keys = jax.random.split(jax.random.key(seed), 4)
    tensor = centred(keys[0], (I, J, K), 1.0, 6.0, ((0, 8), (1, 16), (2, 2)), jnp.float32)
    factor_b = centred(keys[1], (N_JA, J_DEV, R), J ** -0.5, 0.1875, ((0, 16), (1, 16)), jnp.float32)
    factor_c = centred(keys[2], (N_KA, K_DEV, R), K ** -0.5, 0.25, ((0, 2), (1, 128)), jnp.float32)
    return {"tensor": tensor, "factor_b": factor_b, "factor_c": factor_c}


HIGH = lax.Precision.HIGHEST

def gram_of(rows):
    return jnp.dot(rows.T.astype(jnp.float32), rows.astype(jnp.float32), precision=HIGH, preferred_element_type=jnp.float32)

def solve_rows(right, gram):
    factor = jnp.linalg.cholesky(gram)
    return jax.scipy.linalg.cho_solve((factor, True), right.T).T

def reference(tensor, factor_b, factor_c):
    mat_b = factor_b.reshape(J, R)
    mat_c = factor_c.reshape(K, R)
    gram_b = gram_of(mat_b)
    gram_c = gram_of(mat_c)
    blocks = tensor.reshape(N_IA, I_DEV, J, K)

    def first(block):
        inner = jnp.einsum('ijk,kr->ijr', block, mat_c, precision=HIGH)
        return jnp.einsum('ijr,jr->ir', inner, mat_b, precision=HIGH)
    mttkrp_a = lax.map(first, blocks).reshape(I, R)
    mat_a = solve_rows(mttkrp_a, gram_b * gram_c)
    gram_a = gram_of(mat_a)
    rows_a = mat_a.reshape(N_IA, I_DEV, R)

    def second(total, pair):
        block, part_a = pair
        inner = jnp.einsum('ijk,kr->ijr', block, mat_c, precision=HIGH)
        return (total + jnp.einsum('ijr,ir->jr', inner, part_a, precision=HIGH), None)
    mttkrp_b, unused = lax.scan(second, jnp.zeros((J, R), jnp.float32), (blocks, rows_a))
    mat_b2 = solve_rows(mttkrp_b, gram_a * gram_c)
    gram_b2 = gram_of(mat_b2)

    def third(total, pair):
        block, part_a = pair
        weights = part_a[:, None, :] * mat_b2[None, :, :]
        return (total + jnp.einsum('ijk,ijr->kr', block, weights, precision=HIGH), None)
    mttkrp_c, unused = lax.scan(third, jnp.zeros((K, R), jnp.float32), (blocks, rows_a))
    mat_c2 = solve_rows(mttkrp_c, gram_a * gram_b2)
    return (mat_a.reshape(N_IA, I_DEV, R), mat_b2.reshape(N_JA, J_DEV, R), mat_c2.reshape(N_KA, K_DEV, R))
```

```python
import functools

import jax
import jax.numpy as jnp
from jax import lax
from jax.experimental import pallas as pl
from jax.experimental.pallas import tpu as pltpu
from jax.sharding import PartitionSpec as P

HIGH = lax.Precision.HIGHEST
MESH = pl.DeviceIdType.MESH
F32 = jnp.float32
BF16 = jnp.bfloat16
NB = 32


def dot_f32(x, y, dims):
    return lax.dot_general(x, y, (dims, ((), ())), precision=HIGH, preferred_element_type=F32)


def dot_bf16(x, y, dims):
    return lax.dot_general(x, y, (dims, ((), ())), preferred_element_type=F32)


def split2(x):
    high = x.astype(BF16)
    return high, (x - high.astype(F32)).astype(BF16)


def split3(x):
    first = x.astype(BF16)
    rest = x - first.astype(F32)
    second = rest.astype(BF16)
    return first, second, (rest - second.astype(F32)).astype(BF16)


def invert(s_ref):
    n = s_ref.shape[0]
    rows_at = lax.broadcasted_iota(jnp.int32, (NB, n), 0)
    lanes_at = lax.broadcasted_iota(jnp.int32, (NB, n), 1)

    for block in range(n // NB):
        low = block * NB
        old = s_ref[low : low + NB, :]
        panel = old
        for j in range(NB):
            column = panel[:, low + j : low + j + 1]
            inverse = 1.0 / panel[j : j + 1, low + j : low + j + 1]
            here = lanes_at == low + j
            pivot_row = jnp.where(here[:1], 1.0, panel[j : j + 1, :]) * inverse
            panel = jnp.where(here, 0.0, panel)
            panel = jnp.where(rows_at == j, pivot_row, panel - column * pivot_row)
        signed = jnp.where(lanes_at < low, -old, jnp.where(lanes_at < low + NB, 0.0, old))
        x1, x2, x3 = split3(signed)
        y1, y2, y3 = split3(panel)
        update = dot_bf16(
            jnp.concatenate([x1, x1, x2, x2, x1, x3], axis=0),
            jnp.concatenate([y1, y2, y1, y2, y3, y1], axis=0),
            ((0,), (0,)),
        )
        all_lanes = lax.broadcasted_iota(jnp.int32, (n, n), 1)
        inside = (all_lanes >= low) & (all_lanes < low + NB)
        s_ref[...] = jnp.where(inside, 0.0, s_ref[...]) - update
        s_ref[low : low + NB, :] = panel


def kernel(
    n_ia, n_ja, n_ka,
    t_hbm, b_ref, c_ref,
    a_out, b_out, c_out,
    t_ref, thi, tlo, p_ref,
    c_in1, c_in2, c_all, b_in, b_all,
    gb_mine, gb_in, gc_mine, gc_in, gc_rows, ga_rows,
    g_send, g_all,
    a_parts, a_in, a_own, a_in2, a_slice, ga_mine, ga_in,
    bm_parts, bm_in, b_own, b_in2, b_slice, gb2_mine, gb2_in,
    cm_mine, cm_parts, cm_in, cm_sum, cm_in2,
    t_sem, send_sem, recv_sem,
):
    i_dev, j_dev, k_dev = t_hbm.shape
    rank = c_ref.shape[-1]
    ia, ja, ka = lax.axis_index("ia"), lax.axis_index("ja"), lax.axis_index("ka")
    n_g, n_h = n_ja * n_ka, n_ia * n_ka
    g_at = ja * n_ka + ka
    h_at = ia * n_ka + ka
    g_tall = rank // n_g

    def device(z, j, k):
        return {"ia": z, "ja": j, "ka": k}

    def plane(step):
        at = lax.rem(g_at + step, n_g)
        return at, device(ia, at // n_ka, lax.rem(at, n_ka))

    def column(step):
        at = lax.rem(ia + step, n_ia)
        return at, device(at, ja, ka)

    def column_pair(step):
        at = lax.rem(h_at + step, n_h)
        return at, device(at // n_ka, ja, lax.rem(at, n_ka))

    def row(step):
        at = lax.rem(ja + step, n_ja)
        return at, device(ia, at, ka)

    def send(phase, n, peer, source, target):
        def body(step, carry):
            at, who = peer(step)
            pltpu.make_async_remote_copy(
                src_ref=source(at), dst_ref=target(at), send_sem=send_sem.at[phase],
                recv_sem=recv_sem.at[phase], device_id=who, device_id_type=MESH,
            ).start()
            return carry
        lax.fori_loop(1, n, body, 0)

    def done(phase, ref, sem):
        pltpu.make_async_copy(ref, ref, sem.at[phase]).wait()

    chunks = t_sem.shape[0]
    i_chunk = i_dev // chunks

    def load(at):
        span = pl.ds(at * i_chunk, i_chunk)
        return pltpu.make_async_copy(t_hbm.at[span], t_ref.at[span], t_sem.at[at])

    for at in range(chunks):
        load(at).start()

    barrier = pltpu.get_barrier_semaphore()

    def greet_plane(step, carry):
        pl.semaphore_signal(barrier, inc=1, device_id=plane(step)[1], device_id_type=MESH)
        return carry

    def greet_column(step, carry):
        z = lax.rem(ia + step, n_ia)
        for k in range(n_ka):
            pl.semaphore_signal(barrier, inc=1, device_id=device(z, ja, k), device_id_type=MESH)
        return carry

    lax.fori_loop(1, n_g, greet_plane, 0)
    lax.fori_loop(1, n_ia, greet_column, 0)
    pl.semaphore_wait(barrier, n_g - 1 + (n_ia - 1) * n_ka)

    send(0, n_ia, column, lambda at: c_ref.at[0], lambda at: c_in1.at[ia])
    send(1, n_h, column_pair, lambda at: b_ref.at[0], lambda at: b_in.at[h_at])
    c_in1[ia] = c_ref[0]
    b_in[h_at] = b_ref[0]
    done(0, c_in1.at[pl.ds(0, n_ia - 1)], recv_sem)
    send(2, n_ja, row, lambda at: c_in1, lambda at: c_in2.at[ja])
    c_in2[ja] = c_in1[...]

    for at in range(chunks):
        load(at).wait()

        def split_one(i, carry):
            high, low = split2(t_ref[i])
            thi[i] = high
            tlo[i] = low
            return carry
        lax.fori_loop(at * i_chunk, (at + 1) * i_chunk, split_one, 0)

    done(1, b_in.at[pl.ds(0, n_h - 1)], recv_sem)
    for h in range(n_h):
        b_all[4 * h : 4 * h + 4, :] = b_in[h]
    gb_mine[...] = dot_f32(b_all[...], b_all[...], ((0,), (0,)))

    def rows_of(ref, at):
        return ref.at[pl.ds(pl.multiple_of(at * g_tall, 8), g_tall)]

    send(3, n_ja, row, lambda at: rows_of(gb_mine, at * n_ka + ka), lambda at: gb_in.at[ja])
    done(2, c_in2.at[pl.ds(0, n_ja - 1)], recv_sem)
    for z in range(n_ia):
        for j in range(n_ja):
            low = 2 * (z * n_ja + j)
            c_all[low : low + 2, :] = c_in2[j, z]
    gc_mine[...] = dot_f32(c_all[...], c_all[...], ((0,), (0,)))

    def other(step):
        at = lax.rem(ka + step, n_ka)
        return at, device(ia, ja, at)

    send(4, n_ka, other, lambda at: rows_of(gc_mine, ja * n_ka + at), lambda at: gc_in.at[ka])

    chi, clo = split2(c_all[...])
    per = 8
    b_whole = b_all[...]

    def first(step, carry):
        span = pl.ds(step * per, per)
        left_hi = thi[span].reshape(per * j_dev, k_dev)
        left_lo = tlo[span].reshape(per * j_dev, k_dev)
        inner = dot_bf16(left_hi, chi, ((1,), (0,))) + (
            dot_bf16(left_hi, clo, ((1,), (0,))) + dot_bf16(left_lo, chi, ((1,), (0,)))
        )
        inner = inner.reshape(per, j_dev, rank)
        p_ref[span] = inner
        summed = jnp.sum(inner * b_whole[None], axis=1)
        a_parts[pl.ds(step * (per // 4), per // 4)] = summed.reshape(per // 4, 4, rank)
        return carry
    lax.fori_loop(0, i_dev // per, first, 0)

    send(5, n_g, plane, lambda at: a_parts.at[at], lambda at: a_in.at[g_at])
    a_in[g_at] = a_parts[g_at]

    def gather_gram(phase, slot, rows):
        g_send[slot] = rows
        rows_of(g_all.at[slot], g_at)[...] = rows
        send(phase, n_g, plane, lambda at: g_send.at[slot], lambda at: rows_of(g_all.at[slot], g_at))

    gb_in[ja] = rows_of(gb_mine, g_at)[...]
    gc_in[ka] = rows_of(gc_mine, g_at)[...]
    done(3, gb_in.at[pl.ds(0, n_ja - 1)], recv_sem)
    done(4, gc_in.at[pl.ds(0, n_ka - 1)], recv_sem)
    gc_rows[...] = jnp.sum(gc_in[...], axis=0)
    gather_gram(6, 0, jnp.sum(gb_in[...], axis=0) * gc_rows[...])
    done(6, g_all.at[0, pl.ds(0, rank - g_tall)], recv_sem)
    invert(g_all.at[0])
    done(5, a_in.at[pl.ds(0, n_g - 1)], recv_sem)
    own = dot_f32(jnp.sum(a_in[...], axis=0), g_all[0], ((1,), (0,)))
    a_out[0] = own
    a_own[...] = own

    a_in2[g_at] = own
    send(7, n_g, plane, lambda at: a_own, lambda at: a_in2.at[g_at])
    done(7, a_in2.at[pl.ds(0, n_g - 1)], recv_sem)
    for g in range(n_g):
        a_slice[4 * g : 4 * g + 4, :] = a_in2[g]
    ga_mine[...] = dot_f32(a_slice[...], a_slice[...], ((0,), (0,)))
    send(8, n_ia, column, lambda at: rows_of(ga_mine, g_at), lambda at: ga_in.at[ia])
    ga_in[ia] = rows_of(ga_mine, g_at)[...]

    def second(step, total):
        for e in range(4):
            i = step * 4 + e
            total = total + p_ref[i] * a_slice[pl.ds(i, 1), :]
        return total
    sums = lax.fori_loop(0, i_dev // 4, second, jnp.zeros((j_dev, rank), F32))
    for h in range(n_h):
        bm_parts[h] = sums[4 * h : 4 * h + 4]
    send(9, n_h, column_pair, lambda at: bm_parts.at[at], lambda at: bm_in.at[h_at])
    bm_in[h_at] = bm_parts[h_at]
    done(8, ga_in.at[pl.ds(0, n_ia - 1)], recv_sem)
    ga_rows[...] = jnp.sum(ga_in[...], axis=0)
    gather_gram(10, 1, ga_rows[...] * gc_rows[...])
    done(10, g_all.at[1, pl.ds(0, rank - g_tall)], recv_sem)
    invert(g_all.at[1])
    done(9, bm_in.at[pl.ds(0, n_h - 1)], recv_sem)
    own = dot_f32(jnp.sum(bm_in[...], axis=0), g_all[1], ((1,), (0,)))
    b_out[0] = own
    b_own[...] = own

    b_in2[h_at] = own
    send(11, n_h, column_pair, lambda at: b_own, lambda at: b_in2.at[h_at])
    done(11, b_in2.at[pl.ds(0, n_h - 1)], recv_sem)
    for h in range(n_h):
        b_slice[4 * h : 4 * h + 4, :] = b_in2[h]
    gb2_mine[...] = dot_f32(b_slice[...], b_slice[...], ((0,), (0,)))
    send(12, n_ja, row, lambda at: rows_of(gb2_mine, at * n_ka + ka), lambda at: gb2_in.at[ja])
    gb2_in[ja] = rows_of(gb2_mine, g_at)[...]

    b_now = b_slice[...]
    cm_mine[...] = jnp.zeros_like(cm_mine)

    def third(step, carry):
        span = pl.ds(step * per, per)
        weights = (a_slice[pl.ds(pl.multiple_of(step * per, per), per), :][:, None, :] * b_now[None]).reshape(per * j_dev, rank)
        whi, wlo = split2(weights)
        left_hi = thi[span].reshape(per * j_dev, k_dev)
        left_lo = tlo[span].reshape(per * j_dev, k_dev)
        cm_mine[...] += dot_bf16(left_hi, whi, ((0,), (0,))) + (
            dot_bf16(left_hi, wlo, ((0,), (0,))) + dot_bf16(left_lo, whi, ((0,), (0,)))
        )
        return carry
    lax.fori_loop(0, i_dev // per, third, 0)
    for z in range(n_ia):
        for j in range(n_ja):
            low = 2 * (z * n_ja + j)
            cm_parts[j, z] = cm_mine[low : low + 2, :]
    send(13, n_ja, row, lambda at: cm_parts.at[at], lambda at: cm_in.at[ja])
    cm_in[ja] = cm_parts[ja]
    done(12, gb2_in.at[pl.ds(0, n_ja - 1)], recv_sem)
    gather_gram(14, 2, jnp.sum(gb2_in[...], axis=0) * ga_rows[...])
    done(13, cm_in.at[pl.ds(0, n_ja - 1)], recv_sem)
    cm_sum[...] = jnp.sum(cm_in[...], axis=0)
    send(15, n_ia, column, lambda at: cm_sum.at[at], lambda at: cm_in2.at[ia])
    cm_in2[ia] = cm_sum[ia]
    done(14, g_all.at[2, pl.ds(0, rank - g_tall)], recv_sem)
    invert(g_all.at[2])
    done(15, cm_in2.at[pl.ds(0, n_ia - 1)], recv_sem)
    c_out[0] = dot_f32(jnp.sum(cm_in2[...], axis=0), g_all[2], ((1,), (0,)))

    sent = (
        c_in1.at[pl.ds(0, n_ia - 1)], b_in.at[pl.ds(0, n_h - 1)], c_in2.at[pl.ds(0, n_ja - 1)], gb_in.at[pl.ds(0, n_ja - 1)],
        gc_in.at[pl.ds(0, n_ka - 1)], a_in.at[pl.ds(0, n_g - 1)], g_all.at[0, pl.ds(0, rank - g_tall)], a_in2.at[pl.ds(0, n_g - 1)],
        ga_in.at[pl.ds(0, n_ia - 1)], bm_in.at[pl.ds(0, n_h - 1)], g_all.at[1, pl.ds(0, rank - g_tall)], b_in2.at[pl.ds(0, n_h - 1)],
        gb2_in.at[pl.ds(0, n_ja - 1)], cm_in.at[pl.ds(0, n_ja - 1)], g_all.at[2, pl.ds(0, rank - g_tall)], cm_in2.at[pl.ds(0, n_ia - 1)],
    )
    for phase, ref in enumerate(sent):
        done(phase, ref, send_sem)


def solution(mesh):
    n_ia, n_ja, n_ka = mesh.shape["ia"], mesh.shape["ja"], mesh.shape["ka"]
    n_g, n_h = n_ja * n_ka, n_ia * n_ka

    def on_device(tensor, factor_b, factor_c):
        i_dev, j_dev, k_dev = tensor.shape
        rank = factor_b.shape[-1]
        tall = rank // n_g

        def vmem(*shape, dtype=F32):
            return pltpu.VMEM(shape, dtype)

        square = (rank, rank)
        return pl.pallas_call(
            functools.partial(kernel, n_ia, n_ja, n_ka),
            out_shape=(
                jax.ShapeDtypeStruct((1, 4, rank), F32),
                jax.ShapeDtypeStruct((1, 4, rank), F32),
                jax.ShapeDtypeStruct((1, 2, rank), F32),
            ),
            in_specs=[pl.BlockSpec(memory_space=pl.ANY)] + [pl.BlockSpec(memory_space=pltpu.VMEM)] * 2,
            out_specs=(pl.BlockSpec(memory_space=pltpu.VMEM),) * 3,
            scratch_shapes=[
                vmem(i_dev, j_dev, k_dev), vmem(i_dev, j_dev, k_dev, dtype=BF16), vmem(i_dev, j_dev, k_dev, dtype=BF16),
                vmem(i_dev, j_dev, rank),
                vmem(n_ia, 2, rank), vmem(n_ja, n_ia, 2, rank), vmem(k_dev, rank), vmem(n_h, 4, rank), vmem(j_dev, rank),
                vmem(*square), vmem(n_ja, tall, rank), vmem(*square), vmem(n_ka, tall, rank), vmem(tall, rank), vmem(tall, rank),
                vmem(3, tall, rank), vmem(3, *square),
                vmem(n_g, 4, rank), vmem(n_g, 4, rank), vmem(4, rank), vmem(n_g, 4, rank), vmem(i_dev, rank), vmem(*square), vmem(n_ia, tall, rank),
                vmem(n_h, 4, rank), vmem(n_h, 4, rank), vmem(4, rank), vmem(n_h, 4, rank), vmem(j_dev, rank), vmem(*square), vmem(n_ja, tall, rank),
                vmem(k_dev, rank), vmem(n_ja, n_ia, 2, rank), vmem(n_ja, n_ia, 2, rank), vmem(n_ia, 2, rank), vmem(n_ia, 2, rank),
                pltpu.SemaphoreType.DMA((8,)), pltpu.SemaphoreType.DMA((16,)), pltpu.SemaphoreType.DMA((16,)),
            ],
            compiler_params=pltpu.CompilerParams(
                collective_id=0, has_side_effects=True, vmem_limit_bytes=56 * 1024 * 1024
            ),
        )(tensor, factor_b, factor_c)

    return jax.shard_map(
        on_device,
        mesh=mesh,
        in_specs=(P("ia", "ja", "ka"), P("ja", ("ia", "ka"), None), P("ka", ("ia", "ja"), None)),
        out_specs=(
            P("ia", ("ja", "ka"), None),
            P("ja", ("ia", "ka"), None),
            P("ka", ("ia", "ja"), None),
        ),
        check_vma=False,
    )
```

```python
import functools

import jax
import jax.numpy as jnp
from jax import lax
from jax.experimental import pallas as pl
from jax.experimental.pallas import tpu as pltpu
from jax.sharding import PartitionSpec as P

HIGH = lax.Precision.HIGHEST
MESH = pl.DeviceIdType.MESH
F32 = jnp.float32
BF16 = jnp.bfloat16
NB = 32


def dot_f32(x, y, dims):
    return lax.dot_general(x, y, (dims, ((), ())), precision=HIGH, preferred_element_type=F32)


def dot_bf16(x, y, dims):
    return lax.dot_general(x, y, (dims, ((), ())), preferred_element_type=F32)


def split2(x):
    high = x.astype(BF16)
    return high, (x - high.astype(F32)).astype(BF16)


def split3(x):
    first = x.astype(BF16)
    rest = x - first.astype(F32)
    second = rest.astype(BF16)
    return first, second, (rest - second.astype(F32)).astype(BF16)


def spread(value, at):
    return jnp.broadcast_to(value[at : at + 1, :], value.shape)


def eliminate(old, low, steps):
    n = old.shape[1]
    tall, halves, per = old.shape[0] // 8, n // 128, steps // 8
    rows = lax.broadcasted_iota(jnp.int32, (8, 128), 0)
    lanes = lax.broadcasted_iota(jnp.int32, (8, 128), 1)
    parts = [[old[8 * q : 8 * q + 8, 128 * w : 128 * w + 128] for w in range(halves)] for q in range(tall)]

    def lane(q, at):
        return jnp.broadcast_to(parts[q][at // 128][:, at % 128 : at % 128 + 1], (8, 128))

    for group in range(tall // per):
        base = low + steps * group
        mine = range(group * per, (group + 1) * per)
        half, first = base // 128, base % 128
        inside = (lanes >= first) & (lanes < first + steps)
        own = {(q, c): lane(q, base + c) for q in mine for c in range(steps)}
        for q in mine:
            unit = jnp.where(lanes - first == rows + 8 * (q - group * per), 1.0, 0.0)
            parts[q][half] = jnp.where(inside, unit, parts[q][half])
        pivot = spread(own[mine[0], 0], 0)
        for j in range(steps):
            at, r = group * per + j // 8, j % 8
            here = rows == r
            across = {c: spread(own[at, c], r) for c in range(j + 1, steps)}
            inverse = 1.0 / pivot
            if j + 1 < steps:
                then, rn = group * per + (j + 1) // 8, (j + 1) % 8
                pivot = spread(own[then, j + 1], rn) - (spread(own[then, j], rn) * across[j + 1]) * inverse
            pivot_row = [spread(parts[at][w], r) for w in range(halves)]
            for q in mine:
                factor = own[q, j] * inverse
                if q == at:
                    factor = jnp.where(here, -inverse, factor)
                for w in range(halves):
                    kept = jnp.where(here, 0.0, parts[q][w]) if q == at else parts[q][w]
                    parts[q][w] = kept - factor * pivot_row[w]
                for c in range(j + 1, steps):
                    kept = jnp.where(here, 0.0, own[q, c]) if q == at else own[q, c]
                    own[q, c] = kept - factor * across[c]
        done_rows = [[spread(parts[group * per + c // 8][w], c % 8) for w in range(halves)] for c in range(steps)]
        for q in range(tall):
            if q in mine:
                continue
            factors = [lane(q, base + c) for c in range(steps)]
            parts[q][half] = jnp.where(inside, 0.0, parts[q][half])
            for w in range(halves):
                terms = [factors[c] * done_rows[c][w] for c in range(steps)]
                while len(terms) > 1:
                    terms = [x + y for x, y in zip(terms[::2], terms[1::2])]
                parts[q][w] = parts[q][w] - terms[0]
    return jnp.concatenate([jnp.concatenate(part, axis=1) for part in parts], axis=0)


def invert(s_ref, blocks):
    n = s_ref.shape[0]
    lanes_at = lax.broadcasted_iota(jnp.int32, (NB, n), 1)
    all_lanes = lax.broadcasted_iota(jnp.int32, (n, n), 1)
    for block in blocks:
        low = block * NB
        old = s_ref[low : low + NB, :]
        panel = eliminate(old, low, 16)
        signed = jnp.where(lanes_at < low, -old, jnp.where(lanes_at < low + NB, 0.0, old))
        x1, x2, x3 = split3(signed)
        y1, y2, y3 = split3(panel)
        update = dot_bf16(
            jnp.concatenate([x1, x1, x2, x2, x1, x3], axis=0),
            jnp.concatenate([y1, y2, y1, y2, y3, y1], axis=0),
            ((0,), (0,)),
        )
        inside = (all_lanes >= low) & (all_lanes < low + NB)
        s_ref[...] = jnp.where(inside, 0.0, s_ref[...]) - update
        s_ref[low : low + NB, :] = panel


def kernel(
    n_ia, n_ja, n_ka,
    t_hbm, b_ref, c_ref,
    a_out, b_out, c_out,
    t_ref, thi, tlo, p_ref,
    c_in1, c_in2, c_all, b_in, b_all,
    gb_mine, gb_in, gc_mine, gc_in, gc_rows, ga_rows,
    g_send, g_all,
    a_parts, a_in, a_own, a_in2, a_slice, ga_mine, ga_in,
    bm_parts, bm_in, b_own, b_in2, b_slice, gb2_mine, gb2_in,
    cm_mine, cm_parts, cm_in, cm_sum, cm_in2, a_mine, b_mine,
    t_sem, send_sem, recv_sem,
):
    i_dev, j_dev, k_dev = t_hbm.shape
    rank = c_ref.shape[-1]
    ia, ja, ka = lax.axis_index("ia"), lax.axis_index("ja"), lax.axis_index("ka")
    n_g, n_h = n_ja * n_ka, n_ia * n_ka
    g_at = ja * n_ka + ka
    h_at = ia * n_ka + ka
    g_tall = rank // n_g
    n_blocks = rank // NB

    def device(z, j, k):
        return {"ia": z, "ja": j, "ka": k}

    def plane(step):
        at = lax.rem(g_at + step, n_g)
        return at, device(ia, at // n_ka, lax.rem(at, n_ka))

    def column(step):
        at = lax.rem(ia + step, n_ia)
        return at, device(at, ja, ka)

    def column_pair(step):
        at = lax.rem(h_at + step, n_h)
        return at, device(at // n_ka, ja, lax.rem(at, n_ka))

    def row(step):
        at = lax.rem(ja + step, n_ja)
        return at, device(ia, at, ka)

    def send(phase, n, peer, source, target):
        def body(step, carry):
            at, who = peer(step)
            pltpu.make_async_remote_copy(
                src_ref=source(at), dst_ref=target(at), send_sem=send_sem.at[phase],
                recv_sem=recv_sem.at[phase], device_id=who, device_id_type=MESH,
            ).start()
            return carry
        lax.fori_loop(1, n, body, 0)

    def done(phase, ref, sem):
        pltpu.make_async_copy(ref, ref, sem.at[phase]).wait()

    chunks = t_sem.shape[0]
    i_chunk = i_dev // chunks

    def load(at):
        span = pl.ds(at * i_chunk, i_chunk)
        return pltpu.make_async_copy(t_hbm.at[span], t_ref.at[span], t_sem.at[at])

    for at in range(chunks):
        load(at).start()

    barrier = pltpu.get_barrier_semaphore()

    def greet_plane(step, carry):
        pl.semaphore_signal(barrier, inc=1, device_id=plane(step)[1], device_id_type=MESH)
        return carry

    def greet_column(step, carry):
        z = lax.rem(ia + step, n_ia)
        for k in range(n_ka):
            pl.semaphore_signal(barrier, inc=1, device_id=device(z, ja, k), device_id_type=MESH)
        return carry

    lax.fori_loop(1, n_g, greet_plane, 0)
    lax.fori_loop(1, n_ia, greet_column, 0)
    pl.semaphore_wait(barrier, n_g - 1 + (n_ia - 1) * n_ka)

    send(0, n_ia, column, lambda at: c_ref.at[0], lambda at: c_in1.at[ia])
    send(1, n_h, column_pair, lambda at: b_ref.at[0], lambda at: b_in.at[h_at])
    c_in1[ia] = c_ref[0]
    b_in[h_at] = b_ref[0]
    done(0, c_in1.at[pl.ds(0, n_ia - 1)], recv_sem)
    send(2, n_ja, row, lambda at: c_in1, lambda at: c_in2.at[ja])
    c_in2[ja] = c_in1[...]

    for at in range(chunks):
        load(at).wait()

        def split_one(i, carry):
            high, low = split2(t_ref[i])
            thi[i] = high
            tlo[i] = low
            return carry
        lax.fori_loop(at * i_chunk, (at + 1) * i_chunk, split_one, 0)

    done(1, b_in.at[pl.ds(0, n_h - 1)], recv_sem)
    for h in range(n_h):
        b_all[4 * h : 4 * h + 4, :] = b_in[h]
    gb_mine[...] = dot_f32(b_all[...], b_all[...], ((0,), (0,)))

    def rows_of(ref, at):
        return ref.at[pl.ds(pl.multiple_of(at * g_tall, 8), g_tall)]

    send(3, n_ja, row, lambda at: rows_of(gb_mine, at * n_ka + ka), lambda at: gb_in.at[ja])
    done(2, c_in2.at[pl.ds(0, n_ja - 1)], recv_sem)
    for z in range(n_ia):
        for j in range(n_ja):
            low = 2 * (z * n_ja + j)
            c_all[low : low + 2, :] = c_in2[j, z]
    gc_mine[...] = dot_f32(c_all[...], c_all[...], ((0,), (0,)))

    def other(step):
        at = lax.rem(ka + step, n_ka)
        return at, device(ia, ja, at)

    send(4, n_ka, other, lambda at: rows_of(gc_mine, ja * n_ka + at), lambda at: gc_in.at[ka])

    chi, clo = split2(c_all[...])
    per = 16
    b_whole = b_all[...]

    def first(step, carry):
        span = pl.ds(step * per, per)
        left_hi = thi[span].reshape(per * j_dev, k_dev)
        left_lo = tlo[span].reshape(per * j_dev, k_dev)
        inner = dot_bf16(left_hi, chi, ((1,), (0,))) + (
            dot_bf16(left_hi, clo, ((1,), (0,))) + dot_bf16(left_lo, chi, ((1,), (0,)))
        )
        inner = inner.reshape(per, j_dev, rank)
        p_ref[span] = inner
        summed = jnp.sum(inner * b_whole[None], axis=1)
        a_parts[pl.ds(step * (per // 4), per // 4)] = summed.reshape(per // 4, 4, rank)
        return carry
    lax.fori_loop(0, i_dev // per, first, 0)

    send(5, n_g, plane, lambda at: a_parts.at[at], lambda at: a_in.at[g_at])
    a_in[g_at] = a_parts[g_at]

    def gather_gram(phase, slot, rows):
        g_send[slot] = rows
        rows_of(g_all.at[slot], g_at)[...] = rows
        send(phase, n_g, plane, lambda at: g_send.at[slot], lambda at: rows_of(g_all.at[slot], g_at))

    gb_in[ja] = rows_of(gb_mine, g_at)[...]
    gc_in[ka] = rows_of(gc_mine, g_at)[...]
    done(3, gb_in.at[pl.ds(0, n_ja - 1)], recv_sem)
    done(4, gc_in.at[pl.ds(0, n_ka - 1)], recv_sem)
    gc_rows[...] = jnp.sum(gc_in[...], axis=0)
    gather_gram(6, 0, jnp.sum(gb_in[...], axis=0) * gc_rows[...])
    done(5, a_in.at[pl.ds(0, n_g - 1)], recv_sem)
    own = jnp.sum(a_in[...], axis=0)
    a_own[...] = own
    a_in2[g_at] = own
    send(7, n_g, plane, lambda at: a_own, lambda at: a_in2.at[g_at])
    done(6, g_all.at[0, pl.ds(0, rank - g_tall)], recv_sem)
    invert(g_all.at[0], range(n_blocks))
    done(7, a_in2.at[pl.ds(0, n_g - 1)], recv_sem)
    for g in range(n_g):
        a_slice[4 * g : 4 * g + 4, :] = a_in2[g]
    a_slice[...] = dot_f32(a_slice[...], g_all[0], ((1,), (0,)))
    ga_mine[...] = dot_f32(a_slice[...], a_slice[...], ((0,), (0,)))
    send(8, n_ia, column, lambda at: rows_of(ga_mine, g_at), lambda at: ga_in.at[ia])
    ga_in[ia] = rows_of(ga_mine, g_at)[...]

    def second(step, total):
        for e in range(4):
            i = step * 4 + e
            total = total + p_ref[i] * a_slice[pl.ds(i, 1), :]
        return total
    sums = lax.fori_loop(0, i_dev // 4, second, jnp.zeros((j_dev, rank), F32))
    for h in range(n_h):
        bm_parts[h] = sums[4 * h : 4 * h + 4]
    send(9, n_h, column_pair, lambda at: bm_parts.at[at], lambda at: bm_in.at[h_at])
    bm_in[h_at] = bm_parts[h_at]
    done(8, ga_in.at[pl.ds(0, n_ia - 1)], recv_sem)
    ga_rows[...] = jnp.sum(ga_in[...], axis=0)
    gather_gram(10, 1, ga_rows[...] * gc_rows[...])
    done(9, bm_in.at[pl.ds(0, n_h - 1)], recv_sem)
    own = jnp.sum(bm_in[...], axis=0)
    b_own[...] = own
    b_in2[h_at] = own
    send(11, n_h, column_pair, lambda at: b_own, lambda at: b_in2.at[h_at])
    for g in range(n_g):
        a_mine[g] = a_slice[4 * g : 4 * g + 4, :]
    a_out[0] = a_mine[g_at]
    done(10, g_all.at[1, pl.ds(0, rank - g_tall)], recv_sem)
    invert(g_all.at[1], range(n_blocks))
    done(11, b_in2.at[pl.ds(0, n_h - 1)], recv_sem)
    for h in range(n_h):
        b_slice[4 * h : 4 * h + 4, :] = b_in2[h]
    b_slice[...] = dot_f32(b_slice[...], g_all[1], ((1,), (0,)))
    gb2_mine[...] = dot_f32(b_slice[...], b_slice[...], ((0,), (0,)))
    send(12, n_ja, row, lambda at: rows_of(gb2_mine, at * n_ka + ka), lambda at: gb2_in.at[ja])
    gb2_in[ja] = rows_of(gb2_mine, g_at)[...]

    for h in range(n_h):
        b_mine[h] = b_slice[4 * h : 4 * h + 4, :]
    b_out[0] = b_mine[h_at]
    b_now = b_slice[...]
    cm_mine[...] = jnp.zeros_like(cm_mine)

    def third(step, carry):
        span = pl.ds(step * per, per)
        weights = (a_slice[pl.ds(pl.multiple_of(step * per, per), per), :][:, None, :] * b_now[None]).reshape(per * j_dev, rank)
        whi, wlo = split2(weights)
        left_hi = thi[span].reshape(per * j_dev, k_dev)
        left_lo = tlo[span].reshape(per * j_dev, k_dev)
        cm_mine[...] += dot_bf16(left_hi, whi, ((0,), (0,))) + (
            dot_bf16(left_hi, wlo, ((0,), (0,))) + dot_bf16(left_lo, whi, ((0,), (0,)))
        )
        return carry
    lax.fori_loop(0, i_dev // per, third, 0)
    for z in range(n_ia):
        for j in range(n_ja):
            low = 2 * (z * n_ja + j)
            cm_parts[j, z] = cm_mine[low : low + 2, :]
    send(13, n_ja, row, lambda at: cm_parts.at[at], lambda at: cm_in.at[ja])
    cm_in[ja] = cm_parts[ja]
    done(12, gb2_in.at[pl.ds(0, n_ja - 1)], recv_sem)
    gather_gram(14, 2, jnp.sum(gb2_in[...], axis=0) * ga_rows[...])
    done(13, cm_in.at[pl.ds(0, n_ja - 1)], recv_sem)
    cm_sum[...] = jnp.sum(cm_in[...], axis=0)
    send(15, n_ia, column, lambda at: cm_sum.at[at], lambda at: cm_in2.at[ia])
    cm_in2[ia] = cm_sum[ia]
    done(14, g_all.at[2, pl.ds(0, rank - g_tall)], recv_sem)
    invert(g_all.at[2], range(n_blocks))
    done(15, cm_in2.at[pl.ds(0, n_ia - 1)], recv_sem)
    c_out[0] = dot_f32(jnp.sum(cm_in2[...], axis=0), g_all[2], ((1,), (0,)))

    sent = (
        c_in1.at[pl.ds(0, n_ia - 1)], b_in.at[pl.ds(0, n_h - 1)], c_in2.at[pl.ds(0, n_ja - 1)], gb_in.at[pl.ds(0, n_ja - 1)],
        gc_in.at[pl.ds(0, n_ka - 1)], a_in.at[pl.ds(0, n_g - 1)], g_all.at[0, pl.ds(0, rank - g_tall)], a_in2.at[pl.ds(0, n_g - 1)],
        ga_in.at[pl.ds(0, n_ia - 1)], bm_in.at[pl.ds(0, n_h - 1)], g_all.at[1, pl.ds(0, rank - g_tall)], b_in2.at[pl.ds(0, n_h - 1)],
        gb2_in.at[pl.ds(0, n_ja - 1)], cm_in.at[pl.ds(0, n_ja - 1)], g_all.at[2, pl.ds(0, rank - g_tall)], cm_in2.at[pl.ds(0, n_ia - 1)],
    )
    for phase, ref in enumerate(sent):
        done(phase, ref, send_sem)


def solution(mesh):
    n_ia, n_ja, n_ka = mesh.shape["ia"], mesh.shape["ja"], mesh.shape["ka"]
    n_g, n_h = n_ja * n_ka, n_ia * n_ka

    def on_device(tensor, factor_b, factor_c):
        i_dev, j_dev, k_dev = tensor.shape
        rank = factor_b.shape[-1]
        tall = rank // n_g

        def vmem(*shape, dtype=F32):
            return pltpu.VMEM(shape, dtype)

        square = (rank, rank)
        return pl.pallas_call(
            functools.partial(kernel, n_ia, n_ja, n_ka),
            out_shape=(
                jax.ShapeDtypeStruct((1, 4, rank), F32),
                jax.ShapeDtypeStruct((1, 4, rank), F32),
                jax.ShapeDtypeStruct((1, 2, rank), F32),
            ),
            in_specs=[pl.BlockSpec(memory_space=pl.ANY)] + [pl.BlockSpec(memory_space=pltpu.VMEM)] * 2,
            out_specs=(pl.BlockSpec(memory_space=pltpu.VMEM),) * 3,
            scratch_shapes=[
                vmem(i_dev, j_dev, k_dev), vmem(i_dev, j_dev, k_dev, dtype=BF16), vmem(i_dev, j_dev, k_dev, dtype=BF16),
                vmem(i_dev, j_dev, rank),
                vmem(n_ia, 2, rank), vmem(n_ja, n_ia, 2, rank), vmem(k_dev, rank), vmem(n_h, 4, rank), vmem(j_dev, rank),
                vmem(*square), vmem(n_ja, tall, rank), vmem(*square), vmem(n_ka, tall, rank), vmem(tall, rank), vmem(tall, rank),
                vmem(3, tall, rank), vmem(3, *square),
                vmem(n_g, 4, rank), vmem(n_g, 4, rank), vmem(4, rank), vmem(n_g, 4, rank), vmem(i_dev, rank), vmem(*square), vmem(n_ia, tall, rank),
                vmem(n_h, 4, rank), vmem(n_h, 4, rank), vmem(4, rank), vmem(n_h, 4, rank), vmem(j_dev, rank), vmem(*square), vmem(n_ja, tall, rank),
                vmem(k_dev, rank), vmem(n_ja, n_ia, 2, rank), vmem(n_ja, n_ia, 2, rank), vmem(n_ia, 2, rank), vmem(n_ia, 2, rank),
                vmem(n_g, 4, rank), vmem(n_h, 4, rank),
                pltpu.SemaphoreType.DMA((8,)), pltpu.SemaphoreType.DMA((16,)), pltpu.SemaphoreType.DMA((16,)),
            ],
            compiler_params=pltpu.CompilerParams(
                collective_id=0, has_side_effects=True, vmem_limit_bytes=56 * 1024 * 1024
            ),
        )(tensor, factor_b, factor_c)

    return jax.shard_map(
        on_device,
        mesh=mesh,
        in_specs=(P("ia", "ja", "ka"), P("ja", ("ia", "ka"), None), P("ka", ("ia", "ja"), None)),
        out_specs=(
            P("ia", ("ja", "ka"), None),
            P("ja", ("ia", "ka"), None),
            P("ka", ("ia", "ja"), None),
        ),
        check_vma=False,
    )
```

```python
import functools

import jax
import jax.numpy as jnp
from jax import lax
from jax.experimental import pallas as pl
from jax.experimental.pallas import tpu as pltpu
from jax.sharding import PartitionSpec as P

HIGH = lax.Precision.HIGHEST
MESH = pl.DeviceIdType.MESH
F32 = jnp.float32
BF16 = jnp.bfloat16
NB = 32


def dot_f32(x, y, dims):
    return lax.dot_general(x, y, (dims, ((), ())), precision=HIGH, preferred_element_type=F32)


def dot_bf16(x, y, dims):
    return lax.dot_general(x, y, (dims, ((), ())), preferred_element_type=F32)


def split2(x):
    high = x.astype(BF16)
    return high, (x - high.astype(F32)).astype(BF16)


def split3(x):
    first = x.astype(BF16)
    rest = x - first.astype(F32)
    second = rest.astype(BF16)
    return first, second, (rest - second.astype(F32)).astype(BF16)


def spread(value, at):
    return jnp.broadcast_to(value[at : at + 1, :], value.shape)


def eliminate(old, low, steps):
    n = old.shape[1]
    tall, halves, per = old.shape[0] // 8, n // 128, steps // 8
    rows = lax.broadcasted_iota(jnp.int32, (8, 128), 0)
    lanes = lax.broadcasted_iota(jnp.int32, (8, 128), 1)
    parts = [[old[8 * q : 8 * q + 8, 128 * w : 128 * w + 128] for w in range(halves)] for q in range(tall)]

    def lane(q, at):
        return jnp.broadcast_to(parts[q][at // 128][:, at % 128 : at % 128 + 1], (8, 128))

    for group in range(tall // per):
        base = low + steps * group
        mine = range(group * per, (group + 1) * per)
        half, first = base // 128, base % 128
        inside = (lanes >= first) & (lanes < first + steps)
        own = {(q, c): lane(q, base + c) for q in mine for c in range(steps)}
        for q in mine:
            unit = jnp.where(lanes - first == rows + 8 * (q - group * per), 1.0, 0.0)
            parts[q][half] = jnp.where(inside, unit, parts[q][half])
        pivot = spread(own[mine[0], 0], 0)
        for j in range(steps):
            at, r = group * per + j // 8, j % 8
            here = rows == r
            across = {c: spread(own[at, c], r) for c in range(j + 1, steps)}
            inverse = 1.0 / pivot
            if j + 1 < steps:
                then, rn = group * per + (j + 1) // 8, (j + 1) % 8
                pivot = spread(own[then, j + 1], rn) - (spread(own[then, j], rn) * across[j + 1]) * inverse
            pivot_row = [spread(parts[at][w], r) for w in range(halves)]
            for q in mine:
                factor = own[q, j] * inverse
                if q == at:
                    factor = jnp.where(here, -inverse, factor)
                for w in range(halves):
                    kept = jnp.where(here, 0.0, parts[q][w]) if q == at else parts[q][w]
                    parts[q][w] = kept - factor * pivot_row[w]
                for c in range(j + 1, steps):
                    kept = jnp.where(here, 0.0, own[q, c]) if q == at else own[q, c]
                    own[q, c] = kept - factor * across[c]
        done_rows = [[spread(parts[group * per + c // 8][w], c % 8) for w in range(halves)] for c in range(steps)]
        for q in range(tall):
            if q in mine:
                continue
            factors = [lane(q, base + c) for c in range(steps)]
            parts[q][half] = jnp.where(inside, 0.0, parts[q][half])
            for w in range(halves):
                terms = [factors[c] * done_rows[c][w] for c in range(steps)]
                while len(terms) > 1:
                    terms = [x + y for x, y in zip(terms[::2], terms[1::2])]
                parts[q][w] = parts[q][w] - terms[0]
    return jnp.concatenate([jnp.concatenate(part, axis=1) for part in parts], axis=0)


def invert(s_ref, blocks):
    n = s_ref.shape[0]
    lanes_at = lax.broadcasted_iota(jnp.int32, (NB, n), 1)
    all_lanes = lax.broadcasted_iota(jnp.int32, (n, n), 1)
    for block in blocks:
        low = block * NB
        old = s_ref[low : low + NB, :]
        panel = eliminate(old, low, 16)
        signed = jnp.where(lanes_at < low, -old, jnp.where(lanes_at < low + NB, 0.0, old))
        x1, x2, x3 = split3(signed)
        y1, y2, y3 = split3(panel)
        update = dot_bf16(
            jnp.concatenate([x1, x1, x2, x2, x1, x3], axis=0),
            jnp.concatenate([y1, y2, y1, y2, y3, y1], axis=0),
            ((0,), (0,)),
        )
        inside = (all_lanes >= low) & (all_lanes < low + NB)
        s_ref[...] = jnp.where(inside, 0.0, s_ref[...]) - update
        s_ref[low : low + NB, :] = panel


def kernel(
    n_ia, n_ja, n_ka,
    t_hbm, b_ref, c_ref,
    a_out, b_out, c_out,
    t_ref, thi, tlo, p_ref,
    c_in1, c_in2, c_all, b_in, b_all,
    gb_mine, gb_in, gc_mine, gc_in, gc_rows, ga_rows,
    g_send, g_all,
    a_parts, a_in, a_own, a_in2, a_slice, ga_mine, ga_in,
    bm_parts, bm_in, b_own, b_in2, b_slice, gb2_mine, gb2_in,
    cm_mine, cm_parts, cm_in, cm_sum, cm_in2, a_mine, b_mine,
    t_sem, send_sem, recv_sem,
):
    i_dev, j_dev, k_dev = t_hbm.shape
    rank = c_ref.shape[-1]
    ia, ja, ka = lax.axis_index("ia"), lax.axis_index("ja"), lax.axis_index("ka")
    n_g, n_h = n_ja * n_ka, n_ia * n_ka
    g_at = ja * n_ka + ka
    h_at = ia * n_ka + ka
    g_tall = rank // n_g
    n_blocks = rank // NB

    def device(z, j, k):
        return {"ia": z, "ja": j, "ka": k}

    def plane(step):
        at = lax.rem(g_at + step, n_g)
        return at, device(ia, at // n_ka, lax.rem(at, n_ka))

    def column(step):
        at = lax.rem(ia + step, n_ia)
        return at, device(at, ja, ka)

    def column_pair(step):
        at = lax.rem(h_at + step, n_h)
        return at, device(at // n_ka, ja, lax.rem(at, n_ka))

    def row(step):
        at = lax.rem(ja + step, n_ja)
        return at, device(ia, at, ka)

    def start(phase, source, target, who):
        pltpu.make_async_remote_copy(
            src_ref=source, dst_ref=target, send_sem=send_sem.at[phase],
            recv_sem=recv_sem.at[phase], device_id=who, device_id_type=MESH,
        ).start()

    def send(phase, n, peer, source, target):
        def body(step, carry):
            at, who = peer(step)
            start(phase, source(at), target(at), who)
            return carry
        lax.fori_loop(1, n, body, 0)

    def done(phase, ref, sem):
        pltpu.make_async_copy(ref, ref, sem.at[phase]).wait()

    chunks = t_sem.shape[0]
    i_chunk = i_dev // chunks

    def load(at):
        span = pl.ds(at * i_chunk, i_chunk)
        return pltpu.make_async_copy(t_hbm.at[span], t_ref.at[span], t_sem.at[at])

    for at in range(chunks):
        load(at).start()

    barrier = pltpu.get_barrier_semaphore()

    def greet_plane(step, carry):
        pl.semaphore_signal(barrier, inc=1, device_id=plane(step)[1], device_id_type=MESH)
        return carry

    def greet_column(step, carry):
        z = lax.rem(ia + step, n_ia)
        for k in range(n_ka):
            pl.semaphore_signal(barrier, inc=1, device_id=device(z, ja, k), device_id_type=MESH)
        return carry

    lax.fori_loop(1, n_g, greet_plane, 0)
    lax.fori_loop(1, n_ia, greet_column, 0)
    pl.semaphore_wait(barrier, n_g - 1 + (n_ia - 1) * n_ka)

    send(0, n_ia, column, lambda at: c_ref.at[0], lambda at: c_in1.at[ia])
    send(1, n_h, column_pair, lambda at: b_ref.at[0], lambda at: b_in.at[h_at])
    c_in1[ia] = c_ref[0]
    b_in[h_at] = b_ref[0]
    done(0, c_in1.at[pl.ds(0, n_ia - 1)], recv_sem)
    send(2, n_ja, row, lambda at: c_in1, lambda at: c_in2.at[ja])
    c_in2[ja] = c_in1[...]

    for at in range(chunks):
        load(at).wait()

        def split_one(i, carry):
            high, low = split2(t_ref[i])
            thi[i] = high
            tlo[i] = low
            return carry
        lax.fori_loop(at * i_chunk, (at + 1) * i_chunk, split_one, 0)

    done(1, b_in.at[pl.ds(0, n_h - 1)], recv_sem)
    for h in range(n_h):
        b_all[4 * h : 4 * h + 4, :] = b_in[h]
    gb_mine[...] = dot_f32(b_all[...], b_all[...], ((0,), (0,)))

    def rows_of(ref, at):
        return ref.at[pl.ds(pl.multiple_of(at * g_tall, 8), g_tall)]

    send(3, n_ja, row, lambda at: rows_of(gb_mine, at * n_ka + ka), lambda at: gb_in.at[ja])
    done(2, c_in2.at[pl.ds(0, n_ja - 1)], recv_sem)
    for z in range(n_ia):
        for j in range(n_ja):
            low = 2 * (z * n_ja + j)
            c_all[low : low + 2, :] = c_in2[j, z]
    gc_mine[...] = dot_f32(c_all[...], c_all[...], ((0,), (0,)))

    def other(step):
        at = lax.rem(ka + step, n_ka)
        return at, device(ia, ja, at)

    send(4, n_ka, other, lambda at: rows_of(gc_mine, ja * n_ka + at), lambda at: gc_in.at[ka])

    chi, clo = split2(c_all[...])
    per = 16
    b_whole = b_all[...]

    pieces, steps = per // 4, i_dev // per

    def first(step, carry):
        at = lax.rem(g_at // pieces + 1 + step, steps)
        span = pl.ds(at * per, per)
        left_hi = thi[span].reshape(per * j_dev, k_dev)
        left_lo = tlo[span].reshape(per * j_dev, k_dev)
        inner = dot_bf16(left_hi, chi, ((1,), (0,))) + (
            dot_bf16(left_hi, clo, ((1,), (0,))) + dot_bf16(left_lo, chi, ((1,), (0,)))
        )
        inner = inner.reshape(per, j_dev, rank)
        p_ref[span] = inner
        summed = jnp.sum(inner * b_whole[None], axis=1)
        a_parts[pl.ds(at * pieces, pieces)] = summed.reshape(pieces, 4, rank)
        for e in range(pieces):
            to = at * pieces + e

            @pl.when(to != g_at)
            def _():
                start(5, a_parts.at[to], a_in.at[g_at], device(ia, to // n_ka, lax.rem(to, n_ka)))
        return carry

    def gather_gram(phase, slot, rows):
        g_send[slot] = rows
        rows_of(g_all.at[slot], g_at)[...] = rows
        send(phase, n_g, plane, lambda at: g_send.at[slot], lambda at: rows_of(g_all.at[slot], g_at))

    lax.fori_loop(0, steps // 2, first, 0)
    gb_in[ja] = rows_of(gb_mine, g_at)[...]
    gc_in[ka] = rows_of(gc_mine, g_at)[...]
    done(3, gb_in.at[pl.ds(0, n_ja - 1)], recv_sem)
    done(4, gc_in.at[pl.ds(0, n_ka - 1)], recv_sem)
    gc_rows[...] = jnp.sum(gc_in[...], axis=0)
    gather_gram(6, 0, jnp.sum(gb_in[...], axis=0) * gc_rows[...])
    lax.fori_loop(steps // 2, steps, first, 0)
    a_in[g_at] = a_parts[g_at]

    done(5, a_in.at[pl.ds(0, n_g - 1)], recv_sem)
    own = jnp.sum(a_in[...], axis=0)
    a_own[...] = own
    a_in2[g_at] = own
    send(7, n_g, plane, lambda at: a_own, lambda at: a_in2.at[g_at])
    done(6, g_all.at[0, pl.ds(0, rank - g_tall)], recv_sem)
    invert(g_all.at[0], range(n_blocks))
    done(7, a_in2.at[pl.ds(0, n_g - 1)], recv_sem)
    for g in range(n_g):
        a_slice[4 * g : 4 * g + 4, :] = a_in2[g]
    a_slice[...] = dot_f32(a_slice[...], g_all[0], ((1,), (0,)))
    ga_mine[...] = dot_f32(a_slice[...], a_slice[...], ((0,), (0,)))
    send(8, n_ia, column, lambda at: rows_of(ga_mine, g_at), lambda at: ga_in.at[ia])
    ga_in[ia] = rows_of(ga_mine, g_at)[...]

    def second(step, total):
        for e in range(4):
            i = step * 4 + e
            total = total + p_ref[i] * a_slice[pl.ds(i, 1), :]
        return total
    sums = lax.fori_loop(0, i_dev // 4, second, jnp.zeros((j_dev, rank), F32))
    for h in range(n_h):
        bm_parts[h] = sums[4 * h : 4 * h + 4]
    send(9, n_h, column_pair, lambda at: bm_parts.at[at], lambda at: bm_in.at[h_at])
    bm_in[h_at] = bm_parts[h_at]
    done(8, ga_in.at[pl.ds(0, n_ia - 1)], recv_sem)
    ga_rows[...] = jnp.sum(ga_in[...], axis=0)
    gather_gram(10, 1, ga_rows[...] * gc_rows[...])
    done(9, bm_in.at[pl.ds(0, n_h - 1)], recv_sem)
    own = jnp.sum(bm_in[...], axis=0)
    b_own[...] = own
    b_in2[h_at] = own
    send(11, n_h, column_pair, lambda at: b_own, lambda at: b_in2.at[h_at])
    for g in range(n_g):
        a_mine[g] = a_slice[4 * g : 4 * g + 4, :]
    a_out[0] = a_mine[g_at]
    done(10, g_all.at[1, pl.ds(0, rank - g_tall)], recv_sem)
    invert(g_all.at[1], range(n_blocks))
    done(11, b_in2.at[pl.ds(0, n_h - 1)], recv_sem)
    for h in range(n_h):
        b_slice[4 * h : 4 * h + 4, :] = b_in2[h]
    b_slice[...] = dot_f32(b_slice[...], g_all[1], ((1,), (0,)))
    gb2_mine[...] = dot_f32(b_slice[...], b_slice[...], ((0,), (0,)))
    send(12, n_ja, row, lambda at: rows_of(gb2_mine, at * n_ka + ka), lambda at: gb2_in.at[ja])
    gb2_in[ja] = rows_of(gb2_mine, g_at)[...]

    for h in range(n_h):
        b_mine[h] = b_slice[4 * h : 4 * h + 4, :]
    b_out[0] = b_mine[h_at]
    b_now = b_slice[...]
    cm_mine[...] = jnp.zeros_like(cm_mine)

    def third(step, carry):
        span = pl.ds(step * per, per)
        weights = (a_slice[pl.ds(pl.multiple_of(step * per, per), per), :][:, None, :] * b_now[None]).reshape(per * j_dev, rank)
        whi, wlo = split2(weights)
        left_hi = thi[span].reshape(per * j_dev, k_dev)
        left_lo = tlo[span].reshape(per * j_dev, k_dev)
        cm_mine[...] += dot_bf16(left_hi, whi, ((0,), (0,))) + (
            dot_bf16(left_hi, wlo, ((0,), (0,))) + dot_bf16(left_lo, whi, ((0,), (0,)))
        )
        return carry
    early = steps * 3 // 4
    lax.fori_loop(0, early, third, 0)
    done(12, gb2_in.at[pl.ds(0, n_ja - 1)], recv_sem)
    gather_gram(14, 2, jnp.sum(gb2_in[...], axis=0) * ga_rows[...])
    lax.fori_loop(early, steps, third, 0)
    for z in range(n_ia):
        for j in range(n_ja):
            low = 2 * (z * n_ja + j)
            cm_parts[j, z] = cm_mine[low : low + 2, :]
    send(13, n_ja, row, lambda at: cm_parts.at[at], lambda at: cm_in.at[ja])
    cm_in[ja] = cm_parts[ja]
    done(13, cm_in.at[pl.ds(0, n_ja - 1)], recv_sem)
    cm_sum[...] = jnp.sum(cm_in[...], axis=0)
    send(15, n_ia, column, lambda at: cm_sum.at[at], lambda at: cm_in2.at[ia])
    cm_in2[ia] = cm_sum[ia]
    done(14, g_all.at[2, pl.ds(0, rank - g_tall)], recv_sem)
    invert(g_all.at[2], range(n_blocks))
    done(15, cm_in2.at[pl.ds(0, n_ia - 1)], recv_sem)
    c_out[0] = dot_f32(jnp.sum(cm_in2[...], axis=0), g_all[2], ((1,), (0,)))

    sent = (
        c_in1.at[pl.ds(0, n_ia - 1)], b_in.at[pl.ds(0, n_h - 1)], c_in2.at[pl.ds(0, n_ja - 1)], gb_in.at[pl.ds(0, n_ja - 1)],
        gc_in.at[pl.ds(0, n_ka - 1)], a_in.at[pl.ds(0, n_g - 1)], g_all.at[0, pl.ds(0, rank - g_tall)], a_in2.at[pl.ds(0, n_g - 1)],
        ga_in.at[pl.ds(0, n_ia - 1)], bm_in.at[pl.ds(0, n_h - 1)], g_all.at[1, pl.ds(0, rank - g_tall)], b_in2.at[pl.ds(0, n_h - 1)],
        gb2_in.at[pl.ds(0, n_ja - 1)], cm_in.at[pl.ds(0, n_ja - 1)], g_all.at[2, pl.ds(0, rank - g_tall)], cm_in2.at[pl.ds(0, n_ia - 1)],
    )
    for phase, ref in enumerate(sent):
        done(phase, ref, send_sem)


def hand_over(a_ref, b_ref, c_ref, a_out, b_out, c_out, sem):
    copies = [
        pltpu.make_async_copy(source, target, sem.at[at])
        for at, (source, target) in enumerate(((a_ref, a_out), (b_ref, b_out), (c_ref, c_out)))
    ]
    for copy in copies:
        copy.start()
    for copy in copies:
        copy.wait()


def solution(mesh):
    n_ia, n_ja, n_ka = mesh.shape["ia"], mesh.shape["ja"], mesh.shape["ka"]
    n_g, n_h = n_ja * n_ka, n_ia * n_ka

    def on_device(tensor, factor_b, factor_c):
        i_dev, j_dev, k_dev = tensor.shape
        rank = factor_b.shape[-1]
        tall = rank // n_g

        def vmem(*shape, dtype=F32):
            return pltpu.VMEM(shape, dtype)

        square = (rank, rank)
        outs = tuple(jax.ShapeDtypeStruct((1, rows, rank), F32) for rows in (4, 4, 2))
        found = pl.pallas_call(
            functools.partial(kernel, n_ia, n_ja, n_ka),
            out_shape=outs,
            in_specs=[pl.BlockSpec(memory_space=pl.ANY)] + [pl.BlockSpec(memory_space=pltpu.VMEM)] * 2,
            out_specs=(pl.BlockSpec(memory_space=pltpu.VMEM),) * 3,
            scratch_shapes=[
                vmem(i_dev, j_dev, k_dev), vmem(i_dev, j_dev, k_dev, dtype=BF16), vmem(i_dev, j_dev, k_dev, dtype=BF16),
                vmem(i_dev, j_dev, rank),
                vmem(n_ia, 2, rank), vmem(n_ja, n_ia, 2, rank), vmem(k_dev, rank), vmem(n_h, 4, rank), vmem(j_dev, rank),
                vmem(*square), vmem(n_ja, tall, rank), vmem(*square), vmem(n_ka, tall, rank), vmem(tall, rank), vmem(tall, rank),
                vmem(3, tall, rank), vmem(3, *square),
                vmem(n_g, 4, rank), vmem(n_g, 4, rank), vmem(4, rank), vmem(n_g, 4, rank), vmem(i_dev, rank), vmem(*square), vmem(n_ia, tall, rank),
                vmem(n_h, 4, rank), vmem(n_h, 4, rank), vmem(4, rank), vmem(n_h, 4, rank), vmem(j_dev, rank), vmem(*square), vmem(n_ja, tall, rank),
                vmem(k_dev, rank), vmem(n_ja, n_ia, 2, rank), vmem(n_ja, n_ia, 2, rank), vmem(n_ia, 2, rank), vmem(n_ia, 2, rank),
                vmem(n_g, 4, rank), vmem(n_h, 4, rank),
                pltpu.SemaphoreType.DMA((8,)), pltpu.SemaphoreType.DMA((16,)), pltpu.SemaphoreType.DMA((16,)),
            ],
            compiler_params=pltpu.CompilerParams(
                collective_id=0, has_side_effects=True, vmem_limit_bytes=56 * 1024 * 1024
            ),
        )(tensor, factor_b, factor_c)
        return pl.pallas_call(
            hand_over,
            out_shape=outs,
            in_specs=[pl.BlockSpec(memory_space=pl.ANY)] * 3,
            out_specs=(pl.BlockSpec(memory_space=pl.ANY),) * 3,
            scratch_shapes=[pltpu.SemaphoreType.DMA((3,))],
        )(*found)

    return jax.shard_map(
        on_device,
        mesh=mesh,
        in_specs=(P("ia", "ja", "ka"), P("ja", ("ia", "ka"), None), P("ka", ("ia", "ja"), None)),
        out_specs=(
            P("ia", ("ja", "ka"), None),
            P("ja", ("ia", "ka"), None),
            P("ka", ("ia", "ja"), None),
        ),
        check_vma=False,
    )
```

```python
import functools

import jax
import jax.numpy as jnp
from jax import lax
from jax.experimental import pallas as pl
from jax.experimental.pallas import tpu as pltpu
from jax.sharding import PartitionSpec as P

HIGH = lax.Precision.HIGHEST
MESH = pl.DeviceIdType.MESH
F32 = jnp.float32
BF16 = jnp.bfloat16
NB = 32
NEAR = [(1, 0, 0), (-1, 0, 0), (0, 1, 0), (0, -1, 0), (1, 1, 0), (1, -1, 0), (-1, 1, 0), (-1, -1, 0), (2, 0, 0), (0, 2, 0)]
ACROSS = [(0, 0, 1), (1, 0, -1), (-1, 0, 1), (0, 1, -1), (0, -1, 1)]


def dot_f32(x, y, dims):
    return lax.dot_general(x, y, (dims, ((), ())), precision=HIGH, preferred_element_type=F32)


def dot_bf16(x, y, dims):
    return lax.dot_general(x, y, (dims, ((), ())), preferred_element_type=F32)


def split2(x):
    high = x.astype(BF16)
    return high, (x - high.astype(F32)).astype(BF16)


def split3(x):
    first = x.astype(BF16)
    rest = x - first.astype(F32)
    second = rest.astype(BF16)
    return first, second, (rest - second.astype(F32)).astype(BF16)


def spread(value, at):
    return jnp.broadcast_to(value[at : at + 1, :], value.shape)


def eliminate(old, low, steps):
    n = old.shape[1]
    tall, halves, per = old.shape[0] // 8, n // 128, steps // 8
    rows = lax.broadcasted_iota(jnp.int32, (8, 128), 0)
    lanes = lax.broadcasted_iota(jnp.int32, (8, 128), 1)
    parts = [[old[8 * q : 8 * q + 8, 128 * w : 128 * w + 128] for w in range(halves)] for q in range(tall)]

    def lane(q, at):
        return jnp.broadcast_to(parts[q][at // 128][:, at % 128 : at % 128 + 1], (8, 128))

    for group in range(tall // per):
        base = low + steps * group
        mine = range(group * per, (group + 1) * per)
        half, first = base // 128, base % 128
        inside = (lanes >= first) & (lanes < first + steps)
        own = {(q, c): lane(q, base + c) for q in mine for c in range(steps)}
        for q in mine:
            unit = jnp.where(lanes - first == rows + 8 * (q - group * per), 1.0, 0.0)
            parts[q][half] = jnp.where(inside, unit, parts[q][half])
        pivot = spread(own[mine[0], 0], 0)
        for j in range(steps):
            at, r = group * per + j // 8, j % 8
            here = rows == r
            across = {c: spread(own[at, c], r) for c in range(j + 1, steps)}
            inverse = 1.0 / pivot
            if j + 1 < steps:
                then, rn = group * per + (j + 1) // 8, (j + 1) % 8
                pivot = spread(own[then, j + 1], rn) - (spread(own[then, j], rn) * across[j + 1]) * inverse
            pivot_row = [spread(parts[at][w], r) for w in range(halves)]
            for q in mine:
                factor = own[q, j] * inverse
                if q == at:
                    factor = jnp.where(here, -inverse, factor)
                for w in range(halves):
                    kept = jnp.where(here, 0.0, parts[q][w]) if q == at else parts[q][w]
                    parts[q][w] = kept - factor * pivot_row[w]
                for c in range(j + 1, steps):
                    kept = jnp.where(here, 0.0, own[q, c]) if q == at else own[q, c]
                    own[q, c] = kept - factor * across[c]
        done_rows = [[spread(parts[group * per + c // 8][w], c % 8) for w in range(halves)] for c in range(steps)]
        for q in range(tall):
            if q in mine:
                continue
            factors = [lane(q, base + c) for c in range(steps)]
            parts[q][half] = jnp.where(inside, 0.0, parts[q][half])
            for w in range(halves):
                terms = [factors[c] * done_rows[c][w] for c in range(steps)]
                while len(terms) > 1:
                    terms = [x + y for x, y in zip(terms[::2], terms[1::2])]
                parts[q][w] = parts[q][w] - terms[0]
    return jnp.concatenate([jnp.concatenate(part, axis=1) for part in parts], axis=0)


def invert(s_ref, blocks):
    n = s_ref.shape[0]
    lanes_at = lax.broadcasted_iota(jnp.int32, (NB, n), 1)
    all_lanes = lax.broadcasted_iota(jnp.int32, (n, n), 1)
    for block in blocks:
        low = block * NB
        old = s_ref[low : low + NB, :]
        panel = eliminate(old, low, 16)
        signed = jnp.where(lanes_at < low, -old, jnp.where(lanes_at < low + NB, 0.0, old))
        x1, x2, x3 = split3(signed)
        y1, y2, y3 = split3(panel)
        update = dot_bf16(
            jnp.concatenate([x1, x1, x2, x2, x1, x3], axis=0),
            jnp.concatenate([y1, y2, y1, y2, y3, y1], axis=0),
            ((0,), (0,)),
        )
        inside = (all_lanes >= low) & (all_lanes < low + NB)
        s_ref[...] = jnp.where(inside, 0.0, s_ref[...]) - update
        s_ref[low : low + NB, :] = panel


def kernel(
    n_ia, n_ja, n_ka,
    t_hbm, b_ref, c_ref,
    a_out, b_out, c_out,
    t_ref, thi, tlo, p_ref,
    c_in1, c_in2, c_all, b_in, b_all,
    gb_mine, gb_in, gc_mine, gc_in, gc_rows, ga_rows,
    g_send, g_all,
    a_parts, a_in, a_own, a_in2, a_slice, ga_mine, ga_in,
    bm_parts, bm_in, b_own, b_in2, b_slice, gb2_mine, gb2_in,
    cm_mine, cm_parts, cm_in, cm_sum, cm_in2, a_mine, b_mine,
    t_sem, send_sem, recv_sem,
):
    i_dev, j_dev, k_dev = t_hbm.shape
    rank = c_ref.shape[-1]
    ia, ja, ka = lax.axis_index("ia"), lax.axis_index("ja"), lax.axis_index("ka")
    n_g, n_h = n_ja * n_ka, n_ia * n_ka
    g_at = ja * n_ka + ka
    h_at = ia * n_ka + ka
    g_tall = rank // n_g
    n_blocks = rank // NB

    def device(z, j, k):
        return {"ia": z, "ja": j, "ka": k}

    def plane(step):
        at = lax.rem(g_at + step, n_g)
        return at, device(ia, at // n_ka, lax.rem(at, n_ka))

    def column(step):
        at = lax.rem(ia + step, n_ia)
        return at, device(at, ja, ka)

    def column_pair(step):
        at = lax.rem(h_at + step, n_h)
        return at, device(at // n_ka, ja, lax.rem(at, n_ka))

    def row(step):
        at = lax.rem(ja + step, n_ja)
        return at, device(ia, at, ka)

    def start(phase, source, target, who):
        pltpu.make_async_remote_copy(
            src_ref=source, dst_ref=target, send_sem=send_sem.at[phase],
            recv_sem=recv_sem.at[phase], device_id=who, device_id_type=MESH,
        ).start()

    def piece(z, j, k):
        odd = lax.rem(z, 2)
        return lax.rem(j + odd * (n_ja // 2), n_ja) * n_ka + lax.rem(k + odd, n_ka)

    piece_at = piece(ia, ja, ka)
    chip_x, chip_y, core = ja // 4, ka * 2 + lax.rem(ja // 2, 2), lax.rem(ja, 2)

    def chip(offset, other):
        x, y = lax.rem(chip_x + offset[0] + 4, 4), lax.rem(chip_y + offset[1] + 4, 4)
        z, c = lax.rem(ia + offset[2] + n_ia, n_ia), lax.rem(core + other, 2)
        return device(z, x * 4 + lax.rem(y, 2) * 2 + c, y // 2)

    def send(phase, n, peer, source, target):
        def body(step, carry):
            at, who = peer(step)
            start(phase, source(at), target(at), who)
            return carry
        lax.fori_loop(1, n, body, 0)

    def done(phase, ref, sem):
        pltpu.make_async_copy(ref, ref, sem.at[phase]).wait()

    chunks = t_sem.shape[0]
    i_chunk = i_dev // chunks

    def load(at):
        span = pl.ds(at * i_chunk, i_chunk)
        return pltpu.make_async_copy(t_hbm.at[span], t_ref.at[span], t_sem.at[at])

    for at in range(chunks):
        load(at).start()

    barrier = pltpu.get_barrier_semaphore()

    def greet_plane(step, carry):
        pl.semaphore_signal(barrier, inc=1, device_id=plane(step)[1], device_id_type=MESH)
        return carry

    def greet_column(step, carry):
        z = lax.rem(ia + step, n_ia)
        for k in range(n_ka):
            pl.semaphore_signal(barrier, inc=1, device_id=device(z, ja, k), device_id_type=MESH)
        return carry

    lax.fori_loop(1, n_g, greet_plane, 0)
    lax.fori_loop(1, n_ia, greet_column, 0)
    beyond = [(offset, other) for offset in ACROSS for other in (0, 1) if (offset[:2], other) != ((0, 0), 0)]
    for (x, y, z), other in beyond:
        pl.semaphore_signal(barrier, inc=1, device_id=chip((-x, -y, -z), other), device_id_type=MESH)
    pl.semaphore_wait(barrier, n_g - 1 + (n_ia - 1) * n_ka + len(beyond))

    send(0, n_ia, column, lambda at: c_ref.at[0], lambda at: c_in1.at[ia])
    send(1, n_h, column_pair, lambda at: b_ref.at[0], lambda at: b_in.at[h_at])
    c_in1[ia] = c_ref[0]
    b_in[h_at] = b_ref[0]
    done(0, c_in1.at[pl.ds(0, n_ia - 1)], recv_sem)
    send(2, n_ja, row, lambda at: c_in1, lambda at: c_in2.at[ja])
    c_in2[ja] = c_in1[...]

    for at in range(chunks):
        load(at).wait()

        def split_one(i, carry):
            high, low = split2(t_ref[i])
            thi[i] = high
            tlo[i] = low
            return carry
        lax.fori_loop(at * i_chunk, (at + 1) * i_chunk, split_one, 0)

    done(1, b_in.at[pl.ds(0, n_h - 1)], recv_sem)
    for h in range(n_h):
        b_all[4 * h : 4 * h + 4, :] = b_in[h]
    gb_mine[...] = dot_f32(b_all[...], b_all[...], ((0,), (0,)))

    def rows_of(ref, at):
        return ref.at[pl.ds(pl.multiple_of(at * g_tall, 8), g_tall)]

    send(3, n_ja, row, lambda at: rows_of(gb_mine, piece(ia, at, ka)), lambda at: gb_in.at[ja])
    done(2, c_in2.at[pl.ds(0, n_ja - 1)], recv_sem)
    for z in range(n_ia):
        for j in range(n_ja):
            low = 2 * (z * n_ja + j)
            c_all[low : low + 2, :] = c_in2[j, z]
    gc_mine[...] = dot_f32(c_all[...], c_all[...], ((0,), (0,)))

    def other(step):
        at = lax.rem(ka + step, n_ka)
        return at, device(ia, ja, at)

    send(4, n_ka, other, lambda at: rows_of(gc_mine, piece(ia, ja, at)), lambda at: gc_in.at[ka])

    chi, clo = split2(c_all[...])
    per = 32
    b_whole = b_all[...]

    pieces, steps = per // 4, i_dev // per

    def first(step, carry):
        at = lax.rem(g_at // pieces + 1 + step, steps)
        span = pl.ds(at * per, per)
        left_hi = thi[span].reshape(per * j_dev, k_dev)
        left_lo = tlo[span].reshape(per * j_dev, k_dev)
        inner = dot_bf16(left_hi, chi, ((1,), (0,))) + (
            dot_bf16(left_hi, clo, ((1,), (0,))) + dot_bf16(left_lo, chi, ((1,), (0,)))
        )
        inner = inner.reshape(per, j_dev, rank)
        p_ref[span] = inner
        summed = jnp.sum(inner * b_whole[None], axis=1)
        a_parts[pl.ds(at * pieces, pieces)] = summed.reshape(pieces, 4, rank)
        for e in range(pieces):
            to = at * pieces + e

            @pl.when(to != g_at)
            def _():
                start(5, a_parts.at[to], a_in.at[g_at], device(ia, to // n_ka, lax.rem(to, n_ka)))
        return carry

    def gather_gram(phase, slot, rows):
        g_send[slot] = rows
        rows_of(g_all.at[slot], piece_at)[...] = rows
        for offset, other in [((0, 0, 0), 1)] + [(offset, other) for offset in ACROSS + NEAR[::-1] for other in (0, 1)]:
            start(phase, g_send.at[slot], rows_of(g_all.at[slot], piece_at), chip(offset, other))

    lax.fori_loop(0, steps // 2, first, 0)
    gb_in[ja] = rows_of(gb_mine, piece_at)[...]
    gc_in[ka] = rows_of(gc_mine, piece_at)[...]
    done(3, gb_in.at[pl.ds(0, n_ja - 1)], recv_sem)
    done(4, gc_in.at[pl.ds(0, n_ka - 1)], recv_sem)
    gc_rows[...] = jnp.sum(gc_in[...], axis=0)
    gather_gram(6, 0, jnp.sum(gb_in[...], axis=0) * gc_rows[...])
    lax.fori_loop(steps // 2, steps, first, 0)
    a_in[g_at] = a_parts[g_at]

    done(5, a_in.at[pl.ds(0, n_g - 1)], recv_sem)
    own = jnp.sum(a_in[...], axis=0)
    a_own[...] = own
    a_in2[g_at] = own
    send(7, n_g, plane, lambda at: a_own, lambda at: a_in2.at[g_at])
    done(6, g_all.at[0, pl.ds(0, rank - g_tall)], recv_sem)
    invert(g_all.at[0], range(n_blocks))
    done(7, a_in2.at[pl.ds(0, n_g - 1)], recv_sem)
    for g in range(n_g):
        a_slice[4 * g : 4 * g + 4, :] = a_in2[g]
    a_slice[...] = dot_f32(a_slice[...], g_all[0], ((1,), (0,)))
    ga_mine[...] = dot_f32(a_slice[...], a_slice[...], ((0,), (0,)))
    send(8, n_ia, column, lambda at: rows_of(ga_mine, piece(at, ja, ka)), lambda at: ga_in.at[ia])
    ga_in[ia] = rows_of(ga_mine, piece_at)[...]

    def second(step, total):
        for e in range(4):
            i = step * 4 + e
            total = total + p_ref[i] * a_slice[pl.ds(i, 1), :]
        return total
    sums = lax.fori_loop(0, i_dev // 4, second, jnp.zeros((j_dev, rank), F32))
    for h in range(n_h):
        bm_parts[h] = sums[4 * h : 4 * h + 4]
    send(9, n_h, column_pair, lambda at: bm_parts.at[at], lambda at: bm_in.at[h_at])
    bm_in[h_at] = bm_parts[h_at]
    done(8, ga_in.at[pl.ds(0, n_ia - 1)], recv_sem)
    ga_rows[...] = jnp.sum(ga_in[...], axis=0)
    gather_gram(10, 1, ga_rows[...] * gc_rows[...])
    done(9, bm_in.at[pl.ds(0, n_h - 1)], recv_sem)
    own = jnp.sum(bm_in[...], axis=0)
    b_own[...] = own
    b_in2[h_at] = own
    send(11, n_h, column_pair, lambda at: b_own, lambda at: b_in2.at[h_at])
    for g in range(n_g):
        a_mine[g] = a_slice[4 * g : 4 * g + 4, :]
    a_out[0] = a_mine[g_at]
    done(10, g_all.at[1, pl.ds(0, rank - g_tall)], recv_sem)
    invert(g_all.at[1], range(n_blocks))
    done(11, b_in2.at[pl.ds(0, n_h - 1)], recv_sem)
    for h in range(n_h):
        b_slice[4 * h : 4 * h + 4, :] = b_in2[h]
    b_slice[...] = dot_f32(b_slice[...], g_all[1], ((1,), (0,)))
    gb2_mine[...] = dot_f32(b_slice[...], b_slice[...], ((0,), (0,)))
    send(12, n_ja, row, lambda at: rows_of(gb2_mine, piece(ia, at, ka)), lambda at: gb2_in.at[ja])
    gb2_in[ja] = rows_of(gb2_mine, piece_at)[...]

    for h in range(n_h):
        b_mine[h] = b_slice[4 * h : 4 * h + 4, :]
    b_out[0] = b_mine[h_at]
    b_now = b_slice[...]
    cm_mine[...] = jnp.zeros_like(cm_mine)

    def third(step, carry):
        span = pl.ds(step * per, per)
        weights = (a_slice[pl.ds(pl.multiple_of(step * per, per), per), :][:, None, :] * b_now[None]).reshape(per * j_dev, rank)
        whi, wlo = split2(weights)
        left_hi = thi[span].reshape(per * j_dev, k_dev)
        left_lo = tlo[span].reshape(per * j_dev, k_dev)
        cm_mine[...] += dot_bf16(left_hi, whi, ((0,), (0,))) + (
            dot_bf16(left_hi, wlo, ((0,), (0,))) + dot_bf16(left_lo, whi, ((0,), (0,)))
        )
        return carry
    early = steps * 3 // 4
    lax.fori_loop(0, early, third, 0)
    done(12, gb2_in.at[pl.ds(0, n_ja - 1)], recv_sem)
    gather_gram(14, 2, jnp.sum(gb2_in[...], axis=0) * ga_rows[...])
    lax.fori_loop(early, steps, third, 0)
    for z in range(n_ia):
        for j in range(n_ja):
            low = 2 * (z * n_ja + j)
            cm_parts[j, z] = cm_mine[low : low + 2, :]
    send(13, n_ja, row, lambda at: cm_parts.at[at], lambda at: cm_in.at[ja])
    cm_in[ja] = cm_parts[ja]
    done(13, cm_in.at[pl.ds(0, n_ja - 1)], recv_sem)
    cm_sum[...] = jnp.sum(cm_in[...], axis=0)
    send(15, n_ia, column, lambda at: cm_sum.at[at], lambda at: cm_in2.at[ia])
    cm_in2[ia] = cm_sum[ia]
    done(14, g_all.at[2, pl.ds(0, rank - g_tall)], recv_sem)
    invert(g_all.at[2], range(n_blocks))
    done(15, cm_in2.at[pl.ds(0, n_ia - 1)], recv_sem)
    c_out[0] = dot_f32(jnp.sum(cm_in2[...], axis=0), g_all[2], ((1,), (0,)))

    sent = (
        c_in1.at[pl.ds(0, n_ia - 1)], b_in.at[pl.ds(0, n_h - 1)], c_in2.at[pl.ds(0, n_ja - 1)], gb_in.at[pl.ds(0, n_ja - 1)],
        gc_in.at[pl.ds(0, n_ka - 1)], a_in.at[pl.ds(0, n_g - 1)], g_all.at[0, pl.ds(0, rank - g_tall)], a_in2.at[pl.ds(0, n_g - 1)],
        ga_in.at[pl.ds(0, n_ia - 1)], bm_in.at[pl.ds(0, n_h - 1)], g_all.at[1, pl.ds(0, rank - g_tall)], b_in2.at[pl.ds(0, n_h - 1)],
        gb2_in.at[pl.ds(0, n_ja - 1)], cm_in.at[pl.ds(0, n_ja - 1)], g_all.at[2, pl.ds(0, rank - g_tall)], cm_in2.at[pl.ds(0, n_ia - 1)],
    )
    for phase, ref in enumerate(sent):
        done(phase, ref, send_sem)


def hand_over(a_ref, b_ref, c_ref, a_out, b_out, c_out, sem):
    copies = [
        pltpu.make_async_copy(source, target, sem.at[at])
        for at, (source, target) in enumerate(((a_ref, a_out), (b_ref, b_out), (c_ref, c_out)))
    ]
    for copy in copies:
        copy.start()
    for copy in copies:
        copy.wait()


def solution(mesh):
    n_ia, n_ja, n_ka = mesh.shape["ia"], mesh.shape["ja"], mesh.shape["ka"]
    n_g, n_h = n_ja * n_ka, n_ia * n_ka

    def on_device(tensor, factor_b, factor_c):
        i_dev, j_dev, k_dev = tensor.shape
        rank = factor_b.shape[-1]
        tall = rank // n_g

        def vmem(*shape, dtype=F32):
            return pltpu.VMEM(shape, dtype)

        square = (rank, rank)
        outs = tuple(jax.ShapeDtypeStruct((1, rows, rank), F32) for rows in (4, 4, 2))
        found = pl.pallas_call(
            functools.partial(kernel, n_ia, n_ja, n_ka),
            out_shape=outs,
            in_specs=[pl.BlockSpec(memory_space=pl.ANY)] + [pl.BlockSpec(memory_space=pltpu.VMEM)] * 2,
            out_specs=(pl.BlockSpec(memory_space=pltpu.VMEM),) * 3,
            scratch_shapes=[
                vmem(i_dev, j_dev, k_dev), vmem(i_dev, j_dev, k_dev, dtype=BF16), vmem(i_dev, j_dev, k_dev, dtype=BF16),
                vmem(i_dev, j_dev, rank),
                vmem(n_ia, 2, rank), vmem(n_ja, n_ia, 2, rank), vmem(k_dev, rank), vmem(n_h, 4, rank), vmem(j_dev, rank),
                vmem(*square), vmem(n_ja, tall, rank), vmem(*square), vmem(n_ka, tall, rank), vmem(tall, rank), vmem(tall, rank),
                vmem(3, tall, rank), vmem(3, *square),
                vmem(n_g, 4, rank), vmem(n_g, 4, rank), vmem(4, rank), vmem(n_g, 4, rank), vmem(i_dev, rank), vmem(*square), vmem(n_ia, tall, rank),
                vmem(n_h, 4, rank), vmem(n_h, 4, rank), vmem(4, rank), vmem(n_h, 4, rank), vmem(j_dev, rank), vmem(*square), vmem(n_ja, tall, rank),
                vmem(k_dev, rank), vmem(n_ja, n_ia, 2, rank), vmem(n_ja, n_ia, 2, rank), vmem(n_ia, 2, rank), vmem(n_ia, 2, rank),
                vmem(n_g, 4, rank), vmem(n_h, 4, rank),
                pltpu.SemaphoreType.DMA((8,)), pltpu.SemaphoreType.DMA((16,)), pltpu.SemaphoreType.DMA((16,)),
            ],
            compiler_params=pltpu.CompilerParams(
                collective_id=0, has_side_effects=True, vmem_limit_bytes=56 * 1024 * 1024
            ),
        )(tensor, factor_b, factor_c)
        return pl.pallas_call(
            hand_over,
            out_shape=outs,
            in_specs=[pl.BlockSpec(memory_space=pl.ANY)] * 3,
            out_specs=(pl.BlockSpec(memory_space=pl.ANY),) * 3,
            scratch_shapes=[pltpu.SemaphoreType.DMA((3,))],
        )(*found)

    return jax.shard_map(
        on_device,
        mesh=mesh,
        in_specs=(P("ia", "ja", "ka"), P("ja", ("ia", "ka"), None), P("ka", ("ia", "ja"), None)),
        out_specs=(
            P("ia", ("ja", "ka"), None),
            P("ja", ("ia", "ka"), None),
            P("ka", ("ia", "ja"), None),
        ),
        check_vma=False,
    )
```

```python
import functools

import jax
import jax.numpy as jnp
from jax import lax
from jax.experimental import pallas as pl
from jax.experimental.pallas import tpu as pltpu
from jax.sharding import PartitionSpec as P

HIGH = lax.Precision.HIGHEST
MESH = pl.DeviceIdType.MESH
F32 = jnp.float32
BF16 = jnp.bfloat16
NB = 32
NEAR = [(1, 0, 0), (-1, 0, 0), (0, 1, 0), (0, -1, 0), (1, 1, 0), (1, -1, 0), (-1, 1, 0), (-1, -1, 0), (2, 0, 0), (0, 2, 0)]
ACROSS = [(0, 0, 1), (1, 0, -1), (-1, 0, 1), (0, 1, -1), (0, -1, 1)]


def dot_f32(x, y, dims):
    return lax.dot_general(x, y, (dims, ((), ())), precision=HIGH, preferred_element_type=F32)


def dot_bf16(x, y, dims):
    return lax.dot_general(x, y, (dims, ((), ())), preferred_element_type=F32)


def split2(x):
    high = x.astype(BF16)
    return high, (x - high.astype(F32)).astype(BF16)


def split3(x):
    first = x.astype(BF16)
    rest = x - first.astype(F32)
    second = rest.astype(BF16)
    return first, second, (rest - second.astype(F32)).astype(BF16)


def spread(value, at):
    return jnp.broadcast_to(value[at : at + 1, :], value.shape)


def eliminate(old, low, steps):
    n = old.shape[1]
    tall, halves, per = old.shape[0] // 8, n // 128, steps // 8
    rows = lax.broadcasted_iota(jnp.int32, (8, 128), 0)
    lanes = lax.broadcasted_iota(jnp.int32, (8, 128), 1)
    parts = [[old[8 * q : 8 * q + 8, 128 * w : 128 * w + 128] for w in range(halves)] for q in range(tall)]

    def lane(q, at):
        return jnp.broadcast_to(parts[q][at // 128][:, at % 128 : at % 128 + 1], (8, 128))

    for group in range(tall // per):
        base = low + steps * group
        mine = range(group * per, (group + 1) * per)
        half, first = base // 128, base % 128
        inside = (lanes >= first) & (lanes < first + steps)
        own = {(q, c): lane(q, base + c) for q in mine for c in range(steps)}
        for q in mine:
            unit = jnp.where(lanes - first == rows + 8 * (q - group * per), 1.0, 0.0)
            parts[q][half] = jnp.where(inside, unit, parts[q][half])
        pivot = spread(own[mine[0], 0], 0)
        for j in range(steps):
            at, r = group * per + j // 8, j % 8
            here = rows == r
            across = {c: spread(own[at, c], r) for c in range(j + 1, steps)}
            inverse = 1.0 / pivot
            if j + 1 < steps:
                then, rn = group * per + (j + 1) // 8, (j + 1) % 8
                pivot = spread(own[then, j + 1], rn) - (spread(own[then, j], rn) * across[j + 1]) * inverse
            pivot_row = [spread(parts[at][w], r) for w in range(halves)]
            for q in mine:
                factor = own[q, j] * inverse
                if q == at:
                    factor = jnp.where(here, -inverse, factor)
                for w in range(halves):
                    kept = jnp.where(here, 0.0, parts[q][w]) if q == at else parts[q][w]
                    parts[q][w] = kept - factor * pivot_row[w]
                for c in range(j + 1, steps):
                    kept = jnp.where(here, 0.0, own[q, c]) if q == at else own[q, c]
                    own[q, c] = kept - factor * across[c]
        done_rows = [[spread(parts[group * per + c // 8][w], c % 8) for w in range(halves)] for c in range(steps)]
        for q in range(tall):
            if q in mine:
                continue
            factors = [lane(q, base + c) for c in range(steps)]
            parts[q][half] = jnp.where(inside, 0.0, parts[q][half])
            for w in range(halves):
                terms = [factors[c] * done_rows[c][w] for c in range(steps)]
                while len(terms) > 1:
                    terms = [x + y for x, y in zip(terms[::2], terms[1::2])]
                parts[q][w] = parts[q][w] - terms[0]
    return jnp.concatenate([jnp.concatenate(part, axis=1) for part in parts], axis=0)


def invert(s_ref, blocks):
    n = s_ref.shape[0]
    lanes_at = lax.broadcasted_iota(jnp.int32, (NB, n), 1)
    all_lanes = lax.broadcasted_iota(jnp.int32, (n, n), 1)
    for block in blocks:
        low = block * NB
        old = s_ref[low : low + NB, :]
        panel = eliminate(old, low, 16)
        signed = jnp.where(lanes_at < low, -old, jnp.where(lanes_at < low + NB, 0.0, old))
        x1, x2, x3 = split3(signed)
        y1, y2, y3 = split3(panel)
        update = dot_bf16(
            jnp.concatenate([x1, x1, x2, x2, x1, x3], axis=0),
            jnp.concatenate([y1, y2, y1, y2, y3, y1], axis=0),
            ((0,), (0,)),
        )
        inside = (all_lanes >= low) & (all_lanes < low + NB)
        s_ref[...] = jnp.where(inside, 0.0, s_ref[...]) - update
        s_ref[low : low + NB, :] = panel


def kernel(
    n_ia, n_ja, n_ka,
    t_hbm, b_ref, c_ref,
    a_out, b_out, c_out,
    t_ref, thi, tlo, p_ref,
    c_in1, c_in2, c_all, b_in, b_all,
    gb_mine, gb_in, gc_mine, gc_in, gc_rows, ga_rows,
    g_send, g_all,
    a_parts, a_in, a_own, a_in2, a_slice, ga_mine, ga_in,
    bm_parts, bm_in, b_own, b_in2, b_slice, gb2_mine, gb2_in,
    cm_mine, cm_parts, cm_in, cm_sum, cm_in2, a_mine, b_mine,
    t_sem, send_sem, recv_sem,
):
    i_dev, j_dev, k_dev = t_hbm.shape
    rank = c_ref.shape[-1]
    ia, ja, ka = lax.axis_index("ia"), lax.axis_index("ja"), lax.axis_index("ka")
    n_g, n_h = n_ja * n_ka, n_ia * n_ka
    g_at = ja * n_ka + ka
    h_at = ia * n_ka + ka
    g_tall = rank // n_g
    n_blocks = rank // NB

    def device(z, j, k):
        return {"ia": z, "ja": j, "ka": k}

    def far_first(step, n):
        return n // 2 + step // 2 * (2 * lax.rem(step, 2) - 1)

    def plane(step):
        at = lax.rem(g_at + far_first(step, n_g), n_g)
        return at, device(ia, at // n_ka, lax.rem(at, n_ka))

    def column(step):
        at = lax.rem(ia + far_first(step, n_ia), n_ia)
        return at, device(at, ja, ka)

    def column_pair(step):
        at = lax.rem(h_at + far_first(step, n_h), n_h)
        return at, device(at // n_ka, ja, lax.rem(at, n_ka))

    def row(step):
        at = lax.rem(ja + far_first(step, n_ja), n_ja)
        return at, device(ia, at, ka)

    def start(phase, source, target, who):
        pltpu.make_async_remote_copy(
            src_ref=source, dst_ref=target, send_sem=send_sem.at[phase],
            recv_sem=recv_sem.at[phase], device_id=who, device_id_type=MESH,
        ).start()

    def piece(z, j, k):
        odd = lax.rem(z, 2)
        return lax.rem(j + odd * (n_ja // 2), n_ja) * n_ka + lax.rem(k + odd, n_ka)

    piece_at = piece(ia, ja, ka)
    chip_x, chip_y, core = ja // 4, ka * 2 + lax.rem(ja // 2, 2), lax.rem(ja, 2)

    def chip(offset, other):
        x, y = lax.rem(chip_x + offset[0] + 4, 4), lax.rem(chip_y + offset[1] + 4, 4)
        z, c = lax.rem(ia + offset[2] + n_ia, n_ia), lax.rem(core + other, 2)
        return device(z, x * 4 + lax.rem(y, 2) * 2 + c, y // 2)

    def send(phase, n, peer, source, target):
        def body(step, carry):
            at, who = peer(step)
            start(phase, source(at), target(at), who)
            return carry
        lax.fori_loop(1, n, body, 0)

    def done(phase, ref, sem):
        pltpu.make_async_copy(ref, ref, sem.at[phase]).wait()

    chunks = t_sem.shape[0]
    i_chunk = i_dev // chunks

    def load(at):
        span = pl.ds(at * i_chunk, i_chunk)
        return pltpu.make_async_copy(t_hbm.at[span], t_ref.at[span], t_sem.at[at])

    for at in range(chunks):
        load(at).start()

    barrier = pltpu.get_barrier_semaphore()

    def greet_plane(step, carry):
        pl.semaphore_signal(barrier, inc=1, device_id=plane(step)[1], device_id_type=MESH)
        return carry

    def greet_column(step, carry):
        z = column(step)[0]
        for k in range(n_ka):
            pl.semaphore_signal(barrier, inc=1, device_id=device(z, ja, k), device_id_type=MESH)
        return carry

    lax.fori_loop(1, n_ia, greet_column, 0)
    lax.fori_loop(1, n_g, greet_plane, 0)
    beyond = [(offset, other) for offset in ACROSS for other in (0, 1) if (offset[:2], other) != ((0, 0), 0)]
    for (x, y, z), other in beyond:
        pl.semaphore_signal(barrier, inc=1, device_id=chip((-x, -y, -z), other), device_id_type=MESH)
    pl.semaphore_wait(barrier, n_g - 1 + (n_ia - 1) * n_ka + len(beyond))

    for step in (4, 3, 5, 2, 6, 1, 7):
        who = device(lax.rem(ia + step, n_ia), ja, ka)
        start(0 if step in (1, 2, 6, 7) else 16, c_ref.at[0], c_in1.at[(10 - step) % 8], who)
    send(1, n_h, column_pair, lambda at: b_ref.at[0], lambda at: b_in.at[h_at])
    c_in1[2] = c_ref[0]
    b_in[h_at] = b_ref[0]
    near, rest = pl.ds(0, 5), pl.ds(5, 3)
    done(0, c_in1.at[pl.ds(0, 4)], recv_sem)
    send(2, n_ja, row, lambda at: c_in1.at[near], lambda at: c_in2.at[ja, near])
    done(16, c_in1.at[pl.ds(0, 3)], recv_sem)
    send(17, n_ja, row, lambda at: c_in1.at[rest], lambda at: c_in2.at[ja, rest])
    c_in2[ja] = c_in1[...]

    for at in range(chunks):
        load(at).wait()

        def split_one(i, carry):
            high, low = split2(t_ref[i])
            thi[i] = high
            tlo[i] = low
            return carry
        lax.fori_loop(at * i_chunk, (at + 1) * i_chunk, split_one, 0)

    done(1, b_in.at[pl.ds(0, n_h - 1)], recv_sem)
    for h in range(n_h):
        b_all[4 * h : 4 * h + 4, :] = b_in[h]
    gb_mine[...] = dot_f32(b_all[...], b_all[...], ((0,), (0,)))

    def rows_of(ref, at):
        return ref.at[pl.ds(pl.multiple_of(at * g_tall, 8), g_tall)]

    send(3, n_ja, row, lambda at: rows_of(gb_mine, piece(ia, at, ka)), lambda at: gb_in.at[ja])
    for phase, slots in ((2, range(5)), (17, range(5, 8))):
        done(phase, c_in2.at[pl.ds(0, n_ja - 1), pl.ds(slots[0], len(slots))], recv_sem)
        for slot in slots:
            z = lax.rem(ia + slot + n_ia - 2, n_ia)
            for j in range(n_ja):
                c_all[z, 2 * j : 2 * j + 2, :] = c_in2[j, slot]
    c_whole = c_all[...].reshape(k_dev, rank)
    gc_mine[...] = dot_f32(c_whole, c_whole, ((0,), (0,)))

    def other(step):
        at = lax.rem(ka + step, n_ka)
        return at, device(ia, ja, at)

    send(4, n_ka, other, lambda at: rows_of(gc_mine, piece(ia, ja, at)), lambda at: gc_in.at[ka])

    chi, clo = split2(c_whole)
    per = 32
    b_whole = b_all[...]

    pieces, steps = per // 4, i_dev // per
    early = steps * 3 // 4

    def first(step, carry):
        at = lax.rem(g_at // pieces + 1 + step, steps)
        span = pl.ds(at * per, per)
        left_hi = thi[span].reshape(per * j_dev, k_dev)
        left_lo = tlo[span].reshape(per * j_dev, k_dev)
        inner = dot_bf16(left_hi, chi, ((1,), (0,))) + (
            dot_bf16(left_hi, clo, ((1,), (0,))) + dot_bf16(left_lo, chi, ((1,), (0,)))
        )
        inner = inner.reshape(per, j_dev, rank)
        p_ref[span] = inner
        summed = jnp.sum(inner * b_whole[None], axis=1)
        a_parts[pl.ds(at * pieces, pieces)] = summed.reshape(pieces, 4, rank)
        for e in range(pieces):
            to = at * pieces + e

            @pl.when(to != g_at)
            def _():
                start(5, a_parts.at[to], a_in.at[g_at], device(ia, to // n_ka, lax.rem(to, n_ka)))
        return carry

    def gather_gram(phase, slot, rows):
        g_send[slot] = rows
        rows_of(g_all.at[slot], piece_at)[...] = rows
        for offset, other in [((0, 0, 0), 1)] + [(offset, other) for offset in ACROSS + NEAR[::-1] for other in (0, 1)]:
            start(phase, g_send.at[slot], rows_of(g_all.at[slot], piece_at), chip(offset, other))

    lax.fori_loop(0, early, first, 0)
    gb_in[ja] = rows_of(gb_mine, piece_at)[...]
    gc_in[ka] = rows_of(gc_mine, piece_at)[...]
    done(3, gb_in.at[pl.ds(0, n_ja - 1)], recv_sem)
    done(4, gc_in.at[pl.ds(0, n_ka - 1)], recv_sem)
    gc_rows[...] = jnp.sum(gc_in[...], axis=0)
    gather_gram(6, 0, jnp.sum(gb_in[...], axis=0) * gc_rows[...])
    lax.fori_loop(early, steps, first, 0)
    a_in[g_at] = a_parts[g_at]

    done(6, g_all.at[0, pl.ds(0, rank - g_tall)], recv_sem)
    invert(g_all.at[0], range(3))
    done(5, a_in.at[pl.ds(0, n_g - 1)], recv_sem)
    own = jnp.sum(a_in[...], axis=0)
    a_own[...] = own
    a_in2[g_at] = own
    send(7, n_g, plane, lambda at: a_own, lambda at: a_in2.at[g_at])
    invert(g_all.at[0], range(3, n_blocks))
    done(7, a_in2.at[pl.ds(0, n_g - 1)], recv_sem)
    for g in range(n_g):
        a_slice[4 * g : 4 * g + 4, :] = a_in2[g]
    a_slice[...] = dot_f32(a_slice[...], g_all[0], ((1,), (0,)))
    ga_mine[...] = dot_f32(a_slice[...], a_slice[...], ((0,), (0,)))
    send(8, n_ia, column, lambda at: rows_of(ga_mine, piece(at, ja, ka)), lambda at: ga_in.at[ia])
    ga_in[ia] = rows_of(ga_mine, piece_at)[...]

    def second(step, total):
        for e in range(4):
            i = step * 4 + e
            total = total + p_ref[i] * a_slice[pl.ds(i, 1), :]
        return total
    sums = lax.fori_loop(0, i_dev // 4, second, jnp.zeros((j_dev, rank), F32))
    for h in range(n_h):
        bm_parts[h] = sums[4 * h : 4 * h + 4]
    send(9, n_h, column_pair, lambda at: bm_parts.at[at], lambda at: bm_in.at[h_at])
    bm_in[h_at] = bm_parts[h_at]
    done(8, ga_in.at[pl.ds(0, n_ia - 1)], recv_sem)
    ga_rows[...] = jnp.sum(ga_in[...], axis=0)
    gather_gram(10, 1, ga_rows[...] * gc_rows[...])
    done(9, bm_in.at[pl.ds(0, n_h - 1)], recv_sem)
    own = jnp.sum(bm_in[...], axis=0)
    b_own[...] = own
    b_in2[h_at] = own
    send(11, n_h, column_pair, lambda at: b_own, lambda at: b_in2.at[h_at])
    for g in range(n_g):
        a_mine[g] = a_slice[4 * g : 4 * g + 4, :]
    a_out[0] = a_mine[g_at]
    done(10, g_all.at[1, pl.ds(0, rank - g_tall)], recv_sem)
    invert(g_all.at[1], range(n_blocks))
    done(11, b_in2.at[pl.ds(0, n_h - 1)], recv_sem)
    for h in range(n_h):
        b_slice[4 * h : 4 * h + 4, :] = b_in2[h]
    b_slice[...] = dot_f32(b_slice[...], g_all[1], ((1,), (0,)))
    gb2_mine[...] = dot_f32(b_slice[...], b_slice[...], ((0,), (0,)))
    send(12, n_ja, row, lambda at: rows_of(gb2_mine, piece(ia, at, ka)), lambda at: gb2_in.at[ja])
    gb2_in[ja] = rows_of(gb2_mine, piece_at)[...]

    for h in range(n_h):
        b_mine[h] = b_slice[4 * h : 4 * h + 4, :]
    b_out[0] = b_mine[h_at]
    b_now = b_slice[...]
    cm_mine[...] = jnp.zeros_like(cm_mine)

    def third(step, carry):
        span = pl.ds(step * per, per)
        weights = (a_slice[pl.ds(pl.multiple_of(step * per, per), per), :][:, None, :] * b_now[None]).reshape(per * j_dev, rank)
        whi, wlo = split2(weights)
        left_hi = thi[span].reshape(per * j_dev, k_dev)
        left_lo = tlo[span].reshape(per * j_dev, k_dev)
        cm_mine[...] += dot_bf16(left_hi, whi, ((0,), (0,))) + (
            dot_bf16(left_hi, wlo, ((0,), (0,))) + dot_bf16(left_lo, whi, ((0,), (0,)))
        )
        return carry
    lax.fori_loop(0, early, third, 0)
    done(12, gb2_in.at[pl.ds(0, n_ja - 1)], recv_sem)
    gather_gram(14, 2, jnp.sum(gb2_in[...], axis=0) * ga_rows[...])
    lax.fori_loop(early, steps, third, 0)
    for z in range(n_ia):
        for j in range(n_ja):
            low = 2 * (z * n_ja + j)
            cm_parts[j, z] = cm_mine[low : low + 2, :]
    send(13, n_ja, row, lambda at: cm_parts.at[at], lambda at: cm_in.at[ja])
    cm_in[ja] = cm_parts[ja]
    done(14, g_all.at[2, pl.ds(0, rank - g_tall)], recv_sem)
    invert(g_all.at[2], range(n_blocks // 2))
    done(13, cm_in.at[pl.ds(0, n_ja - 1)], recv_sem)
    cm_sum[...] = jnp.sum(cm_in[...], axis=0)
    send(15, n_ia, column, lambda at: cm_sum.at[at], lambda at: cm_in2.at[ia])
    cm_in2[ia] = cm_sum[ia]
    invert(g_all.at[2], range(n_blocks // 2, n_blocks))
    done(15, cm_in2.at[pl.ds(0, n_ia - 1)], recv_sem)
    c_out[0] = dot_f32(jnp.sum(cm_in2[...], axis=0), g_all[2], ((1,), (0,)))

    sent = (
        c_in1.at[pl.ds(0, 4)], b_in.at[pl.ds(0, n_h - 1)], c_in2.at[pl.ds(0, n_ja - 1), near], gb_in.at[pl.ds(0, n_ja - 1)],
        gc_in.at[pl.ds(0, n_ka - 1)], a_in.at[pl.ds(0, n_g - 1)], g_all.at[0, pl.ds(0, rank - g_tall)], a_in2.at[pl.ds(0, n_g - 1)],
        ga_in.at[pl.ds(0, n_ia - 1)], bm_in.at[pl.ds(0, n_h - 1)], g_all.at[1, pl.ds(0, rank - g_tall)], b_in2.at[pl.ds(0, n_h - 1)],
        gb2_in.at[pl.ds(0, n_ja - 1)], cm_in.at[pl.ds(0, n_ja - 1)], g_all.at[2, pl.ds(0, rank - g_tall)], cm_in2.at[pl.ds(0, n_ia - 1)],
        c_in1.at[pl.ds(0, 3)], c_in2.at[pl.ds(0, n_ja - 1), rest],
    )
    for phase, ref in enumerate(sent):
        done(phase, ref, send_sem)


def hand_over(a_ref, b_ref, c_ref, a_out, b_out, c_out, sem):
    copies = [
        pltpu.make_async_copy(source, target, sem.at[at])
        for at, (source, target) in enumerate(((a_ref, a_out), (b_ref, b_out), (c_ref, c_out)))
    ]
    for copy in copies:
        copy.start()
    for copy in copies:
        copy.wait()


def solution(mesh):
    n_ia, n_ja, n_ka = mesh.shape["ia"], mesh.shape["ja"], mesh.shape["ka"]
    n_g, n_h = n_ja * n_ka, n_ia * n_ka

    def on_device(tensor, factor_b, factor_c):
        i_dev, j_dev, k_dev = tensor.shape
        rank = factor_b.shape[-1]
        tall = rank // n_g

        def vmem(*shape, dtype=F32):
            return pltpu.VMEM(shape, dtype)

        square = (rank, rank)
        outs = tuple(jax.ShapeDtypeStruct((1, rows, rank), F32) for rows in (4, 4, 2))
        found = pl.pallas_call(
            functools.partial(kernel, n_ia, n_ja, n_ka),
            out_shape=outs,
            in_specs=[pl.BlockSpec(memory_space=pl.ANY)] + [pl.BlockSpec(memory_space=pltpu.VMEM)] * 2,
            out_specs=(pl.BlockSpec(memory_space=pltpu.VMEM),) * 3,
            scratch_shapes=[
                vmem(i_dev, j_dev, k_dev), vmem(i_dev, j_dev, k_dev, dtype=BF16), vmem(i_dev, j_dev, k_dev, dtype=BF16),
                vmem(i_dev, j_dev, rank),
                vmem(n_ia, 2, rank), vmem(n_ja, n_ia, 2, rank), vmem(n_ia, k_dev // n_ia, rank), vmem(n_h, 4, rank), vmem(j_dev, rank),
                vmem(*square), vmem(n_ja, tall, rank), vmem(*square), vmem(n_ka, tall, rank), vmem(tall, rank), vmem(tall, rank),
                vmem(3, tall, rank), vmem(3, *square),
                vmem(n_g, 4, rank), vmem(n_g, 4, rank), vmem(4, rank), vmem(n_g, 4, rank), vmem(i_dev, rank), vmem(*square), vmem(n_ia, tall, rank),
                vmem(n_h, 4, rank), vmem(n_h, 4, rank), vmem(4, rank), vmem(n_h, 4, rank), vmem(j_dev, rank), vmem(*square), vmem(n_ja, tall, rank),
                vmem(k_dev, rank), vmem(n_ja, n_ia, 2, rank), vmem(n_ja, n_ia, 2, rank), vmem(n_ia, 2, rank), vmem(n_ia, 2, rank),
                vmem(n_g, 4, rank), vmem(n_h, 4, rank),
                pltpu.SemaphoreType.DMA((8,)), pltpu.SemaphoreType.DMA((18,)), pltpu.SemaphoreType.DMA((18,)),
            ],
            compiler_params=pltpu.CompilerParams(
                collective_id=0, has_side_effects=True, vmem_limit_bytes=56 * 1024 * 1024
            ),
        )(tensor, factor_b, factor_c)
        return pl.pallas_call(
            hand_over,
            out_shape=outs,
            in_specs=[pl.BlockSpec(memory_space=pl.ANY)] * 3,
            out_specs=(pl.BlockSpec(memory_space=pl.ANY),) * 3,
            scratch_shapes=[pltpu.SemaphoreType.DMA((3,))],
        )(*found)

    return jax.shard_map(
        on_device,
        mesh=mesh,
        in_specs=(P("ia", "ja", "ka"), P("ja", ("ia", "ka"), None), P("ka", ("ia", "ja"), None)),
        out_specs=(
            P("ia", ("ja", "ka"), None),
            P("ja", ("ia", "ka"), None),
            P("ka", ("ia", "ja"), None),
        ),
        check_vma=False,
    )
```

```python
import functools

import jax
import jax.numpy as jnp
from jax import lax
from jax.experimental import pallas as pl
from jax.experimental.pallas import tpu as pltpu
from jax.sharding import PartitionSpec as P

HIGH = lax.Precision.HIGHEST
MESH = pl.DeviceIdType.MESH
F32 = jnp.float32
BF16 = jnp.bfloat16
NB = 32
NEAR = [(1, 0, 0), (-1, 0, 0), (0, 1, 0), (0, -1, 0), (1, 1, 0), (1, -1, 0), (-1, 1, 0), (-1, -1, 0), (2, 0, 0), (0, 2, 0)]
ACROSS = [(0, 0, 1), (1, 0, -1), (-1, 0, 1), (0, 1, -1), (0, -1, 1)]


def dot_f32(x, y, dims):
    return lax.dot_general(x, y, (dims, ((), ())), precision=HIGH, preferred_element_type=F32)


def dot_bf16(x, y, dims):
    return lax.dot_general(x, y, (dims, ((), ())), preferred_element_type=F32)


def split2(x):
    high = x.astype(BF16)
    return high, (x - high.astype(F32)).astype(BF16)


def split3(x):
    first = x.astype(BF16)
    rest = x - first.astype(F32)
    second = rest.astype(BF16)
    return first, second, (rest - second.astype(F32)).astype(BF16)


def spread(value, at):
    return jnp.broadcast_to(value[at : at + 1, :], value.shape)


def eliminate(old, low, steps):
    n = old.shape[1]
    tall, halves, per = old.shape[0] // 8, n // 128, steps // 8
    rows = lax.broadcasted_iota(jnp.int32, (8, 128), 0)
    lanes = lax.broadcasted_iota(jnp.int32, (8, 128), 1)
    wide = lax.broadcasted_iota(jnp.int32, (8, n), 1)
    parts = [[old[8 * q : 8 * q + 8, 128 * w : 128 * w + 128] for w in range(halves)] for q in range(tall)]
    before, after = [], []

    def lane(q, at):
        return jnp.broadcast_to(parts[q][at // 128][:, at % 128 : at % 128 + 1], (8, 128))

    for group in range(tall // per):
        base = low + steps * group
        mine = range(group * per, (group + 1) * per)
        half, first = base // 128, base % 128
        inside = (lanes >= first) & (lanes < first + steps)
        for q in mine:
            whole = jnp.concatenate(parts[q], axis=1)
            before.append(jnp.where(wide < base, -whole, jnp.where(wide < low + old.shape[0], 0.0, whole)))
        own = {(q, c): lane(q, base + c) for q in mine for c in range(steps)}
        for q in mine:
            unit = jnp.where(lanes - first == rows + 8 * (q - group * per), 1.0, 0.0)
            parts[q][half] = jnp.where(inside, unit, parts[q][half])
        pivot = spread(own[mine[0], 0], 0)
        for j in range(steps):
            at, r = group * per + j // 8, j % 8
            here = rows == r
            across = {c: spread(own[at, c], r) for c in range(j + 1, steps)}
            inverse = 1.0 / pivot
            if j + 1 < steps:
                then, rn = group * per + (j + 1) // 8, (j + 1) % 8
                pivot = spread(own[then, j + 1], rn) - (spread(own[then, j], rn) * across[j + 1]) * inverse
            pivot_row = [spread(parts[at][w], r) for w in range(halves)]
            for q in mine:
                factor = own[q, j] * inverse
                if q == at:
                    factor = jnp.where(here, -inverse, factor)
                for w in range(halves):
                    kept = jnp.where(here, 0.0, parts[q][w]) if q == at else parts[q][w]
                    parts[q][w] = kept - factor * pivot_row[w]
                for c in range(j + 1, steps):
                    kept = jnp.where(here, 0.0, own[q, c]) if q == at else own[q, c]
                    own[q, c] = kept - factor * across[c]
        for q in mine:
            whole = jnp.concatenate(parts[q], axis=1)
            after.append(jnp.where((wide >= base + steps) & (wide < low + old.shape[0]), 0.0, whole))
        done_rows = [[spread(parts[group * per + c // 8][w], c % 8) for w in range(halves)] for c in range(steps)]
        for q in range((group + 1) * per, tall):
            factors = [lane(q, base + c) for c in range(steps)]
            parts[q][half] = jnp.where(inside, 0.0, parts[q][half])
            for w in range(halves):
                terms = [factors[c] * done_rows[c][w] for c in range(steps)]
                while len(terms) > 1:
                    terms = [x + y for x, y in zip(terms[::2], terms[1::2])]
                parts[q][w] = parts[q][w] - terms[0]
    return jnp.concatenate(before, axis=0), jnp.concatenate(after, axis=0)


def stacked(x, y):
    x1, x2, x3 = split3(x)
    y1, y2, y3 = split3(y)
    return dot_bf16(
        jnp.concatenate([x1, x1, x2, x2, x1, x3], axis=0),
        jnp.concatenate([y1, y2, y1, y2, y3, y1], axis=0),
        ((0,), (0,)),
    )


def invert(s_ref, blocks):
    n = s_ref.shape[0]
    all_lanes = lax.broadcasted_iota(jnp.int32, (n, n), 1)
    for block in blocks:
        low = block * NB
        before, after = eliminate(s_ref[low : low + NB, :], low, 16)
        update = stacked(before, after)
        inside = (all_lanes >= low) & (all_lanes < low + NB)
        s_ref[...] = jnp.where(inside, 0.0, s_ref[...]) - update
        s_ref[low : low + NB, :] = after - update[low : low + NB, :]


def kernel(
    n_ia, n_ja, n_ka,
    t_hbm, b_ref, c_ref,
    a_out, b_out, c_out,
    t_ref, thi, tlo, p_ref,
    c_in1, c_in2, c_all, b_in, b_all,
    gb_mine, gb_in, gc_mine, gc_in, gc_rows, ga_rows,
    g_send, g_all,
    a_parts, a_in, a_own, a_in2, a_slice, ga_mine, ga_in,
    bm_parts, bm_in, b_own, b_in2, b_slice, gb2_mine, gb2_in,
    cm_mine, cm_parts, cm_in, cm_sum, cm_in2, a_mine, b_mine,
    t_sem, send_sem, recv_sem,
):
    i_dev, j_dev, k_dev = t_hbm.shape
    rank = c_ref.shape[-1]
    ia, ja, ka = lax.axis_index("ia"), lax.axis_index("ja"), lax.axis_index("ka")
    n_g, n_h = n_ja * n_ka, n_ia * n_ka
    g_at = ja * n_ka + ka
    h_at = ia * n_ka + ka
    g_tall = rank // n_g
    n_blocks = rank // NB

    def device(z, j, k):
        return {"ia": z, "ja": j, "ka": k}

    def far_first(step, n):
        return n // 2 + step // 2 * (2 * lax.rem(step, 2) - 1)

    def plane(step):
        at = lax.rem(g_at + far_first(step, n_g), n_g)
        return at, device(ia, at // n_ka, lax.rem(at, n_ka))

    def column(step):
        at = lax.rem(ia + far_first(step, n_ia), n_ia)
        return at, device(at, ja, ka)

    def column_pair(step):
        at = lax.rem(h_at + far_first(step, n_h), n_h)
        return at, device(at // n_ka, ja, lax.rem(at, n_ka))

    def row(step):
        at = lax.rem(ja + far_first(step, n_ja), n_ja)
        return at, device(ia, at, ka)

    def start(phase, source, target, who):
        pltpu.make_async_remote_copy(
            src_ref=source, dst_ref=target, send_sem=send_sem.at[phase],
            recv_sem=recv_sem.at[phase], device_id=who, device_id_type=MESH,
        ).start()

    def piece(z, j, k):
        odd = lax.rem(z, 2)
        return lax.rem(j + odd * (n_ja // 2), n_ja) * n_ka + lax.rem(k + odd, n_ka)

    piece_at = piece(ia, ja, ka)
    chip_x, chip_y, core = ja // 4, ka * 2 + lax.rem(ja // 2, 2), lax.rem(ja, 2)

    def chip(offset, other):
        x, y = lax.rem(chip_x + offset[0] + 4, 4), lax.rem(chip_y + offset[1] + 4, 4)
        z, c = lax.rem(ia + offset[2] + n_ia, n_ia), lax.rem(core + other, 2)
        return device(z, x * 4 + lax.rem(y, 2) * 2 + c, y // 2)

    def send(phase, n, peer, source, target):
        def body(step, carry):
            at, who = peer(step)
            start(phase, source(at), target(at), who)
            return carry
        lax.fori_loop(1, n, body, 0)

    def done(phase, ref, sem):
        pltpu.make_async_copy(ref, ref, sem.at[phase]).wait()

    chunks = t_sem.shape[0]
    i_chunk = i_dev // chunks

    def load(at):
        span = pl.ds(at * i_chunk, i_chunk)
        return pltpu.make_async_copy(t_hbm.at[span], t_ref.at[span], t_sem.at[at])

    for at in range(chunks):
        load(at).start()

    barrier = pltpu.get_barrier_semaphore()

    def greet_plane(step, carry):
        pl.semaphore_signal(barrier, inc=1, device_id=plane(step)[1], device_id_type=MESH)
        return carry

    def greet_column(step, carry):
        z = column(step)[0]
        for k in range(n_ka):
            pl.semaphore_signal(barrier, inc=1, device_id=device(z, ja, k), device_id_type=MESH)
        return carry

    lax.fori_loop(1, n_ia, greet_column, 0)
    lax.fori_loop(1, n_g, greet_plane, 0)
    beyond = [(offset, other) for offset in ACROSS for other in (0, 1) if (offset[:2], other) != ((0, 0), 0)]
    for (x, y, z), other in beyond:
        pl.semaphore_signal(barrier, inc=1, device_id=chip((-x, -y, -z), other), device_id_type=MESH)
    pl.semaphore_wait(barrier, n_g - 1 + (n_ia - 1) * n_ka + len(beyond))

    for step in (4, 3, 5, 2, 6, 1, 7):
        who = device(lax.rem(ia + step, n_ia), ja, ka)
        start(0 if step in (1, 2, 6, 7) else 16, c_ref.at[0], c_in1.at[(10 - step) % 8], who)
    send(1, n_h, column_pair, lambda at: b_ref.at[0], lambda at: b_in.at[h_at])
    c_in1[2] = c_ref[0]
    b_in[h_at] = b_ref[0]
    near, rest = pl.ds(0, 5), pl.ds(5, 3)
    done(0, c_in1.at[pl.ds(0, 4)], recv_sem)
    send(2, n_ja, row, lambda at: c_in1.at[near], lambda at: c_in2.at[ja, near])
    done(16, c_in1.at[pl.ds(0, 3)], recv_sem)
    send(17, n_ja, row, lambda at: c_in1.at[rest], lambda at: c_in2.at[ja, rest])
    c_in2[ja] = c_in1[...]

    for at in range(chunks):
        load(at).wait()

        def split_one(i, carry):
            high, low = split2(t_ref[i])
            thi[i] = high
            tlo[i] = low
            return carry
        lax.fori_loop(at * i_chunk, (at + 1) * i_chunk, split_one, 0)

    done(1, b_in.at[pl.ds(0, n_h - 1)], recv_sem)
    for h in range(n_h):
        b_all[4 * h : 4 * h + 4, :] = b_in[h]
    gb_mine[...] = dot_f32(b_all[...], b_all[...], ((0,), (0,)))

    def rows_of(ref, at):
        return ref.at[pl.ds(pl.multiple_of(at * g_tall, 8), g_tall)]

    send(3, n_ja, row, lambda at: rows_of(gb_mine, piece(ia, at, ka)), lambda at: gb_in.at[ja])
    for phase, slots in ((2, range(5)), (17, range(5, 8))):
        done(phase, c_in2.at[pl.ds(0, n_ja - 1), pl.ds(slots[0], len(slots))], recv_sem)
        for slot in slots:
            z = lax.rem(ia + slot + n_ia - 2, n_ia)
            for j in range(n_ja):
                c_all[z, 2 * j : 2 * j + 2, :] = c_in2[j, slot]
    c_whole = c_all[...].reshape(k_dev, rank)
    gc_mine[...] = dot_f32(c_whole, c_whole, ((0,), (0,)))

    def other(step):
        at = lax.rem(ka + step, n_ka)
        return at, device(ia, ja, at)

    send(4, n_ka, other, lambda at: rows_of(gc_mine, piece(ia, ja, at)), lambda at: gc_in.at[ka])

    chi, clo = split2(c_whole)
    per = 32
    b_whole = b_all[...]

    pieces, steps = per // 4, i_dev // per

    for at in range(steps):
        span = pl.ds(at * per, per)
        left_hi = thi[span].reshape(per * j_dev, k_dev)
        left_lo = tlo[span].reshape(per * j_dev, k_dev)
        inner = dot_bf16(left_hi, chi, ((1,), (0,))) + (
            dot_bf16(left_hi, clo, ((1,), (0,))) + dot_bf16(left_lo, chi, ((1,), (0,)))
        )
        inner = inner.reshape(per, j_dev, rank)
        p_ref[span] = inner
        a_parts[pl.ds(at * pieces, pieces)] = jnp.sum(inner * b_whole[None], axis=1).reshape(pieces, 4, rank)
    send(5, n_g, plane, lambda at: a_parts.at[at], lambda at: a_in.at[g_at])
    a_in[g_at] = a_parts[g_at]

    def gather_gram(phase, slot, rows):
        g_send[slot] = rows
        rows_of(g_all.at[slot], piece_at)[...] = rows
        for offset, other in [((0, 0, 0), 1)] + [(offset, other) for offset in ACROSS + NEAR[::-1] for other in (0, 1)]:
            start(phase, g_send.at[slot], rows_of(g_all.at[slot], piece_at), chip(offset, other))

    gb_in[ja] = rows_of(gb_mine, piece_at)[...]
    gc_in[ka] = rows_of(gc_mine, piece_at)[...]
    done(3, gb_in.at[pl.ds(0, n_ja - 1)], recv_sem)
    done(4, gc_in.at[pl.ds(0, n_ka - 1)], recv_sem)
    gc_rows[...] = jnp.sum(gc_in[...], axis=0)
    gather_gram(6, 0, jnp.sum(gb_in[...], axis=0) * gc_rows[...])

    done(5, a_in.at[pl.ds(0, n_g - 1)], recv_sem)
    own = jnp.sum(a_in[...], axis=0)
    a_own[...] = own
    a_in2[g_at] = own
    send(7, n_g, plane, lambda at: a_own, lambda at: a_in2.at[g_at])
    done(6, g_all.at[0, pl.ds(0, rank - g_tall)], recv_sem)
    invert(g_all.at[0], range(n_blocks))
    done(7, a_in2.at[pl.ds(0, n_g - 1)], recv_sem)
    for g in range(n_g):
        a_slice[4 * g : 4 * g + 4, :] = a_in2[g]
    a_slice[...] = dot_f32(a_slice[...], g_all[0], ((1,), (0,)))
    a_now = a_slice[...]
    ga_mine[...] = stacked(a_now, a_now)
    send(8, n_ia, column, lambda at: rows_of(ga_mine, piece(at, ja, ka)), lambda at: ga_in.at[ia])
    ga_in[ia] = rows_of(ga_mine, piece_at)[...]

    def second(step, total):
        for e in range(4):
            i = step * 4 + e
            total = total + p_ref[i] * a_slice[pl.ds(i, 1), :]
        return total
    sums = lax.fori_loop(0, i_dev // 4, second, jnp.zeros((j_dev, rank), F32))
    for h in range(n_h):
        bm_parts[h] = sums[4 * h : 4 * h + 4]
    send(9, n_h, column_pair, lambda at: bm_parts.at[at], lambda at: bm_in.at[h_at])
    bm_in[h_at] = bm_parts[h_at]
    done(8, ga_in.at[pl.ds(0, n_ia - 1)], recv_sem)
    ga_rows[...] = jnp.sum(ga_in[...], axis=0)
    gather_gram(10, 1, ga_rows[...] * gc_rows[...])
    done(9, bm_in.at[pl.ds(0, n_h - 1)], recv_sem)
    own = jnp.sum(bm_in[...], axis=0)
    b_own[...] = own
    b_in2[h_at] = own
    send(11, n_h, column_pair, lambda at: b_own, lambda at: b_in2.at[h_at])
    for g in range(n_g):
        a_mine[g] = a_slice[4 * g : 4 * g + 4, :]
    a_out[0] = a_mine[g_at]
    done(10, g_all.at[1, pl.ds(0, rank - g_tall)], recv_sem)
    invert(g_all.at[1], range(n_blocks))
    done(11, b_in2.at[pl.ds(0, n_h - 1)], recv_sem)
    for h in range(n_h):
        b_slice[4 * h : 4 * h + 4, :] = b_in2[h]
    b_slice[...] = dot_f32(b_slice[...], g_all[1], ((1,), (0,)))
    b_now = b_slice[...]
    gb2_mine[...] = stacked(b_now, b_now)
    send(12, n_ja, row, lambda at: rows_of(gb2_mine, piece(ia, at, ka)), lambda at: gb2_in.at[ja])
    gb2_in[ja] = rows_of(gb2_mine, piece_at)[...]

    for h in range(n_h):
        b_mine[h] = b_slice[4 * h : 4 * h + 4, :]
    b_out[0] = b_mine[h_at]
    for at in range(steps):
        span = pl.ds(at * per, per)
        weights = (a_slice[span, :][:, None, :] * b_now[None]).reshape(per * j_dev, rank)
        whi, wlo = split2(weights)
        left_hi = thi[span].reshape(per * j_dev, k_dev)
        left_lo = tlo[span].reshape(per * j_dev, k_dev)
        product = dot_bf16(left_hi, whi, ((0,), (0,))) + (
            dot_bf16(left_hi, wlo, ((0,), (0,))) + dot_bf16(left_lo, whi, ((0,), (0,)))
        )
        cm_mine[...] = product if at == 0 else cm_mine[...] + product
    done(12, gb2_in.at[pl.ds(0, n_ja - 1)], recv_sem)
    gather_gram(14, 2, jnp.sum(gb2_in[...], axis=0) * ga_rows[...])
    for z in range(n_ia):
        for j in range(n_ja):
            low = 2 * (z * n_ja + j)
            cm_parts[j, z] = cm_mine[low : low + 2, :]
    send(13, n_ja, row, lambda at: cm_parts.at[at], lambda at: cm_in.at[ja])
    cm_in[ja] = cm_parts[ja]
    done(14, g_all.at[2, pl.ds(0, rank - g_tall)], recv_sem)
    invert(g_all.at[2], range(n_blocks // 2))
    done(13, cm_in.at[pl.ds(0, n_ja - 1)], recv_sem)
    cm_sum[...] = jnp.sum(cm_in[...], axis=0)
    send(15, n_ia, column, lambda at: cm_sum.at[at], lambda at: cm_in2.at[ia])
    cm_in2[ia] = cm_sum[ia]
    invert(g_all.at[2], range(n_blocks // 2, n_blocks))
    done(15, cm_in2.at[pl.ds(0, n_ia - 1)], recv_sem)
    c_out[0] = dot_f32(jnp.sum(cm_in2[...], axis=0), g_all[2], ((1,), (0,)))

    sent = (
        c_in1.at[pl.ds(0, 4)], b_in.at[pl.ds(0, n_h - 1)], c_in2.at[pl.ds(0, n_ja - 1), near], gb_in.at[pl.ds(0, n_ja - 1)],
        gc_in.at[pl.ds(0, n_ka - 1)], a_in.at[pl.ds(0, n_g - 1)], g_all.at[0, pl.ds(0, rank - g_tall)], a_in2.at[pl.ds(0, n_g - 1)],
        ga_in.at[pl.ds(0, n_ia - 1)], bm_in.at[pl.ds(0, n_h - 1)], g_all.at[1, pl.ds(0, rank - g_tall)], b_in2.at[pl.ds(0, n_h - 1)],
        gb2_in.at[pl.ds(0, n_ja - 1)], cm_in.at[pl.ds(0, n_ja - 1)], g_all.at[2, pl.ds(0, rank - g_tall)], cm_in2.at[pl.ds(0, n_ia - 1)],
        c_in1.at[pl.ds(0, 3)], c_in2.at[pl.ds(0, n_ja - 1), rest],
    )
    for phase, ref in enumerate(sent):
        done(phase, ref, send_sem)


def hand_over(a_ref, b_ref, c_ref, a_out, b_out, c_out, sem):
    copies = [
        pltpu.make_async_copy(source, target, sem.at[at])
        for at, (source, target) in enumerate(((a_ref, a_out), (b_ref, b_out), (c_ref, c_out)))
    ]
    for copy in copies:
        copy.start()
    for copy in copies:
        copy.wait()


def solution(mesh):
    n_ia, n_ja, n_ka = mesh.shape["ia"], mesh.shape["ja"], mesh.shape["ka"]
    n_g, n_h = n_ja * n_ka, n_ia * n_ka

    def on_device(tensor, factor_b, factor_c):
        i_dev, j_dev, k_dev = tensor.shape
        rank = factor_b.shape[-1]
        tall = rank // n_g

        def vmem(*shape, dtype=F32):
            return pltpu.VMEM(shape, dtype)

        square = (rank, rank)
        outs = tuple(jax.ShapeDtypeStruct((1, rows, rank), F32) for rows in (4, 4, 2))
        found = pl.pallas_call(
            functools.partial(kernel, n_ia, n_ja, n_ka),
            out_shape=outs,
            in_specs=[pl.BlockSpec(memory_space=pl.ANY)] + [pl.BlockSpec(memory_space=pltpu.VMEM)] * 2,
            out_specs=(pl.BlockSpec(memory_space=pltpu.VMEM),) * 3,
            scratch_shapes=[
                vmem(i_dev, j_dev, k_dev), vmem(i_dev, j_dev, k_dev, dtype=BF16), vmem(i_dev, j_dev, k_dev, dtype=BF16),
                vmem(i_dev, j_dev, rank),
                vmem(n_ia, 2, rank), vmem(n_ja, n_ia, 2, rank), vmem(n_ia, k_dev // n_ia, rank), vmem(n_h, 4, rank), vmem(j_dev, rank),
                vmem(*square), vmem(n_ja, tall, rank), vmem(*square), vmem(n_ka, tall, rank), vmem(tall, rank), vmem(tall, rank),
                vmem(3, tall, rank), vmem(3, *square),
                vmem(n_g, 4, rank), vmem(n_g, 4, rank), vmem(4, rank), vmem(n_g, 4, rank), vmem(i_dev, rank), vmem(*square), vmem(n_ia, tall, rank),
                vmem(n_h, 4, rank), vmem(n_h, 4, rank), vmem(4, rank), vmem(n_h, 4, rank), vmem(j_dev, rank), vmem(*square), vmem(n_ja, tall, rank),
                vmem(k_dev, rank), vmem(n_ja, n_ia, 2, rank), vmem(n_ja, n_ia, 2, rank), vmem(n_ia, 2, rank), vmem(n_ia, 2, rank),
                vmem(n_g, 4, rank), vmem(n_h, 4, rank),
                pltpu.SemaphoreType.DMA((8,)), pltpu.SemaphoreType.DMA((18,)), pltpu.SemaphoreType.DMA((18,)),
            ],
            compiler_params=pltpu.CompilerParams(
                collective_id=0, has_side_effects=True, vmem_limit_bytes=56 * 1024 * 1024
            ),
        )(tensor, factor_b, factor_c)
        return pl.pallas_call(
            hand_over,
            out_shape=outs,
            in_specs=[pl.BlockSpec(memory_space=pl.ANY)] * 3,
            out_specs=(pl.BlockSpec(memory_space=pl.ANY),) * 3,
            scratch_shapes=[pltpu.SemaphoreType.DMA((3,))],
        )(*found)

    return jax.shard_map(
        on_device,
        mesh=mesh,
        in_specs=(P("ia", "ja", "ka"), P("ja", ("ia", "ka"), None), P("ka", ("ia", "ja"), None)),
        out_specs=(
            P("ia", ("ja", "ka"), None),
            P("ja", ("ia", "ka"), None),
            P("ka", ("ia", "ja"), None),
        ),
        check_vma=False,
    )
```

```python
import functools

import jax
import jax.numpy as jnp
from jax import lax
from jax.experimental import pallas as pl
from jax.experimental.pallas import tpu as pltpu
from jax.sharding import PartitionSpec as P

HIGH = lax.Precision.HIGHEST
MESH = pl.DeviceIdType.MESH
F32 = jnp.float32
BF16 = jnp.bfloat16
NB = 32
NEAR = [(1, 0, 0), (-1, 0, 0), (0, 1, 0), (0, -1, 0), (1, 1, 0), (1, -1, 0), (-1, 1, 0), (-1, -1, 0), (2, 0, 0), (0, 2, 0)]
ACROSS = [(0, 0, 1), (1, 0, -1), (-1, 0, 1), (0, 1, -1), (0, -1, 1)]


def dot_f32(x, y, dims):
    return lax.dot_general(x, y, (dims, ((), ())), precision=HIGH, preferred_element_type=F32)


def dot_bf16(x, y, dims):
    return lax.dot_general(x, y, (dims, ((), ())), preferred_element_type=F32)


def split2(x):
    high = x.astype(BF16)
    return high, (x - high.astype(F32)).astype(BF16)


def split3(x):
    first = x.astype(BF16)
    rest = x - first.astype(F32)
    second = rest.astype(BF16)
    return first, second, (rest - second.astype(F32)).astype(BF16)


def spread(value, at):
    return jnp.broadcast_to(value[at : at + 1, :], value.shape)


def eliminate(own_half, other_half, first, processed, steps):
    tall, per, end = NB // 8, steps // 8, first + NB
    rows = lax.broadcasted_iota(jnp.int32, (8, 128), 0)
    lanes = lax.broadcasted_iota(jnp.int32, (8, 128), 1)
    parts = [[half[8 * q : 8 * q + 8, :] for half in (own_half, other_half)] for q in range(tall)]
    before, after = [], []

    def lane(q, at):
        return jnp.broadcast_to(parts[q][0][:, at : at + 1], (8, 128))

    for group in range(tall // per):
        base = first + steps * group
        mine = range(group * per, (group + 1) * per)
        inside = (lanes >= base) & (lanes < base + steps)
        for q in mine:
            near, far = parts[q]
            near = jnp.where(lanes < base, -near, jnp.where(lanes < end, 0.0, near))
            before.append(jnp.concatenate([near, jnp.where(processed, -far, far)], axis=1))
        own = {(q, c): lane(q, base + c) for q in mine for c in range(steps)}
        for q in mine:
            unit = jnp.where(lanes - base == rows + 8 * (q - group * per), 1.0, 0.0)
            parts[q][0] = jnp.where(inside, unit, parts[q][0])
        pivot = spread(own[mine[0], 0], 0)
        for j in range(steps):
            at, r = group * per + j // 8, j % 8
            here = rows == r
            across = {c: spread(own[at, c], r) for c in range(j + 1, steps)}
            inverse = 1.0 / pivot
            if j + 1 < steps:
                then, rn = group * per + (j + 1) // 8, (j + 1) % 8
                pivot = spread(own[then, j + 1], rn) - (spread(own[then, j], rn) * across[j + 1]) * inverse
            pivot_row = [spread(parts[at][w], r) for w in range(2)]
            for q in mine:
                factor = own[q, j] * inverse
                if q == at:
                    factor = jnp.where(here, -inverse, factor)
                for w in range(2):
                    kept = jnp.where(here, 0.0, parts[q][w]) if q == at else parts[q][w]
                    parts[q][w] = kept - factor * pivot_row[w]
                for c in range(j + 1, steps):
                    kept = jnp.where(here, 0.0, own[q, c]) if q == at else own[q, c]
                    own[q, c] = kept - factor * across[c]
        for q in mine:
            near = jnp.where((lanes >= base + steps) & (lanes < end), 0.0, parts[q][0])
            after.append(jnp.concatenate([near, parts[q][1]], axis=1))
        done_rows = [[spread(parts[group * per + c // 8][w], c % 8) for w in range(2)] for c in range(steps)]
        for q in range((group + 1) * per, tall):
            factors = [lane(q, base + c) for c in range(steps)]
            parts[q][0] = jnp.where(inside, 0.0, parts[q][0])
            for w in range(2):
                terms = [factors[c] * done_rows[c][w] for c in range(steps)]
                while len(terms) > 1:
                    terms = [x + y for x, y in zip(terms[::2], terms[1::2])]
                parts[q][w] = parts[q][w] - terms[0]
    return jnp.concatenate(before, axis=0), jnp.concatenate(after, axis=0)


def stacked(x, y):
    x1, x2, x3 = split3(x)
    y1, y2, y3 = split3(y)
    return dot_bf16(
        jnp.concatenate([x1, x1, x2, x2, x1, x3], axis=0),
        jnp.concatenate([y1, y2, y1, y2, y3, y1], axis=0),
        ((0,), (0,)),
    )


def invert(s_ref, between=None):
    lanes = lax.broadcasted_iota(jnp.int32, (128, 128), 1)

    def half(h, carry):
        if between is not None:
            pl.when(h == 1)(between)
        spans = [pl.ds(pl.multiple_of(at * 128, 128), 128) for at in (h, 1 - h)]
        processed = jnp.full((8, 128), h, jnp.int32) == 1
        for first in range(0, 128, NB):
            block = pl.ds(pl.multiple_of(h * 128 + first, NB), NB)
            before, after = eliminate(s_ref[block, spans[0]], s_ref[block, spans[1]], first, processed, 16)
            update = stacked(before, after)
            inside = (lanes >= first) & (lanes < first + NB)
            for down in range(2):
                for along in range(2):
                    kept = s_ref[spans[down], spans[along]]
                    kept = jnp.where(inside, 0.0, kept) if along == 0 else kept
                    s_ref[spans[down], spans[along]] = kept - update[128 * down : 128 * down + 128, 128 * along : 128 * along + 128]
            found = after - update[first : first + NB, :]
            for along in range(2):
                s_ref[block, spans[along]] = found[:, 128 * along : 128 * along + 128]
        return carry

    lax.fori_loop(0, 2, half, 0)


def kernel(
    n_ia, n_ja, n_ka,
    t_hbm, b_ref, c_ref,
    a_out, b_out, c_out,
    t_ref, thi, tlo, p_ref,
    c_in1, c_in2, c_all, b_in, b_all,
    gb_mine, gb_in, gc_mine, gc_in, gc_rows, ga_rows,
    g_send, g_all,
    a_parts, a_in, a_own, a_in2, a_slice, ga_mine, ga_in,
    bm_parts, bm_in, b_own, b_in2, b_slice, gb2_mine, gb2_in,
    cm_mine, cm_parts, cm_in, cm_sum, cm_in2, a_mine, b_mine,
    t_sem, send_sem, recv_sem,
):
    i_dev, j_dev, k_dev = t_hbm.shape
    rank = c_ref.shape[-1]
    ia, ja, ka = lax.axis_index("ia"), lax.axis_index("ja"), lax.axis_index("ka")
    n_g, n_h = n_ja * n_ka, n_ia * n_ka
    g_at = ja * n_ka + ka
    h_at = ia * n_ka + ka
    g_tall = rank // n_g

    def device(z, j, k):
        return {"ia": z, "ja": j, "ka": k}

    def far_first(step, n):
        return n // 2 + step // 2 * (2 * lax.rem(step, 2) - 1)

    def plane(step):
        at = lax.rem(g_at + far_first(step, n_g), n_g)
        return at, device(ia, at // n_ka, lax.rem(at, n_ka))

    def column(step):
        at = lax.rem(ia + far_first(step, n_ia), n_ia)
        return at, device(at, ja, ka)

    def column_pair(step):
        at = lax.rem(h_at + far_first(step, n_h), n_h)
        return at, device(at // n_ka, ja, lax.rem(at, n_ka))

    def row(step):
        at = lax.rem(ja + far_first(step, n_ja), n_ja)
        return at, device(ia, at, ka)

    def start(phase, source, target, who):
        pltpu.make_async_remote_copy(
            src_ref=source, dst_ref=target, send_sem=send_sem.at[phase],
            recv_sem=recv_sem.at[phase], device_id=who, device_id_type=MESH,
        ).start()

    def piece(z, j, k):
        odd = lax.rem(z, 2)
        return lax.rem(j + odd * (n_ja // 2), n_ja) * n_ka + lax.rem(k + odd, n_ka)

    piece_at = piece(ia, ja, ka)
    chip_x, chip_y, core = ja // 4, ka * 2 + lax.rem(ja // 2, 2), lax.rem(ja, 2)

    def chip(offset, other):
        x, y = lax.rem(chip_x + offset[0] + 4, 4), lax.rem(chip_y + offset[1] + 4, 4)
        z, c = lax.rem(ia + offset[2] + n_ia, n_ia), lax.rem(core + other, 2)
        return device(z, x * 4 + lax.rem(y, 2) * 2 + c, y // 2)

    def send(phase, n, peer, source, target):
        def body(step, carry):
            at, who = peer(step)
            start(phase, source(at), target(at), who)
            return carry
        lax.fori_loop(1, n, body, 0)

    def done(phase, ref, sem):
        pltpu.make_async_copy(ref, ref, sem.at[phase]).wait()

    chunks = t_sem.shape[0]
    i_chunk = i_dev // chunks

    def load(at):
        span = pl.ds(at * i_chunk, i_chunk)
        return pltpu.make_async_copy(t_hbm.at[span], t_ref.at[span], t_sem.at[at])

    for at in range(chunks):
        load(at).start()

    barrier = pltpu.get_barrier_semaphore()

    def greet_plane(step, carry):
        pl.semaphore_signal(barrier, inc=1, device_id=plane(step)[1], device_id_type=MESH)
        return carry

    def greet_column(step, carry):
        z = column(step)[0]
        for k in range(n_ka):
            pl.semaphore_signal(barrier, inc=1, device_id=device(z, ja, k), device_id_type=MESH)
        return carry

    lax.fori_loop(1, n_ia, greet_column, 0)
    lax.fori_loop(1, n_g, greet_plane, 0)
    beyond = [(offset, other) for offset in ACROSS for other in (0, 1) if (offset[:2], other) != ((0, 0), 0)]
    for (x, y, z), other in beyond:
        pl.semaphore_signal(barrier, inc=1, device_id=chip((-x, -y, -z), other), device_id_type=MESH)
    pl.semaphore_wait(barrier, n_g - 1 + (n_ia - 1) * n_ka + len(beyond))

    for step in (4, 3, 5, 2, 6, 1, 7):
        who = device(lax.rem(ia + step, n_ia), ja, ka)
        start(0 if step in (1, 2, 6, 7) else 16, c_ref.at[0], c_in1.at[(10 - step) % 8], who)
    send(1, n_h, column_pair, lambda at: b_ref.at[0], lambda at: b_in.at[h_at])
    c_in1[2] = c_ref[0]
    b_in[h_at] = b_ref[0]
    near, rest = pl.ds(0, 5), pl.ds(5, 3)
    done(0, c_in1.at[pl.ds(0, 4)], recv_sem)
    send(2, n_ja, row, lambda at: c_in1.at[near], lambda at: c_in2.at[ja, near])
    done(16, c_in1.at[pl.ds(0, 3)], recv_sem)
    send(17, n_ja, row, lambda at: c_in1.at[rest], lambda at: c_in2.at[ja, rest])
    c_in2[ja] = c_in1[...]

    for at in range(chunks):
        load(at).wait()

        def split_one(i, carry):
            high, low = split2(t_ref[i])
            thi[i] = high
            tlo[i] = low
            return carry
        lax.fori_loop(at * i_chunk, (at + 1) * i_chunk, split_one, 0)

    done(1, b_in.at[pl.ds(0, n_h - 1)], recv_sem)
    for h in range(n_h):
        b_all[4 * h : 4 * h + 4, :] = b_in[h]
    gb_mine[...] = dot_f32(b_all[...], b_all[...], ((0,), (0,)))

    def rows_of(ref, at):
        return ref.at[pl.ds(pl.multiple_of(at * g_tall, 8), g_tall)]

    send(3, n_ja, row, lambda at: rows_of(gb_mine, piece(ia, at, ka)), lambda at: gb_in.at[ja])
    for phase, slots in ((2, range(5)), (17, range(5, 8))):
        done(phase, c_in2.at[pl.ds(0, n_ja - 1), pl.ds(slots[0], len(slots))], recv_sem)
        for slot in slots:
            z = lax.rem(ia + slot + n_ia - 2, n_ia)
            for j in range(n_ja):
                c_all[z, 2 * j : 2 * j + 2, :] = c_in2[j, slot]
    c_whole = c_all[...].reshape(k_dev, rank)
    gc_mine[...] = dot_f32(c_whole, c_whole, ((0,), (0,)))

    def other(step):
        at = lax.rem(ka + step, n_ka)
        return at, device(ia, ja, at)

    send(4, n_ka, other, lambda at: rows_of(gc_mine, piece(ia, ja, at)), lambda at: gc_in.at[ka])

    chi, clo = split2(c_whole)
    per = 32
    b_whole = b_all[...]

    pieces, steps = per // 4, i_dev // per
    early = steps * 3 // 4

    def first(step, carry):
        at = lax.rem(g_at // pieces + 1 + step, steps)
        span = pl.ds(at * per, per)
        left_hi = thi[span].reshape(per * j_dev, k_dev)
        left_lo = tlo[span].reshape(per * j_dev, k_dev)
        inner = dot_bf16(left_hi, chi, ((1,), (0,))) + (
            dot_bf16(left_hi, clo, ((1,), (0,))) + dot_bf16(left_lo, chi, ((1,), (0,)))
        )
        inner = inner.reshape(per, j_dev, rank)
        p_ref[span] = inner
        summed = jnp.sum(inner * b_whole[None], axis=1)
        a_parts[pl.ds(at * pieces, pieces)] = summed.reshape(pieces, 4, rank)
        for e in range(pieces):
            to = at * pieces + e

            @pl.when(to != g_at)
            def _():
                start(5, a_parts.at[to], a_in.at[g_at], device(ia, to // n_ka, lax.rem(to, n_ka)))
        return carry

    def gather_gram(phase, slot, rows):
        g_send[slot] = rows
        rows_of(g_all.at[slot], piece_at)[...] = rows
        for offset, other in [((0, 0, 0), 1)] + [(offset, other) for offset in ACROSS + NEAR[::-1] for other in (0, 1)]:
            start(phase, g_send.at[slot], rows_of(g_all.at[slot], piece_at), chip(offset, other))

    lax.fori_loop(0, early, first, 0)
    gb_in[ja] = rows_of(gb_mine, piece_at)[...]
    gc_in[ka] = rows_of(gc_mine, piece_at)[...]
    done(3, gb_in.at[pl.ds(0, n_ja - 1)], recv_sem)
    done(4, gc_in.at[pl.ds(0, n_ka - 1)], recv_sem)
    gc_rows[...] = jnp.sum(gc_in[...], axis=0)
    gather_gram(6, 0, jnp.sum(gb_in[...], axis=0) * gc_rows[...])
    lax.fori_loop(early, steps, first, 0)
    a_in[g_at] = a_parts[g_at]

    done(5, a_in.at[pl.ds(0, n_g - 1)], recv_sem)
    own = jnp.sum(a_in[...], axis=0)
    a_own[...] = own
    a_in2[g_at] = own
    send(7, n_g, plane, lambda at: a_own, lambda at: a_in2.at[g_at])
    done(6, g_all.at[0, pl.ds(0, rank - g_tall)], recv_sem)
    invert(g_all.at[0])
    done(7, a_in2.at[pl.ds(0, n_g - 1)], recv_sem)
    for g in range(n_g):
        a_slice[4 * g : 4 * g + 4, :] = a_in2[g]
    a_slice[...] = dot_f32(a_slice[...], g_all[0], ((1,), (0,)))
    a_now = a_slice[...]
    ga_mine[...] = stacked(a_now, a_now)
    send(8, n_ia, column, lambda at: rows_of(ga_mine, piece(at, ja, ka)), lambda at: ga_in.at[ia])
    ga_in[ia] = rows_of(ga_mine, piece_at)[...]

    def second(step, total):
        for e in range(4):
            i = step * 4 + e
            total = total + p_ref[i] * a_slice[pl.ds(i, 1), :]
        return total
    sums = lax.fori_loop(0, i_dev // 4, second, jnp.zeros((j_dev, rank), F32))
    for h in range(n_h):
        bm_parts[h] = sums[4 * h : 4 * h + 4]
    send(9, n_h, column_pair, lambda at: bm_parts.at[at], lambda at: bm_in.at[h_at])
    bm_in[h_at] = bm_parts[h_at]
    done(8, ga_in.at[pl.ds(0, n_ia - 1)], recv_sem)
    ga_rows[...] = jnp.sum(ga_in[...], axis=0)
    gather_gram(10, 1, ga_rows[...] * gc_rows[...])
    done(9, bm_in.at[pl.ds(0, n_h - 1)], recv_sem)
    own = jnp.sum(bm_in[...], axis=0)
    b_own[...] = own
    b_in2[h_at] = own
    send(11, n_h, column_pair, lambda at: b_own, lambda at: b_in2.at[h_at])
    for g in range(n_g):
        a_mine[g] = a_slice[4 * g : 4 * g + 4, :]
    a_out[0] = a_mine[g_at]
    done(10, g_all.at[1, pl.ds(0, rank - g_tall)], recv_sem)
    invert(g_all.at[1])
    done(11, b_in2.at[pl.ds(0, n_h - 1)], recv_sem)
    for h in range(n_h):
        b_slice[4 * h : 4 * h + 4, :] = b_in2[h]
    b_slice[...] = dot_f32(b_slice[...], g_all[1], ((1,), (0,)))
    b_now = b_slice[...]
    gb2_mine[...] = stacked(b_now, b_now)
    send(12, n_ja, row, lambda at: rows_of(gb2_mine, piece(ia, at, ka)), lambda at: gb2_in.at[ja])
    gb2_in[ja] = rows_of(gb2_mine, piece_at)[...]

    for h in range(n_h):
        b_mine[h] = b_slice[4 * h : 4 * h + 4, :]
    b_out[0] = b_mine[h_at]
    cm_mine[...] = jnp.zeros_like(cm_mine)

    def third(step, carry):
        span = pl.ds(step * per, per)
        weights = (a_slice[pl.ds(pl.multiple_of(step * per, per), per), :][:, None, :] * b_now[None]).reshape(per * j_dev, rank)
        whi, wlo = split2(weights)
        left_hi = thi[span].reshape(per * j_dev, k_dev)
        left_lo = tlo[span].reshape(per * j_dev, k_dev)
        cm_mine[...] += dot_bf16(left_hi, whi, ((0,), (0,))) + (
            dot_bf16(left_hi, wlo, ((0,), (0,))) + dot_bf16(left_lo, whi, ((0,), (0,)))
        )
        return carry
    lax.fori_loop(0, early, third, 0)
    done(12, gb2_in.at[pl.ds(0, n_ja - 1)], recv_sem)
    gather_gram(14, 2, jnp.sum(gb2_in[...], axis=0) * ga_rows[...])
    lax.fori_loop(early, steps, third, 0)
    for z in range(n_ia):
        for j in range(n_ja):
            low = 2 * (z * n_ja + j)
            cm_parts[j, z] = cm_mine[low : low + 2, :]
    send(13, n_ja, row, lambda at: cm_parts.at[at], lambda at: cm_in.at[ja])
    cm_in[ja] = cm_parts[ja]
    done(14, g_all.at[2, pl.ds(0, rank - g_tall)], recv_sem)
    def pass_third_products_on():
        done(13, cm_in.at[pl.ds(0, n_ja - 1)], recv_sem)
        cm_sum[...] = jnp.sum(cm_in[...], axis=0)
        send(15, n_ia, column, lambda at: cm_sum.at[at], lambda at: cm_in2.at[ia])
        cm_in2[ia] = cm_sum[ia]

    invert(g_all.at[2], pass_third_products_on)
    done(15, cm_in2.at[pl.ds(0, n_ia - 1)], recv_sem)
    c_out[0] = dot_f32(jnp.sum(cm_in2[...], axis=0), g_all[2], ((1,), (0,)))

    sent = (
        c_in1.at[pl.ds(0, 4)], b_in.at[pl.ds(0, n_h - 1)], c_in2.at[pl.ds(0, n_ja - 1), near], gb_in.at[pl.ds(0, n_ja - 1)],
        gc_in.at[pl.ds(0, n_ka - 1)], a_in.at[pl.ds(0, n_g - 1)], g_all.at[0, pl.ds(0, rank - g_tall)], a_in2.at[pl.ds(0, n_g - 1)],
        ga_in.at[pl.ds(0, n_ia - 1)], bm_in.at[pl.ds(0, n_h - 1)], g_all.at[1, pl.ds(0, rank - g_tall)], b_in2.at[pl.ds(0, n_h - 1)],
        gb2_in.at[pl.ds(0, n_ja - 1)], cm_in.at[pl.ds(0, n_ja - 1)], g_all.at[2, pl.ds(0, rank - g_tall)], cm_in2.at[pl.ds(0, n_ia - 1)],
        c_in1.at[pl.ds(0, 3)], c_in2.at[pl.ds(0, n_ja - 1), rest],
    )
    for phase, ref in enumerate(sent):
        done(phase, ref, send_sem)


def hand_over(a_ref, b_ref, c_ref, a_out, b_out, c_out, sem):
    copies = [
        pltpu.make_async_copy(source, target, sem.at[at])
        for at, (source, target) in enumerate(((a_ref, a_out), (b_ref, b_out), (c_ref, c_out)))
    ]
    for copy in copies:
        copy.start()
    for copy in copies:
        copy.wait()


def solution(mesh):
    n_ia, n_ja, n_ka = mesh.shape["ia"], mesh.shape["ja"], mesh.shape["ka"]
    n_g, n_h = n_ja * n_ka, n_ia * n_ka

    def on_device(tensor, factor_b, factor_c):
        i_dev, j_dev, k_dev = tensor.shape
        rank = factor_b.shape[-1]
        tall = rank // n_g

        def vmem(*shape, dtype=F32):
            return pltpu.VMEM(shape, dtype)

        square = (rank, rank)
        outs = tuple(jax.ShapeDtypeStruct((1, rows, rank), F32) for rows in (4, 4, 2))
        found = pl.pallas_call(
            functools.partial(kernel, n_ia, n_ja, n_ka),
            out_shape=outs,
            in_specs=[pl.BlockSpec(memory_space=pl.ANY)] + [pl.BlockSpec(memory_space=pltpu.VMEM)] * 2,
            out_specs=(pl.BlockSpec(memory_space=pltpu.VMEM),) * 3,
            scratch_shapes=[
                vmem(i_dev, j_dev, k_dev), vmem(i_dev, j_dev, k_dev, dtype=BF16), vmem(i_dev, j_dev, k_dev, dtype=BF16),
                vmem(i_dev, j_dev, rank),
                vmem(n_ia, 2, rank), vmem(n_ja, n_ia, 2, rank), vmem(n_ia, k_dev // n_ia, rank), vmem(n_h, 4, rank), vmem(j_dev, rank),
                vmem(*square), vmem(n_ja, tall, rank), vmem(*square), vmem(n_ka, tall, rank), vmem(tall, rank), vmem(tall, rank),
                vmem(3, tall, rank), vmem(3, *square),
                vmem(n_g, 4, rank), vmem(n_g, 4, rank), vmem(4, rank), vmem(n_g, 4, rank), vmem(i_dev, rank), vmem(*square), vmem(n_ia, tall, rank),
                vmem(n_h, 4, rank), vmem(n_h, 4, rank), vmem(4, rank), vmem(n_h, 4, rank), vmem(j_dev, rank), vmem(*square), vmem(n_ja, tall, rank),
                vmem(k_dev, rank), vmem(n_ja, n_ia, 2, rank), vmem(n_ja, n_ia, 2, rank), vmem(n_ia, 2, rank), vmem(n_ia, 2, rank),
                vmem(n_g, 4, rank), vmem(n_h, 4, rank),
                pltpu.SemaphoreType.DMA((8,)), pltpu.SemaphoreType.DMA((18,)), pltpu.SemaphoreType.DMA((18,)),
            ],
            compiler_params=pltpu.CompilerParams(
                collective_id=0, has_side_effects=True, vmem_limit_bytes=56 * 1024 * 1024
            ),
        )(tensor, factor_b, factor_c)
        return pl.pallas_call(
            hand_over,
            out_shape=outs,
            in_specs=[pl.BlockSpec(memory_space=pl.ANY)] * 3,
            out_specs=(pl.BlockSpec(memory_space=pl.ANY),) * 3,
            scratch_shapes=[pltpu.SemaphoreType.DMA((3,))],
        )(*found)

    return jax.shard_map(
        on_device,
        mesh=mesh,
        in_specs=(P("ia", "ja", "ka"), P("ja", ("ia", "ka"), None), P("ka", ("ia", "ja"), None)),
        out_specs=(
            P("ia", ("ja", "ka"), None),
            P("ja", ("ia", "ka"), None),
            P("ka", ("ia", "ja"), None),
        ),
        check_vma=False,
    )
```

```python
import functools

import jax
import jax.numpy as jnp
from jax import lax
from jax.experimental import pallas as pl
from jax.experimental.pallas import tpu as pltpu
from jax.sharding import PartitionSpec as P

HIGH = lax.Precision.HIGHEST
MESH = pl.DeviceIdType.MESH
F32 = jnp.float32
BF16 = jnp.bfloat16
NB = 32
NEAR = [(1, 0, 0), (-1, 0, 0), (0, 1, 0), (0, -1, 0), (1, 1, 0), (1, -1, 0), (-1, 1, 0), (-1, -1, 0), (2, 0, 0), (0, 2, 0)]
ACROSS = [(0, 0, 1), (1, 0, -1), (-1, 0, 1), (0, 1, -1), (0, -1, 1)]


def dot_f32(x, y, dims):
    return lax.dot_general(x, y, (dims, ((), ())), precision=HIGH, preferred_element_type=F32)


def dot_bf16(x, y, dims):
    return lax.dot_general(x, y, (dims, ((), ())), preferred_element_type=F32)


def split2(x):
    high = x.astype(BF16)
    return high, (x - high.astype(F32)).astype(BF16)


def split3(x):
    first = x.astype(BF16)
    rest = x - first.astype(F32)
    second = rest.astype(BF16)
    return first, second, (rest - second.astype(F32)).astype(BF16)


def spread(value, at):
    return jnp.broadcast_to(value[at : at + 1, :], value.shape)


def eliminate(old, low, steps):
    n = old.shape[1]
    tall, halves, per = old.shape[0] // 8, n // 128, steps // 8
    rows = lax.broadcasted_iota(jnp.int32, (8, 128), 0)
    lanes = lax.broadcasted_iota(jnp.int32, (8, 128), 1)
    wide = lax.broadcasted_iota(jnp.int32, (8, n), 1)
    parts = [[old[8 * q : 8 * q + 8, 128 * w : 128 * w + 128] for w in range(halves)] for q in range(tall)]
    before, after = [], []

    def lane(q, at):
        return jnp.broadcast_to(parts[q][at // 128][:, at % 128 : at % 128 + 1], (8, 128))

    for group in range(tall // per):
        base = low + steps * group
        mine = range(group * per, (group + 1) * per)
        half, first = base // 128, base % 128
        inside = (lanes >= first) & (lanes < first + steps)
        for q in mine:
            whole = jnp.concatenate(parts[q], axis=1)
            before.append(jnp.where(wide < base, -whole, jnp.where(wide < low + old.shape[0], 0.0, whole)))
        own = {(q, c): lane(q, base + c) for q in mine for c in range(steps)}
        for q in mine:
            unit = jnp.where(lanes - first == rows + 8 * (q - group * per), 1.0, 0.0)
            parts[q][half] = jnp.where(inside, unit, parts[q][half])
        pivot = spread(own[mine[0], 0], 0)
        for j in range(steps):
            at, r = group * per + j // 8, j % 8
            here = rows == r
            across = {c: spread(own[at, c], r) for c in range(j + 1, steps)}
            inverse = 1.0 / pivot
            if j + 1 < steps:
                then, rn = group * per + (j + 1) // 8, (j + 1) % 8
                pivot = spread(own[then, j + 1], rn) - (spread(own[then, j], rn) * across[j + 1]) * inverse
            pivot_row = [spread(parts[at][w], r) for w in range(halves)]
            for q in mine:
                factor = own[q, j] * inverse
                if q == at:
                    factor = jnp.where(here, -inverse, factor)
                for w in range(halves):
                    kept = jnp.where(here, 0.0, parts[q][w]) if q == at else parts[q][w]
                    parts[q][w] = kept - factor * pivot_row[w]
                for c in range(j + 1, steps):
                    kept = jnp.where(here, 0.0, own[q, c]) if q == at else own[q, c]
                    own[q, c] = kept - factor * across[c]
        for q in mine:
            whole = jnp.concatenate(parts[q], axis=1)
            after.append(jnp.where((wide >= base + steps) & (wide < low + old.shape[0]), 0.0, whole))
        done_rows = [[spread(parts[group * per + c // 8][w], c % 8) for w in range(halves)] for c in range(steps)]
        for q in range((group + 1) * per, tall):
            factors = [lane(q, base + c) for c in range(steps)]
            parts[q][half] = jnp.where(inside, 0.0, parts[q][half])
            for w in range(halves):
                terms = [factors[c] * done_rows[c][w] for c in range(steps)]
                while len(terms) > 1:
                    terms = [x + y for x, y in zip(terms[::2], terms[1::2])]
                parts[q][w] = parts[q][w] - terms[0]
    return jnp.concatenate(before, axis=0), jnp.concatenate(after, axis=0)


def stacked(x, y):
    x1, x2, x3 = split3(x)
    y1, y2, y3 = split3(y)
    return dot_bf16(
        jnp.concatenate([x1, x1, x2, x2, x1, x3], axis=0),
        jnp.concatenate([y1, y2, y1, y2, y3, y1], axis=0),
        ((0,), (0,)),
    )


def invert(s_ref, blocks):
    n = s_ref.shape[0]
    all_lanes = lax.broadcasted_iota(jnp.int32, (n, n), 1)
    for block in blocks:
        low = block * NB
        before, after = eliminate(s_ref[low : low + NB, :], low, 16)
        update = stacked(before, after)
        inside = (all_lanes >= low) & (all_lanes < low + NB)
        s_ref[...] = jnp.where(inside, 0.0, s_ref[...]) - update
        s_ref[low : low + NB, :] = after - update[low : low + NB, :]


def kernel(
    n_ia, n_ja, n_ka,
    t_hbm, b_ref, c_ref,
    a_out, b_out, c_out,
    t_ref, thi, tlo, p_ref,
    c_in1, c_in2, c_all, b_in, b_all,
    gb_mine, gb_in, gc_mine, gc_in, gc_rows, ga_rows,
    g_send, g_all,
    a_parts, a_in, a_own, a_in2, a_slice, ga_mine, ga_in,
    bm_parts, bm_in, b_own, b_in2, b_slice, gb2_mine, gb2_in,
    cm_mine, cm_parts, cm_in, cm_sum, cm_in2, a_mine, b_mine,
    t_sem, send_sem, recv_sem,
):
    i_dev, j_dev, k_dev = t_hbm.shape
    rank = c_ref.shape[-1]
    ia, ja, ka = lax.axis_index("ia"), lax.axis_index("ja"), lax.axis_index("ka")
    n_g, n_h = n_ja * n_ka, n_ia * n_ka
    g_at = ja * n_ka + ka
    h_at = ia * n_ka + ka
    g_tall = rank // n_g
    n_blocks = rank // NB

    def device(z, j, k):
        return {"ia": z, "ja": j, "ka": k}

    def far_first(step, n):
        return n // 2 + step // 2 * (2 * lax.rem(step, 2) - 1)

    def plane(step):
        at = lax.rem(g_at + far_first(step, n_g), n_g)
        return at, device(ia, at // n_ka, lax.rem(at, n_ka))

    def column(step):
        at = lax.rem(ia + far_first(step, n_ia), n_ia)
        return at, device(at, ja, ka)

    def column_pair(step):
        at = lax.rem(h_at + far_first(step, n_h), n_h)
        return at, device(at // n_ka, ja, lax.rem(at, n_ka))

    def row(step):
        at = lax.rem(ja + far_first(step, n_ja), n_ja)
        return at, device(ia, at, ka)

    def start(phase, source, target, who):
        pltpu.make_async_remote_copy(
            src_ref=source, dst_ref=target, send_sem=send_sem.at[phase],
            recv_sem=recv_sem.at[phase], device_id=who, device_id_type=MESH,
        ).start()

    def piece(z, j, k):
        odd = lax.rem(z, 2)
        return lax.rem(j + odd * (n_ja // 2), n_ja) * n_ka + lax.rem(k + odd, n_ka)

    piece_at = piece(ia, ja, ka)
    chip_x, chip_y, core = ja // 4, ka * 2 + lax.rem(ja // 2, 2), lax.rem(ja, 2)

    def chip(offset, other):
        x, y = lax.rem(chip_x + offset[0] + 4, 4), lax.rem(chip_y + offset[1] + 4, 4)
        z, c = lax.rem(ia + offset[2] + n_ia, n_ia), lax.rem(core + other, 2)
        return device(z, x * 4 + lax.rem(y, 2) * 2 + c, y // 2)

    def send(phase, n, peer, source, target):
        def body(step, carry):
            at, who = peer(step)
            start(phase, source(at), target(at), who)
            return carry
        lax.fori_loop(1, n, body, 0)

    def done(phase, ref, sem):
        pltpu.make_async_copy(ref, ref, sem.at[phase]).wait()

    chunks = t_sem.shape[0]
    i_chunk = i_dev // chunks

    def load(at):
        span = pl.ds(at * i_chunk, i_chunk)
        return pltpu.make_async_copy(t_hbm.at[span], t_ref.at[span], t_sem.at[at])

    for at in range(chunks):
        load(at).start()

    barrier = pltpu.get_barrier_semaphore()

    def greet_plane(step, carry):
        pl.semaphore_signal(barrier, inc=1, device_id=plane(step)[1], device_id_type=MESH)
        return carry

    def greet_column(step, carry):
        z = column(step)[0]
        for k in range(n_ka):
            pl.semaphore_signal(barrier, inc=1, device_id=device(z, ja, k), device_id_type=MESH)
        return carry

    lax.fori_loop(1, n_ia, greet_column, 0)
    lax.fori_loop(1, n_g, greet_plane, 0)
    beyond = [(offset, other) for offset in ACROSS for other in (0, 1) if (offset[:2], other) != ((0, 0), 0)]
    for (x, y, z), other in beyond:
        pl.semaphore_signal(barrier, inc=1, device_id=chip((-x, -y, -z), other), device_id_type=MESH)
    pl.semaphore_wait(barrier, n_g - 1 + (n_ia - 1) * n_ka + len(beyond))

    for step in (4, 3, 5, 2, 6, 1, 7):
        who = device(lax.rem(ia + step, n_ia), ja, ka)
        start(0 if step in (1, 2, 6, 7) else 16, c_ref.at[0], c_in1.at[(10 - step) % 8], who)
    send(1, n_h, column_pair, lambda at: b_ref.at[0], lambda at: b_in.at[h_at])
    c_in1[2] = c_ref[0]
    b_in[h_at] = b_ref[0]
    near, rest = pl.ds(0, 5), pl.ds(5, 3)
    done(0, c_in1.at[pl.ds(0, 4)], recv_sem)
    send(2, n_ja, row, lambda at: c_in1.at[near], lambda at: c_in2.at[ja, near])
    done(16, c_in1.at[pl.ds(0, 3)], recv_sem)
    send(17, n_ja, row, lambda at: c_in1.at[rest], lambda at: c_in2.at[ja, rest])
    c_in2[ja] = c_in1[...]

    for at in range(chunks):
        load(at).wait()

        def split_one(i, carry):
            high, low = split2(t_ref[i])
            thi[i] = high
            tlo[i] = low
            return carry
        lax.fori_loop(at * i_chunk, (at + 1) * i_chunk, split_one, 0)

    done(1, b_in.at[pl.ds(0, n_h - 1)], recv_sem)
    for h in range(n_h):
        b_all[4 * h : 4 * h + 4, :] = b_in[h]
    gb_mine[...] = dot_f32(b_all[...], b_all[...], ((0,), (0,)))

    def rows_of(ref, at):
        return ref.at[pl.ds(pl.multiple_of(at * g_tall, 8), g_tall)]

    send(3, n_ja, row, lambda at: rows_of(gb_mine, piece(ia, at, ka)), lambda at: gb_in.at[ja])
    for phase, slots in ((2, range(5)), (17, range(5, 8))):
        done(phase, c_in2.at[pl.ds(0, n_ja - 1), pl.ds(slots[0], len(slots))], recv_sem)
        for slot in slots:
            z = lax.rem(ia + slot + n_ia - 2, n_ia)
            for j in range(n_ja):
                c_all[z, 2 * j : 2 * j + 2, :] = c_in2[j, slot]
    c_whole = c_all[...].reshape(k_dev, rank)
    gc_mine[...] = dot_f32(c_whole, c_whole, ((0,), (0,)))

    def other(step):
        at = lax.rem(ka + step, n_ka)
        return at, device(ia, ja, at)

    send(4, n_ka, other, lambda at: rows_of(gc_mine, piece(ia, ja, at)), lambda at: gc_in.at[ka])

    chi, clo = split2(c_whole)
    per = 32
    b_whole = b_all[...]

    pieces, steps = per // 4, i_dev // per
    early = steps * 3 // 4

    def first(step, carry):
        at = lax.rem(g_at // pieces + 1 + step, steps)
        span = pl.ds(at * per, per)
        left_hi = thi[span].reshape(per * j_dev, k_dev)
        left_lo = tlo[span].reshape(per * j_dev, k_dev)
        inner = dot_bf16(left_hi, chi, ((1,), (0,))) + (
            dot_bf16(left_hi, clo, ((1,), (0,))) + dot_bf16(left_lo, chi, ((1,), (0,)))
        )
        inner = inner.reshape(per, j_dev, rank)
        p_ref[span] = inner
        summed = jnp.sum(inner * b_whole[None], axis=1)
        a_parts[pl.ds(at * pieces, pieces)] = summed.reshape(pieces, 4, rank)
        for e in range(pieces):
            to = at * pieces + e

            @pl.when(to != g_at)
            def _():
                start(5, a_parts.at[to], a_in.at[g_at], device(ia, to // n_ka, lax.rem(to, n_ka)))
        return carry

    def gather_gram(phase, slot, rows):
        g_send[slot] = rows
        rows_of(g_all.at[slot], piece_at)[...] = rows
        for offset, other in [(offset, other) for offset in ACROSS[::-1] + NEAR[::-1] for other in (0, 1)] + [((0, 0, 0), 1)]:
            start(phase, g_send.at[slot], rows_of(g_all.at[slot], piece_at), chip(offset, other))

    lax.fori_loop(0, early, first, 0)
    gb_in[ja] = rows_of(gb_mine, piece_at)[...]
    gc_in[ka] = rows_of(gc_mine, piece_at)[...]
    done(3, gb_in.at[pl.ds(0, n_ja - 1)], recv_sem)
    done(4, gc_in.at[pl.ds(0, n_ka - 1)], recv_sem)
    gc_rows[...] = jnp.sum(gc_in[...], axis=0)
    gather_gram(6, 0, jnp.sum(gb_in[...], axis=0) * gc_rows[...])
    lax.fori_loop(early, steps, first, 0)
    a_in[g_at] = a_parts[g_at]

    done(6, g_all.at[0, pl.ds(0, rank - g_tall)], recv_sem)
    invert(g_all.at[0], range(3))
    done(5, a_in.at[pl.ds(0, n_g - 1)], recv_sem)
    own = jnp.sum(a_in[...], axis=0)
    a_own[...] = own
    a_in2[g_at] = own
    send(7, n_g, plane, lambda at: a_own, lambda at: a_in2.at[g_at])
    invert(g_all.at[0], range(3, n_blocks))
    done(7, a_in2.at[pl.ds(0, n_g - 1)], recv_sem)
    for g in range(n_g):
        a_slice[4 * g : 4 * g + 4, :] = a_in2[g]
    a_slice[...] = dot_f32(a_slice[...], g_all[0], ((1,), (0,)))
    a_now = a_slice[...]
    ga_mine[...] = stacked(a_now, a_now)
    send(8, n_ia, column, lambda at: rows_of(ga_mine, piece(at, ja, ka)), lambda at: ga_in.at[ia])
    ga_in[ia] = rows_of(ga_mine, piece_at)[...]

    def second(step, total):
        for e in range(4):
            i = step * 4 + e
            total = total + p_ref[i] * a_slice[pl.ds(i, 1), :]
        return total
    sums = lax.fori_loop(0, i_dev // 4, second, jnp.zeros((j_dev, rank), F32))
    for h in range(n_h):
        bm_parts[h] = sums[4 * h : 4 * h + 4]
    send(9, n_h, column_pair, lambda at: bm_parts.at[at], lambda at: bm_in.at[h_at])
    bm_in[h_at] = bm_parts[h_at]
    done(8, ga_in.at[pl.ds(0, n_ia - 1)], recv_sem)
    ga_rows[...] = jnp.sum(ga_in[...], axis=0)
    gather_gram(10, 1, ga_rows[...] * gc_rows[...])
    done(9, bm_in.at[pl.ds(0, n_h - 1)], recv_sem)
    own = jnp.sum(bm_in[...], axis=0)
    b_own[...] = own
    b_in2[h_at] = own
    send(11, n_h, column_pair, lambda at: b_own, lambda at: b_in2.at[h_at])
    for g in range(n_g):
        a_mine[g] = a_slice[4 * g : 4 * g + 4, :]
    a_out[0] = a_mine[g_at]
    done(10, g_all.at[1, pl.ds(0, rank - g_tall)], recv_sem)
    invert(g_all.at[1], range(n_blocks))
    done(11, b_in2.at[pl.ds(0, n_h - 1)], recv_sem)
    for h in range(n_h):
        b_slice[4 * h : 4 * h + 4, :] = b_in2[h]
    b_slice[...] = dot_f32(b_slice[...], g_all[1], ((1,), (0,)))
    b_now = b_slice[...]
    gb2_mine[...] = stacked(b_now, b_now)
    send(12, n_ja, row, lambda at: rows_of(gb2_mine, piece(ia, at, ka)), lambda at: gb2_in.at[ja])
    gb2_in[ja] = rows_of(gb2_mine, piece_at)[...]

    for h in range(n_h):
        b_mine[h] = b_slice[4 * h : 4 * h + 4, :]
    b_out[0] = b_mine[h_at]
    cm_mine[...] = jnp.zeros_like(cm_mine)

    def third(step, carry):
        span = pl.ds(step * per, per)
        weights = (a_slice[pl.ds(pl.multiple_of(step * per, per), per), :][:, None, :] * b_now[None]).reshape(per * j_dev, rank)
        whi, wlo = split2(weights)
        left_hi = thi[span].reshape(per * j_dev, k_dev)
        left_lo = tlo[span].reshape(per * j_dev, k_dev)
        cm_mine[...] += dot_bf16(left_hi, whi, ((0,), (0,))) + (
            dot_bf16(left_hi, wlo, ((0,), (0,))) + dot_bf16(left_lo, whi, ((0,), (0,)))
        )
        return carry
    lax.fori_loop(0, early, third, 0)
    done(12, gb2_in.at[pl.ds(0, n_ja - 1)], recv_sem)
    gather_gram(14, 2, jnp.sum(gb2_in[...], axis=0) * ga_rows[...])
    lax.fori_loop(early, steps, third, 0)
    for z in range(n_ia):
        for j in range(n_ja):
            low = 2 * (z * n_ja + j)
            cm_parts[j, z] = cm_mine[low : low + 2, :]
    send(13, n_ja, row, lambda at: cm_parts.at[at], lambda at: cm_in.at[ja])
    cm_in[ja] = cm_parts[ja]
    done(14, g_all.at[2, pl.ds(0, rank - g_tall)], recv_sem)
    invert(g_all.at[2], range(n_blocks // 2))
    done(13, cm_in.at[pl.ds(0, n_ja - 1)], recv_sem)
    cm_sum[...] = jnp.sum(cm_in[...], axis=0)
    send(15, n_ia, column, lambda at: cm_sum.at[at], lambda at: cm_in2.at[ia])
    cm_in2[ia] = cm_sum[ia]
    invert(g_all.at[2], range(n_blocks // 2, n_blocks))
    done(15, cm_in2.at[pl.ds(0, n_ia - 1)], recv_sem)
    c_out[0] = dot_f32(jnp.sum(cm_in2[...], axis=0), g_all[2], ((1,), (0,)))

    sent = (
        c_in1.at[pl.ds(0, 4)], b_in.at[pl.ds(0, n_h - 1)], c_in2.at[pl.ds(0, n_ja - 1), near], gb_in.at[pl.ds(0, n_ja - 1)],
        gc_in.at[pl.ds(0, n_ka - 1)], a_in.at[pl.ds(0, n_g - 1)], g_all.at[0, pl.ds(0, rank - g_tall)], a_in2.at[pl.ds(0, n_g - 1)],
        ga_in.at[pl.ds(0, n_ia - 1)], bm_in.at[pl.ds(0, n_h - 1)], g_all.at[1, pl.ds(0, rank - g_tall)], b_in2.at[pl.ds(0, n_h - 1)],
        gb2_in.at[pl.ds(0, n_ja - 1)], cm_in.at[pl.ds(0, n_ja - 1)], g_all.at[2, pl.ds(0, rank - g_tall)], cm_in2.at[pl.ds(0, n_ia - 1)],
        c_in1.at[pl.ds(0, 3)], c_in2.at[pl.ds(0, n_ja - 1), rest],
    )
    for phase, ref in enumerate(sent):
        done(phase, ref, send_sem)


def hand_over(a_ref, b_ref, c_ref, a_out, b_out, c_out, sem):
    copies = [
        pltpu.make_async_copy(source, target, sem.at[at])
        for at, (source, target) in enumerate(((a_ref, a_out), (b_ref, b_out), (c_ref, c_out)))
    ]
    for copy in copies:
        copy.start()
    for copy in copies:
        copy.wait()


def solution(mesh):
    n_ia, n_ja, n_ka = mesh.shape["ia"], mesh.shape["ja"], mesh.shape["ka"]
    n_g, n_h = n_ja * n_ka, n_ia * n_ka

    def on_device(tensor, factor_b, factor_c):
        i_dev, j_dev, k_dev = tensor.shape
        rank = factor_b.shape[-1]
        tall = rank // n_g

        def vmem(*shape, dtype=F32):
            return pltpu.VMEM(shape, dtype)

        square = (rank, rank)
        outs = tuple(jax.ShapeDtypeStruct((1, rows, rank), F32) for rows in (4, 4, 2))
        found = pl.pallas_call(
            functools.partial(kernel, n_ia, n_ja, n_ka),
            out_shape=outs,
            in_specs=[pl.BlockSpec(memory_space=pl.ANY)] + [pl.BlockSpec(memory_space=pltpu.VMEM)] * 2,
            out_specs=(pl.BlockSpec(memory_space=pltpu.VMEM),) * 3,
            scratch_shapes=[
                vmem(i_dev, j_dev, k_dev), vmem(i_dev, j_dev, k_dev, dtype=BF16), vmem(i_dev, j_dev, k_dev, dtype=BF16),
                vmem(i_dev, j_dev, rank),
                vmem(n_ia, 2, rank), vmem(n_ja, n_ia, 2, rank), vmem(n_ia, k_dev // n_ia, rank), vmem(n_h, 4, rank), vmem(j_dev, rank),
                vmem(*square), vmem(n_ja, tall, rank), vmem(*square), vmem(n_ka, tall, rank), vmem(tall, rank), vmem(tall, rank),
                vmem(3, tall, rank), vmem(3, *square),
                vmem(n_g, 4, rank), vmem(n_g, 4, rank), vmem(4, rank), vmem(n_g, 4, rank), vmem(i_dev, rank), vmem(*square), vmem(n_ia, tall, rank),
                vmem(n_h, 4, rank), vmem(n_h, 4, rank), vmem(4, rank), vmem(n_h, 4, rank), vmem(j_dev, rank), vmem(*square), vmem(n_ja, tall, rank),
                vmem(k_dev, rank), vmem(n_ja, n_ia, 2, rank), vmem(n_ja, n_ia, 2, rank), vmem(n_ia, 2, rank), vmem(n_ia, 2, rank),
                vmem(n_g, 4, rank), vmem(n_h, 4, rank),
                pltpu.SemaphoreType.DMA((8,)), pltpu.SemaphoreType.DMA((18,)), pltpu.SemaphoreType.DMA((18,)),
            ],
            compiler_params=pltpu.CompilerParams(
                collective_id=0, has_side_effects=True, vmem_limit_bytes=56 * 1024 * 1024
            ),
        )(tensor, factor_b, factor_c)
        return pl.pallas_call(
            hand_over,
            out_shape=outs,
            in_specs=[pl.BlockSpec(memory_space=pl.ANY)] * 3,
            out_specs=(pl.BlockSpec(memory_space=pl.ANY),) * 3,
            scratch_shapes=[pltpu.SemaphoreType.DMA((3,))],
        )(*found)

    return jax.shard_map(
        on_device,
        mesh=mesh,
        in_specs=(P("ia", "ja", "ka"), P("ja", ("ia", "ka"), None), P("ka", ("ia", "ja"), None)),
        out_specs=(
            P("ia", ("ja", "ka"), None),
            P("ja", ("ia", "ka"), None),
            P("ka", ("ia", "ja"), None),
        ),
        check_vma=False,
    )
```

```python
import functools

import jax
import jax.numpy as jnp
from jax import lax
from jax.experimental import pallas as pl
from jax.experimental.pallas import tpu as pltpu
from jax.sharding import PartitionSpec as P

HIGH = lax.Precision.HIGHEST
MESH = pl.DeviceIdType.MESH
F32 = jnp.float32
BF16 = jnp.bfloat16
NB = 32
NEAR = [(1, 0, 0), (-1, 0, 0), (0, 1, 0), (0, -1, 0), (1, 1, 0), (1, -1, 0), (-1, 1, 0), (-1, -1, 0), (2, 0, 0), (0, 2, 0)]
ACROSS = [(0, 0, 1), (1, 0, -1), (-1, 0, 1), (0, 1, -1), (0, -1, 1)]


def dot_f32(x, y, dims):
    return lax.dot_general(x, y, (dims, ((), ())), precision=HIGH, preferred_element_type=F32)


def dot_bf16(x, y, dims):
    return lax.dot_general(x, y, (dims, ((), ())), preferred_element_type=F32)


def split2(x):
    high = x.astype(BF16)
    return high, (x - high.astype(F32)).astype(BF16)


def split3(x):
    first = x.astype(BF16)
    rest = x - first.astype(F32)
    second = rest.astype(BF16)
    return first, second, (rest - second.astype(F32)).astype(BF16)


def spread(value, at):
    return jnp.broadcast_to(value[at : at + 1, :], value.shape)


def eliminate(old, low, steps):
    n = old.shape[1]
    tall, halves, per = old.shape[0] // 8, n // 128, steps // 8
    rows = lax.broadcasted_iota(jnp.int32, (8, 128), 0)
    lanes = lax.broadcasted_iota(jnp.int32, (8, 128), 1)
    wide = lax.broadcasted_iota(jnp.int32, (8, n), 1)
    parts = [[old[8 * q : 8 * q + 8, 128 * w : 128 * w + 128] for w in range(halves)] for q in range(tall)]
    before, after = [], []

    def lane(q, at):
        return jnp.broadcast_to(parts[q][at // 128][:, at % 128 : at % 128 + 1], (8, 128))

    for group in range(tall // per):
        base = low + steps * group
        mine = range(group * per, (group + 1) * per)
        half, first = base // 128, base % 128
        inside = (lanes >= first) & (lanes < first + steps)
        for q in mine:
            whole = jnp.concatenate(parts[q], axis=1)
            before.append(jnp.where(wide < base, -whole, jnp.where(wide < low + old.shape[0], 0.0, whole)))
        own = {(q, c): lane(q, base + c) for q in mine for c in range(steps)}
        for q in mine:
            unit = jnp.where(lanes - first == rows + 8 * (q - group * per), 1.0, 0.0)
            parts[q][half] = jnp.where(inside, unit, parts[q][half])
        pivot = spread(own[mine[0], 0], 0)
        for j in range(steps):
            at, r = group * per + j // 8, j % 8
            here = rows == r
            across = {c: spread(own[at, c], r) for c in range(j + 1, steps)}
            inverse = 1.0 / pivot
            if j + 1 < steps:
                then, rn = group * per + (j + 1) // 8, (j + 1) % 8
                pivot = spread(own[then, j + 1], rn) - (spread(own[then, j], rn) * across[j + 1]) * inverse
            pivot_row = [spread(parts[at][w], r) for w in range(halves)]
            for q in mine:
                factor = own[q, j] * inverse
                if q == at:
                    factor = jnp.where(here, -inverse, factor)
                for w in range(halves):
                    kept = jnp.where(here, 0.0, parts[q][w]) if q == at else parts[q][w]
                    parts[q][w] = kept - factor * pivot_row[w]
                for c in range(j + 1, steps):
                    kept = jnp.where(here, 0.0, own[q, c]) if q == at else own[q, c]
                    own[q, c] = kept - factor * across[c]
        for q in mine:
            whole = jnp.concatenate(parts[q], axis=1)
            after.append(jnp.where((wide >= base + steps) & (wide < low + old.shape[0]), 0.0, whole))
        done_rows = [[spread(parts[group * per + c // 8][w], c % 8) for w in range(halves)] for c in range(steps)]
        for q in range((group + 1) * per, tall):
            factors = [lane(q, base + c) for c in range(steps)]
            parts[q][half] = jnp.where(inside, 0.0, parts[q][half])
            for w in range(halves):
                terms = [factors[c] * done_rows[c][w] for c in range(steps)]
                while len(terms) > 1:
                    terms = [x + y for x, y in zip(terms[::2], terms[1::2])]
                parts[q][w] = parts[q][w] - terms[0]
    return jnp.concatenate(before, axis=0), jnp.concatenate(after, axis=0)


def stacked(x, y):
    x1, x2, x3 = split3(x)
    y1, y2, y3 = split3(y)
    return dot_bf16(
        jnp.concatenate([x1, x1, x2, x2, x1, x3], axis=0),
        jnp.concatenate([y1, y2, y1, y2, y3, y1], axis=0),
        ((0,), (0,)),
    )


def invert(s_ref, blocks):
    n = s_ref.shape[0]
    all_lanes = lax.broadcasted_iota(jnp.int32, (n, n), 1)
    for block in blocks:
        low = block * NB
        before, after = eliminate(s_ref[low : low + NB, :], low, 16)
        update = stacked(before, after)
        inside = (all_lanes >= low) & (all_lanes < low + NB)
        s_ref[...] = jnp.where(inside, 0.0, s_ref[...]) - update
        s_ref[low : low + NB, :] = after - update[low : low + NB, :]


def kernel(
    n_ia, n_ja, n_ka,
    t_hbm, b_ref, c_ref,
    a_out, b_out, c_out,
    t_ref, thi, tlo, p_ref,
    c_in1, c_in2, c_all, b_in, b_all,
    gb_mine, gb_in, gc_mine, gc_in, gc_rows, ga_rows,
    g_send, g_all,
    a_parts, a_in, a_own, a_in2, a_slice, ga_mine, ga_in,
    bm_parts, bm_in, b_own, b_in2, b_slice, gb2_mine, gb2_in,
    cm_mine, cm_parts, cm_in, cm_sum, cm_in2, a_mine, b_mine,
    t_sem, send_sem, recv_sem,
):
    i_dev, j_dev, k_dev = t_hbm.shape
    rank = c_ref.shape[-1]
    ia, ja, ka = lax.axis_index("ia"), lax.axis_index("ja"), lax.axis_index("ka")
    n_g, n_h = n_ja * n_ka, n_ia * n_ka
    g_at = ja * n_ka + ka
    h_at = ia * n_ka + ka
    g_tall = rank // n_g
    n_blocks = rank // NB

    def device(z, j, k):
        return {"ia": z, "ja": j, "ka": k}

    def far_first(step, n):
        return n // 2 + step // 2 * (2 * lax.rem(step, 2) - 1)

    def plane(step):
        at = lax.rem(g_at + far_first(step, n_g), n_g)
        return at, device(ia, at // n_ka, lax.rem(at, n_ka))

    def column(step):
        at = lax.rem(ia + far_first(step, n_ia), n_ia)
        return at, device(at, ja, ka)

    def column_pair(step):
        at = lax.rem(h_at + far_first(step, n_h), n_h)
        return at, device(at // n_ka, ja, lax.rem(at, n_ka))

    def row(step):
        at = lax.rem(ja + far_first(step, n_ja), n_ja)
        return at, device(ia, at, ka)

    def start(phase, source, target, who):
        pltpu.make_async_remote_copy(
            src_ref=source, dst_ref=target, send_sem=send_sem.at[phase],
            recv_sem=recv_sem.at[phase], device_id=who, device_id_type=MESH,
        ).start()

    def piece(z, j, k):
        odd = lax.rem(z, 2)
        return lax.rem(j + odd * (n_ja // 2), n_ja) * n_ka + lax.rem(k + odd, n_ka)

    piece_at = piece(ia, ja, ka)
    chip_x, chip_y, core = ja // 4, ka * 2 + lax.rem(ja // 2, 2), lax.rem(ja, 2)

    def chip(offset, other):
        x, y = lax.rem(chip_x + offset[0] + 4, 4), lax.rem(chip_y + offset[1] + 4, 4)
        z, c = lax.rem(ia + offset[2] + n_ia, n_ia), lax.rem(core + other, 2)
        return device(z, x * 4 + lax.rem(y, 2) * 2 + c, y // 2)

    def send(phase, n, peer, source, target):
        def body(step, carry):
            at, who = peer(step)
            start(phase, source(at), target(at), who)
            return carry
        lax.fori_loop(1, n, body, 0)

    def done(phase, ref, sem):
        pltpu.make_async_copy(ref, ref, sem.at[phase]).wait()

    chunks = t_sem.shape[0]
    i_chunk = i_dev // chunks

    def load(at):
        span = pl.ds(at * i_chunk, i_chunk)
        return pltpu.make_async_copy(t_hbm.at[span], t_ref.at[span], t_sem.at[at])

    for at in range(chunks):
        load(at).start()

    barrier = pltpu.get_barrier_semaphore()

    def greet_plane(step, carry):
        pl.semaphore_signal(barrier, inc=1, device_id=plane(step)[1], device_id_type=MESH)
        return carry

    def greet_column(step, carry):
        z = column(step)[0]
        for k in range(n_ka):
            pl.semaphore_signal(barrier, inc=1, device_id=device(z, ja, k), device_id_type=MESH)
        return carry

    lax.fori_loop(1, n_ia, greet_column, 0)
    lax.fori_loop(1, n_g, greet_plane, 0)
    beyond = [(offset, other) for offset in ACROSS for other in (0, 1) if (offset[:2], other) != ((0, 0), 0)]
    for (x, y, z), other in beyond:
        pl.semaphore_signal(barrier, inc=1, device_id=chip((-x, -y, -z), other), device_id_type=MESH)
    pl.semaphore_wait(barrier, n_g - 1 + (n_ia - 1) * n_ka + len(beyond))

    for step in (4, 3, 5, 2, 6, 1, 7):
        who = device(lax.rem(ia + step, n_ia), ja, ka)
        start(0 if step in (1, 2, 6, 7) else 16, c_ref.at[0], c_in1.at[(10 - step) % 8], who)
    send(1, n_h, column_pair, lambda at: b_ref.at[0], lambda at: b_in.at[h_at])
    c_in1[2] = c_ref[0]
    b_in[h_at] = b_ref[0]
    near, rest = pl.ds(0, 5), pl.ds(5, 3)
    done(0, c_in1.at[pl.ds(0, 4)], recv_sem)
    send(2, n_ja, row, lambda at: c_in1.at[near], lambda at: c_in2.at[ja, near])
    done(16, c_in1.at[pl.ds(0, 3)], recv_sem)
    send(17, n_ja, row, lambda at: c_in1.at[rest], lambda at: c_in2.at[ja, rest])
    c_in2[ja] = c_in1[...]

    for at in range(chunks):
        load(at).wait()

        def split_one(i, carry):
            high, low = split2(t_ref[i])
            thi[i] = high
            tlo[i] = low
            return carry
        lax.fori_loop(at * i_chunk, (at + 1) * i_chunk, split_one, 0)

    done(1, b_in.at[pl.ds(0, n_h - 1)], recv_sem)
    for h in range(n_h):
        b_all[4 * h : 4 * h + 4, :] = b_in[h]
    gb_mine[...] = dot_f32(b_all[...], b_all[...], ((0,), (0,)))

    def rows_of(ref, at):
        return ref.at[pl.ds(pl.multiple_of(at * g_tall, 8), g_tall)]

    send(3, n_ja, row, lambda at: rows_of(gb_mine, piece(ia, at, ka)), lambda at: gb_in.at[ja])
    for phase, slots in ((2, range(5)), (17, range(5, 8))):
        done(phase, c_in2.at[pl.ds(0, n_ja - 1), pl.ds(slots[0], len(slots))], recv_sem)
        for slot in slots:
            z = lax.rem(ia + slot + n_ia - 2, n_ia)
            for j in range(n_ja):
                c_all[z, 2 * j : 2 * j + 2, :] = c_in2[j, slot]
    c_whole = c_all[...].reshape(k_dev, rank)
    gc_mine[...] = dot_f32(c_whole, c_whole, ((0,), (0,)))

    def other(step):
        at = lax.rem(ka + step, n_ka)
        return at, device(ia, ja, at)

    send(4, n_ka, other, lambda at: rows_of(gc_mine, piece(ia, ja, at)), lambda at: gc_in.at[ka])

    chi, clo = split2(c_whole)
    per = 32
    b_whole = b_all[...]

    pieces, steps = per // 4, i_dev // per
    early = steps * 3 // 4

    def first(step, carry):
        at = lax.rem(g_at // pieces + 1 + step, steps)
        span = pl.ds(at * per, per)
        left_hi = thi[span].reshape(per * j_dev, k_dev)
        left_lo = tlo[span].reshape(per * j_dev, k_dev)
        inner = dot_bf16(left_hi, chi, ((1,), (0,))) + (
            dot_bf16(left_hi, clo, ((1,), (0,))) + dot_bf16(left_lo, chi, ((1,), (0,)))
        )
        inner = inner.reshape(per, j_dev, rank)
        p_ref[span] = inner
        summed = jnp.sum(inner * b_whole[None], axis=1)
        a_parts[pl.ds(at * pieces, pieces)] = summed.reshape(pieces, 4, rank)
        for e in range(pieces):
            to = at * pieces + e

            @pl.when(to != g_at)
            def _():
                start(5, a_parts.at[to], a_in.at[g_at], device(ia, to // n_ka, lax.rem(to, n_ka)))
        return carry

    def gather_gram(phase, slot, rows):
        g_send[slot] = rows
        rows_of(g_all.at[slot], piece_at)[...] = rows
        for offset, other in [(offset, other) for offset in ACROSS[::-1] + NEAR[::-1] for other in (0, 1)] + [((0, 0, 0), 1)]:
            start(phase, g_send.at[slot], rows_of(g_all.at[slot], piece_at), chip(offset, other))

    lax.fori_loop(0, early, first, 0)
    gb_in[ja] = rows_of(gb_mine, piece_at)[...]
    gc_in[ka] = rows_of(gc_mine, piece_at)[...]
    done(3, gb_in.at[pl.ds(0, n_ja - 1)], recv_sem)
    done(4, gc_in.at[pl.ds(0, n_ka - 1)], recv_sem)
    gc_rows[...] = jnp.sum(gc_in[...], axis=0)
    gather_gram(6, 0, jnp.sum(gb_in[...], axis=0) * gc_rows[...])
    lax.fori_loop(early, steps, first, 0)
    a_in[g_at] = a_parts[g_at]

    done(6, g_all.at[0, pl.ds(0, rank - g_tall)], recv_sem)
    invert(g_all.at[0], range(2))
    done(5, a_in.at[pl.ds(0, n_g - 1)], recv_sem)
    own = jnp.sum(a_in[...], axis=0)
    a_own[...] = own
    a_in2[g_at] = own
    send(7, n_g, plane, lambda at: a_own, lambda at: a_in2.at[g_at])
    invert(g_all.at[0], range(2, n_blocks))
    done(7, a_in2.at[pl.ds(0, n_g - 1)], recv_sem)
    for g in range(n_g):
        a_slice[4 * g : 4 * g + 4, :] = a_in2[g]
    a_slice[...] = dot_f32(a_slice[...], g_all[0], ((1,), (0,)))
    a_now = a_slice[...]
    ga_mine[...] = stacked(a_now, a_now)
    send(8, n_ia, column, lambda at: rows_of(ga_mine, piece(at, ja, ka)), lambda at: ga_in.at[ia])
    ga_in[ia] = rows_of(ga_mine, piece_at)[...]

    def second(step, total):
        for e in range(4):
            i = step * 4 + e
            total = total + p_ref[i] * a_slice[pl.ds(i, 1), :]
        return total
    sums = lax.fori_loop(0, i_dev // 4, second, jnp.zeros((j_dev, rank), F32))
    for h in range(n_h):
        bm_parts[h] = sums[4 * h : 4 * h + 4]
    send(9, n_h, column_pair, lambda at: bm_parts.at[at], lambda at: bm_in.at[h_at])
    bm_in[h_at] = bm_parts[h_at]
    done(8, ga_in.at[pl.ds(0, n_ia - 1)], recv_sem)
    ga_rows[...] = jnp.sum(ga_in[...], axis=0)
    gather_gram(10, 1, ga_rows[...] * gc_rows[...])
    done(9, bm_in.at[pl.ds(0, n_h - 1)], recv_sem)
    own = jnp.sum(bm_in[...], axis=0)
    b_own[...] = own
    b_in2[h_at] = own
    send(11, n_h, column_pair, lambda at: b_own, lambda at: b_in2.at[h_at])
    for g in range(n_g):
        a_mine[g] = a_slice[4 * g : 4 * g + 4, :]
    a_out[0] = a_mine[g_at]
    done(10, g_all.at[1, pl.ds(0, rank - g_tall)], recv_sem)
    invert(g_all.at[1], range(n_blocks))
    done(11, b_in2.at[pl.ds(0, n_h - 1)], recv_sem)
    for h in range(n_h):
        b_slice[4 * h : 4 * h + 4, :] = b_in2[h]
    b_slice[...] = dot_f32(b_slice[...], g_all[1], ((1,), (0,)))
    b_now = b_slice[...]
    gb2_mine[...] = stacked(b_now, b_now)
    send(12, n_ja, row, lambda at: rows_of(gb2_mine, piece(ia, at, ka)), lambda at: gb2_in.at[ja])
    gb2_in[ja] = rows_of(gb2_mine, piece_at)[...]

    for h in range(n_h):
        b_mine[h] = b_slice[4 * h : 4 * h + 4, :]
    b_out[0] = b_mine[h_at]
    cm_mine[...] = jnp.zeros_like(cm_mine)

    def third(step, carry):
        span = pl.ds(step * per, per)
        weights = (a_slice[pl.ds(pl.multiple_of(step * per, per), per), :][:, None, :] * b_now[None]).reshape(per * j_dev, rank)
        whi, wlo = split2(weights)
        left_hi = thi[span].reshape(per * j_dev, k_dev)
        left_lo = tlo[span].reshape(per * j_dev, k_dev)
        cm_mine[...] += dot_bf16(left_hi, whi, ((0,), (0,))) + (
            dot_bf16(left_hi, wlo, ((0,), (0,))) + dot_bf16(left_lo, whi, ((0,), (0,)))
        )
        return carry
    lax.fori_loop(0, early, third, 0)
    done(12, gb2_in.at[pl.ds(0, n_ja - 1)], recv_sem)
    gather_gram(14, 2, jnp.sum(gb2_in[...], axis=0) * ga_rows[...])
    lax.fori_loop(early, steps, third, 0)
    for z in range(n_ia):
        for j in range(n_ja):
            low = 2 * (z * n_ja + j)
            cm_parts[j, z] = cm_mine[low : low + 2, :]
    send(13, n_ja, row, lambda at: cm_parts.at[at], lambda at: cm_in.at[ja])
    cm_in[ja] = cm_parts[ja]
    done(14, g_all.at[2, pl.ds(0, rank - g_tall)], recv_sem)
    invert(g_all.at[2], range(n_blocks // 2))
    done(13, cm_in.at[pl.ds(0, n_ja - 1)], recv_sem)
    cm_sum[...] = jnp.sum(cm_in[...], axis=0)
    send(15, n_ia, column, lambda at: cm_sum.at[at], lambda at: cm_in2.at[ia])
    cm_in2[ia] = cm_sum[ia]
    invert(g_all.at[2], range(n_blocks // 2, n_blocks))
    done(15, cm_in2.at[pl.ds(0, n_ia - 1)], recv_sem)
    c_out[0] = dot_f32(jnp.sum(cm_in2[...], axis=0), g_all[2], ((1,), (0,)))

    sent = (
        c_in1.at[pl.ds(0, 4)], b_in.at[pl.ds(0, n_h - 1)], c_in2.at[pl.ds(0, n_ja - 1), near], gb_in.at[pl.ds(0, n_ja - 1)],
        gc_in.at[pl.ds(0, n_ka - 1)], a_in.at[pl.ds(0, n_g - 1)], g_all.at[0, pl.ds(0, rank - g_tall)], a_in2.at[pl.ds(0, n_g - 1)],
        ga_in.at[pl.ds(0, n_ia - 1)], bm_in.at[pl.ds(0, n_h - 1)], g_all.at[1, pl.ds(0, rank - g_tall)], b_in2.at[pl.ds(0, n_h - 1)],
        gb2_in.at[pl.ds(0, n_ja - 1)], cm_in.at[pl.ds(0, n_ja - 1)], g_all.at[2, pl.ds(0, rank - g_tall)], cm_in2.at[pl.ds(0, n_ia - 1)],
        c_in1.at[pl.ds(0, 3)], c_in2.at[pl.ds(0, n_ja - 1), rest],
    )
    for phase, ref in enumerate(sent):
        done(phase, ref, send_sem)


def hand_over(a_ref, b_ref, c_ref, a_out, b_out, c_out, sem):
    copies = [
        pltpu.make_async_copy(source, target, sem.at[at])
        for at, (source, target) in enumerate(((a_ref, a_out), (b_ref, b_out), (c_ref, c_out)))
    ]
    for copy in copies:
        copy.start()
    for copy in copies:
        copy.wait()


def solution(mesh):
    n_ia, n_ja, n_ka = mesh.shape["ia"], mesh.shape["ja"], mesh.shape["ka"]
    n_g, n_h = n_ja * n_ka, n_ia * n_ka

    def on_device(tensor, factor_b, factor_c):
        i_dev, j_dev, k_dev = tensor.shape
        rank = factor_b.shape[-1]
        tall = rank // n_g

        def vmem(*shape, dtype=F32):
            return pltpu.VMEM(shape, dtype)

        square = (rank, rank)
        outs = tuple(jax.ShapeDtypeStruct((1, rows, rank), F32) for rows in (4, 4, 2))
        found = pl.pallas_call(
            functools.partial(kernel, n_ia, n_ja, n_ka),
            out_shape=outs,
            in_specs=[pl.BlockSpec(memory_space=pl.ANY)] + [pl.BlockSpec(memory_space=pltpu.VMEM)] * 2,
            out_specs=(pl.BlockSpec(memory_space=pltpu.VMEM),) * 3,
            scratch_shapes=[
                vmem(i_dev, j_dev, k_dev), vmem(i_dev, j_dev, k_dev, dtype=BF16), vmem(i_dev, j_dev, k_dev, dtype=BF16),
                vmem(i_dev, j_dev, rank),
                vmem(n_ia, 2, rank), vmem(n_ja, n_ia, 2, rank), vmem(n_ia, k_dev // n_ia, rank), vmem(n_h, 4, rank), vmem(j_dev, rank),
                vmem(*square), vmem(n_ja, tall, rank), vmem(*square), vmem(n_ka, tall, rank), vmem(tall, rank), vmem(tall, rank),
                vmem(3, tall, rank), vmem(3, *square),
                vmem(n_g, 4, rank), vmem(n_g, 4, rank), vmem(4, rank), vmem(n_g, 4, rank), vmem(i_dev, rank), vmem(*square), vmem(n_ia, tall, rank),
                vmem(n_h, 4, rank), vmem(n_h, 4, rank), vmem(4, rank), vmem(n_h, 4, rank), vmem(j_dev, rank), vmem(*square), vmem(n_ja, tall, rank),
                vmem(k_dev, rank), vmem(n_ja, n_ia, 2, rank), vmem(n_ja, n_ia, 2, rank), vmem(n_ia, 2, rank), vmem(n_ia, 2, rank),
                vmem(n_g, 4, rank), vmem(n_h, 4, rank),
                pltpu.SemaphoreType.DMA((8,)), pltpu.SemaphoreType.DMA((18,)), pltpu.SemaphoreType.DMA((18,)),
            ],
            compiler_params=pltpu.CompilerParams(
                collective_id=0, has_side_effects=True, vmem_limit_bytes=56 * 1024 * 1024
            ),
        )(tensor, factor_b, factor_c)
        return pl.pallas_call(
            hand_over,
            out_shape=outs,
            in_specs=[pl.BlockSpec(memory_space=pl.ANY)] * 3,
            out_specs=(pl.BlockSpec(memory_space=pl.ANY),) * 3,
            scratch_shapes=[pltpu.SemaphoreType.DMA((3,))],
        )(*found)

    return jax.shard_map(
        on_device,
        mesh=mesh,
        in_specs=(P("ia", "ja", "ka"), P("ja", ("ia", "ka"), None), P("ka", ("ia", "ja"), None)),
        out_specs=(
            P("ia", ("ja", "ka"), None),
            P("ja", ("ia", "ka"), None),
            P("ka", ("ia", "ja"), None),
        ),
        check_vma=False,
    )
```
